128 devices in a mesh: section: 2 (over y_lo), slab: 32 (over x, z, y_hi), rep: 2 (over core).
Axes of the slice: x: 4, y: 4 (y_hi: 2, y_lo: 2; y = y_hi * 2 + y_lo), z: 4, core: 2. Of those that a mesh axis runs over, the one named last changes fastest.
Arguments:
- latent: bfloat16 [4, 64, 64, 8, 128], P(('section', 'rep'), None, 'slab'), may hold values from -250 to 250, as said below
- g_weight: bfloat16 [4, 4, 4, 64, 32], replicated, may hold values from -0.25 to 0.25
- bn_gain: float32 [32], replicated, may hold values from 0.1 to 1.9
- bn_shift: float32 [32], replicated, may hold values from -3 to 3
- real_crops: bfloat16 [4, 32, 128, 16, 256], P(('section', 'rep'), None, 'slab'), may hold values from -6 to 6
- d_weight: bfloat16 [4, 4, 4, 32, 64], replicated, may hold values from -0.125 to 0.125
- cot_fake: bfloat16 [4, 64, 64, 8, 128], P(('section', 'rep'), None, 'slab'), may hold values from -6 to 6
- cot_real: bfloat16 [4, 64, 64, 8, 128], P(('section', 'rep'), None, 'slab'), may hold values from -6 to 6
Outputs:
- d_fake: bfloat16 [4, 64, 64, 8, 128], P(('section', 'rep'), None, 'slab')
- d_real: bfloat16 [4, 64, 64, 8, 128], P(('section', 'rep'), None, 'slab')
- fake_grad: bfloat16 [4, 32, 128, 16, 256], P(('section', 'rep'), None, 'slab')
- weight_grad: float32 [4, 4, 4, 32, 64], replicated
The draws below stay inside these ranges and needn't reach their ends.
Inputs may be any that keep to these rules, and one draw needn't show every extreme that they name: `latent`: entries of order one up to some hundreds.
All inputs are finite; a program needn't handle non-finite values.
Results may differ from the reference program's by a relative error of at most 0.0058.
Values may be sent and summed in bfloat16 or wider, within the bound.
No kernel may reach another device: no remote copies, remote signals or barrier semaphores. Data moves between devices by JAX's collectives and lax.ppermute only.
A program may use at most 64 MiB of HBM per device.

```python
import math
import jax
import jax.numpy as jnp
from jax import lax

CL = 64
CG = 32
CD = 64
LY = 8
LX = 128
BATCH = 4
NZ = 64


def draw_latent(key, part):
    key_base = jax.random.fold_in(key, 0)
    key_rows = jax.random.fold_in(key, 1)
    key_sign = jax.random.fold_in(key, 3)
    full_shape = (BATCH, CL, NZ, LY, LX)
    entries = jnp.clip(jax.random.normal(key_base, full_shape, jnp.float32), -5.0, 5.0)
    rising = 3.0
    sample_rise = 3.0
    channel_sign = jnp.where(jax.random.randint(key_sign, (1, CL, 1, 1, 1), 0, 2) == 0, -1.0, 1.0)
    sample_pos = jnp.arange(BATCH, dtype=jnp.float32) / max(BATCH - 1, 1)
    sample_scale = jnp.exp(sample_pos * math.log(sample_rise))[:, None, None, None, None]
    entries = (entries + 0.6 * channel_sign) * sample_scale
    row_scale = jnp.exp(jax.random.uniform(key_rows, (1, 1, NZ, LY, 1), jnp.float32) * math.log(10.0))
    depth_scale = jnp.exp(jnp.arange(NZ, dtype=jnp.float32) / NZ * math.log(rising))
    return (entries * row_scale * depth_scale[None, None, :, None, None] / 3.0).astype(jnp.bfloat16)


def shard_levels(own_key, dims, pieces, low, largest):
    def one(axis_at, shards_of):
        draws = jax.random.uniform(jax.random.fold_in(jax.random.fold_in(own_key, 6), axis_at), (shards_of,), jnp.float32, low / len(pieces), largest / len(pieces))
        return jnp.repeat(jnp.exp(draws), dims[axis_at] // shards_of).reshape((-1,) + (1,) * (len(dims) - axis_at - 1))

    loudness = one(*pieces[0])
    for cut in pieces[1:]:
        loudness = loudness * one(*cut)
    return loudness


def centred(own_key, shape, width, limit, shards=(), held_as=jnp.bfloat16):
    array = jax.random.normal(own_key, shape, jnp.float32) * width
    if len(shards) > 0:
        array = shard_levels(own_key, shape, shards, -0.22, 0.18) * array
    return jnp.clip(array, min=-limit, max=limit).astype(held_as)


def setup_inputs(seed: int = 0) -> dict:
    seeds = jax.random.split(jax.random.key(seed), 9)
    return {
        "latent": draw_latent(jax.random.fold_in(seeds[8], 71), 0),
        "g_weight": centred(seeds[1], (4, 4, 4, CL, CG), (8 * CL) ** -0.5, 0.25),
        "bn_gain": jnp.clip(1.0 + 0.18 * jax.random.normal(seeds[2], (CG,), jnp.float32), 0.1, 1.9),
        "bn_shift": centred(seeds[3], (CG,), 0.5, 3.0, (), jnp.float32),
        "real_crops": centred(seeds[4], (BATCH, CG, 2 * NZ, 2 * LY, 2 * LX), 1.0, 6.0, ((0, 4), (2, 32))),
        "d_weight": centred(seeds[5], (4, 4, 4, CG, CD), (64 * CG) ** -0.5, 0.125),
        "cot_fake": centred(seeds[6], (BATCH, CD, NZ, LY, LX), 1.0, 6.0, ((0, 4), (2, 32))),
        "cot_real": centred(seeds[7], (BATCH, CD, NZ, LY, LX), 1.0, 6.0, ((0, 4), (2, 32))),
    }


def upsample(latent, g_weight):
    kernel = g_weight[::-1, ::-1, ::-1].astype(jnp.float32)
    return lax.conv_general_dilated(latent.astype(jnp.float32), kernel, (1, 1, 1), [(2, 2), (2, 2), (2, 2)], lhs_dilation=(2, 2, 2), dimension_numbers=('NCDHW', 'DHWIO', 'NCDHW'), precision=lax.Precision.HIGHEST)

def strided(volume, kernel):
    return lax.conv_general_dilated(volume, kernel, (2, 2, 2), [(1, 1), (1, 1), (1, 1)], dimension_numbers=('NCDHW', 'DHWIO', 'NCDHW'), precision=lax.Precision.HIGHEST)

def activate(before):
    squashed = jax.nn.sigmoid(4.0 * before)
    output = before * (0.2 + 0.8 * squashed)
    derivative = 0.2 + 0.8 * squashed + 3.2 * before * squashed * (1.0 - squashed)
    return (output, derivative)

def reference(latent, g_weight, bn_gain, bn_shift, real_crops, d_weight, cot_fake, cot_real):
    before = upsample(latent, g_weight)
    center = lax.optimization_barrier(jnp.mean(before, axis=(0, 2, 3, 4)))
    centered = before - center[None, :, None, None, None]
    variance = lax.optimization_barrier(jnp.mean(centered * centered, axis=(0, 2, 3, 4)))
    factor = bn_gain * lax.rsqrt(variance + 1e-05)
    fake = jnp.maximum(centered * factor[None, :, None, None, None] + bn_shift[None, :, None, None, None], 0.0).astype(jnp.bfloat16)
    fake = lax.optimization_barrier(fake)
    kernel = d_weight.astype(jnp.float32)

    def per_sample(sample_items):
        fake_one, real_one, cot_one, cot_two = sample_items
        fake_input = fake_one[None].astype(jnp.float32)
        real_input = real_one[None].astype(jnp.float32)
        before_fake, pull_fake = jax.vjp(strided, fake_input, kernel)
        before_real, pull_real = jax.vjp(lambda weight_in: strided(real_input, weight_in), kernel)
        out_fake, slope_fake = activate(before_fake)
        out_real, slope_real = activate(before_real)
        grad_fake = lax.optimization_barrier((cot_one[None].astype(jnp.float32) * slope_fake).astype(jnp.bfloat16)).astype(jnp.float32)
        grad_real = lax.optimization_barrier((cot_two[None].astype(jnp.float32) * slope_real).astype(jnp.bfloat16)).astype(jnp.float32)
        input_grad, weight_fake = pull_fake(grad_fake)
        weight_real, = pull_real(grad_real)
        return (out_fake[0].astype(jnp.bfloat16), out_real[0].astype(jnp.bfloat16), input_grad[0].astype(jnp.bfloat16), weight_fake + weight_real)
    d_fake, d_real, fake_grad, weight_parts = lax.map(per_sample, (fake, real_crops, cot_fake, cot_real))
    return (d_fake, d_real, fake_grad, lax.optimization_barrier(jnp.sum(weight_parts, axis=0)))
```

```python
import jax
import jax.numpy as jnp
from jax import lax
from jax.experimental import pallas as pl
from jax.experimental.pallas import tpu as pltpu
from jax.sharding import PartitionSpec as P

AXES = ("section", "slab", "rep")
NDEV = 128
C = 64
G = 32
Y = 8
X = 128
CELLS = Y * X
F32 = jnp.float32
BF16 = jnp.bfloat16

phase_taps = (((1, 0), (3, -1)), ((0, 1), (2, 0)))


def dot(a, b, dims=(1, 0)):
    return lax.dot_general(a, b, (((dims[0],), (dims[1],)), ((), ())), preferred_element_type=F32)


def lanes(shape):
    return lax.broadcasted_iota(jnp.int32, shape, len(shape) - 1)


def from_left(tile, lane):
    return jnp.where(lane == 0, 0.0, pltpu.roll(tile, 1, 1))


def from_right(tile, lane):
    return jnp.where(lane == X - 1, 0.0, pltpu.roll(tile, X - 1, 1))


def spread_weights(taps_ref, wide_ref):
    wide_ref[...] = jnp.zeros_like(wide_ref)
    for pz in range(2):
        for py in range(2):
            for px in range(2):
                row = ((1 - pz) * 4 + py * 2 + px) * G
                for kz, oz in phase_taps[pz]:
                    tz = oz if pz == 1 else oz + 1
                    for ky, oy in phase_taps[py]:
                        for kx, ox in phase_taps[px]:
                            col = tz * 576 + (oy + 1) * 192 + (ox + 1) * 64
                            tap = (kz * 16 + ky * 4 + kx) * G
                            wide_ref[row : row + G, col : col + C] = taps_ref[tap : tap + G, :]


def spread_cells(tile, depth, y, lane, patch_ref):
    for xi, moved in ((0, from_left(tile, lane)), (1, tile), (2, from_right(tile, lane))):
        piece = moved.astype(BF16)
        for yi in range(3):
            to = y - (yi - 1)
            if 0 <= to < Y:
                row = depth * 576 + yi * 192 + xi * 64
                patch_ref[row : row + C, to * X : (to + 1) * X] = piece


def clear_rims(depth, patch_ref):
    edge = jnp.zeros((192, X), BF16)
    patch_ref[depth * 576 : depth * 576 + 192, 0:X] = edge
    patch_ref[depth * 576 + 384 : depth * 576 + 576, CELLS - X : CELLS] = edge


def as_row(column, shift):
    sub = lax.broadcasted_iota(jnp.int32, (G, 128), 0)
    return jnp.sum(jnp.where(lanes((G, 128)) == sub + shift, column, 0.0), axis=0, keepdims=True)


def as_column(row, shift):
    sub = lax.broadcasted_iota(jnp.int32, (G, 128), 0)
    return jnp.sum(jnp.where(lanes((G, 128)) == sub + shift, row, 0.0), axis=1, keepdims=True)


def generator_kernel(lat_ref, prev_ref, next_ref, taps_ref, before_ref, stats_ref, wide, patch, wide_lat):
    spread_weights(taps_ref, wide)
    wide_lat[0:1024, :] = lat_ref[...].astype(F32)
    wide_lat[1024:1536, :] = prev_ref[...].astype(F32)
    wide_lat[1536:2048, :] = next_ref[...].astype(F32)
    lane = lanes((C, X))
    for depth, (base, stride) in enumerate(((1024, 8), (0, 16), (8, 16), (1536, 8))):
        clear_rims(depth, patch)
        for y in range(Y):
            spread_cells(wide_lat[pl.ds(base + y, C, stride=stride), :], depth, y, lane, patch)
    for pair in range(3):
        before_ref[pair * 256 : (pair + 1) * 256, :] = dot(
            wide[...], patch[pair * 576 : pair * 576 + 1152, :]
        )
    count = 16.0 * CELLS
    total = jnp.zeros((G, CELLS), F32)
    for block in range(4, 20):
        total += before_ref[block * G : (block + 1) * G, :]
    mean = jnp.sum(total, axis=1, keepdims=True) * (1.0 / count)
    squares = jnp.zeros((G, CELLS), F32)
    for block in range(4, 20):
        off = before_ref[block * G : (block + 1) * G, :] - mean
        squares += off * off
    spread = jnp.sum(squares, axis=1, keepdims=True)
    stats_ref[...] = jnp.broadcast_to(as_row(mean, 0) + as_row(spread, G), (NDEV, 128))


def activate(before):
    squashed = jax.nn.sigmoid(4.0 * before)
    output = before * (0.2 + 0.8 * squashed)
    derivative = 0.2 + 0.8 * squashed + 3.2 * before * squashed * (1.0 - squashed)
    return (output, derivative)


def discriminate(patch, weight_ref, cot_ref, out_ref, wide_cot, wide_out, grad):
    wide_cot[...] = cot_ref[...].astype(F32)
    for m in range(2):
        pre = dot(weight_ref[...], patch[m * 1024 : m * 1024 + 2048, :])
        for y in range(Y):
            output, slope = activate(pre[:, y * X : (y + 1) * X])
            wide_out[pl.ds(m * Y + y, C, stride=16), :] = output
            cot = wide_cot[pl.ds(m * Y + y, C, stride=16), :]
            grad[m * C : (m + 1) * C, y * X : (y + 1) * X] = (cot * slope).astype(BF16)
    out_ref[...] = wide_out[...].astype(BF16)
    terms = None
    for m in range(2):
        part = dot(patch[m * 1024 : m * 1024 + 2048, :], grad[m * C : (m + 1) * C, :], (1, 1))
        terms = part if terms is None else terms + part
    return terms


def real_kernel(
    real_ref, prev_ref, next_ref, weight_ref, cot_ref, out_ref, terms_ref, patch, split, wide_cot, wide_out, grad
):
    source = lax.broadcasted_iota(jnp.int32, (2 * X, X), 0)
    for kx in range(4):
        pick = jnp.where(source == 2 * lanes((2 * X, X)) + kx - 1, 1.0, 0.0).astype(BF16)
        split[kx, 0:2048, :] = dot(real_ref[...], pick)
        split[kx, 2048:2560, :] = dot(prev_ref[...], pick)
        split[kx, 2560:3072, :] = dot(next_ref[...], pick)
    edge = jnp.zeros((128, X), BF16)
    places = ((2048, 16), (0, 64), (16, 64), (32, 64), (48, 64), (2560, 16))
    for depth, (base, stride) in enumerate(places):
        patch[depth * 512 : depth * 512 + 128, 0:X] = edge
        patch[depth * 512 + 384 : depth * 512 + 512, CELLS - X : CELLS] = edge
        for row in range(2 * Y):
            for kx in range(4):
                piece = split[kx, pl.ds(base + row, G, stride=stride), :].astype(BF16)
                for ky in range(4):
                    if (row + 1 - ky) % 2 == 0 and 0 <= (row + 1 - ky) // 2 < Y:
                        y = (row + 1 - ky) // 2
                        at = depth * 512 + ky * 128 + kx * G
                        patch[at : at + G, y * X : (y + 1) * X] = piece
    terms_ref[...] = discriminate(patch, weight_ref, cot_ref, out_ref, wide_cot, wide_out, grad)


def fake_kernel(
    inside_ref,
    before_ref,
    stats_ref,
    gain_ref,
    shift_ref,
    weight_ref,
    cot_ref,
    real_terms_ref,
    out_ref,
    low_ref,
    high_ref,
    terms_ref,
    patch,
    wide_cot,
    wide_out,
    grad,
):
    stats = stats_ref[...]
    count = 16.0 * CELLS
    sums = jnp.sum(stats, axis=0, keepdims=True)
    mean_row = sums * (1.0 / NDEV)
    off = stats - mean_row
    between = as_column(jnp.sum(off * off, axis=0, keepdims=True), 0)
    center = as_column(mean_row, 0)
    variance = (as_column(sums, G) + count * between) * (1.0 / (count * NDEV))
    factor = as_column(gain_ref[...], 0) * lax.rsqrt(variance + 1e-05)
    shift = as_column(shift_ref[...], 0)
    lane = lanes((G, X))
    edge = jnp.zeros((128, X), BF16)
    for depth in range(6):
        patch[depth * 512 : depth * 512 + 128, 0:X] = edge
        patch[depth * 512 + 384 : depth * 512 + 512, CELLS - X : CELLS] = edge
        for py in range(2):
            for px in range(2):
                block = (depth * 4 + py * 2 + px) * G
                for y in range(Y):
                    cells = before_ref[block : block + G, y * X : (y + 1) * X]
                    fake = jnp.maximum((cells - center) * factor + shift, 0.0)
                    if depth == 0:
                        fake = jnp.where(inside_ref[0] > 0, fake, 0.0)
                    if depth == 5:
                        fake = jnp.where(inside_ref[1] > 0, fake, 0.0)
                    if px == 1:
                        pieces = ((2, fake), (0, from_left(fake, lane)))
                    else:
                        pieces = ((1, fake), (3, from_right(fake, lane)))
                    for kx, piece in pieces:
                        piece = piece.astype(BF16)
                        for ky, to in ((2, y), (0, y + 1)) if py == 1 else ((1, y), (3, y - 1)):
                            if 0 <= to < Y:
                                at = depth * 512 + ky * 128 + kx * G
                                patch[at : at + G, to * X : (to + 1) * X] = piece
    terms = discriminate(patch, weight_ref, cot_ref, out_ref, wide_cot, wide_out, grad)
    low_ref[...] = grad[0:C, :]
    high_ref[...] = grad[C : 2 * C, :]
    terms = (terms + real_terms_ref[...]).reshape(NDEV, 16, C)
    terms_ref[...] = jnp.concatenate([terms[:, 0:8, :], terms[:, 8:16, :]], axis=2)


def pullback_kernel(prev_ref, low_ref, high_ref, next_ref, taps_ref, out_ref, wide, patch, wide_out):
    spread_weights(taps_ref, wide)
    lane = lanes((C, X))
    for depth, ref in enumerate((prev_ref, low_ref, high_ref, next_ref)):
        clear_rims(depth, patch)
        for y in range(Y):
            spread_cells(ref[:, y * X : (y + 1) * X].astype(F32), depth, y, lane, patch)
    column = lax.broadcasted_iota(jnp.int32, (2 * X, 2 * X), 1)
    source = lax.broadcasted_iota(jnp.int32, (2 * X, 2 * X), 0)
    weave = jnp.where(source == (column % 2) * X + column // 2, 1.0, 0.0).astype(BF16)
    for pair, first, depths in ((0, 128, (0,)), (1, 0, (1, 2)), (2, 0, (3,))):
        rows = 128 * len(depths)
        result = dot(wide[first : first + rows, :], patch[pair * 576 : pair * 576 + 1152, :])
        result = result.astype(BF16)
        for at, depth in enumerate(depths):
            for py in range(2):
                even = result[at * 128 + py * 64 : at * 128 + py * 64 + G, :]
                odd = result[at * 128 + py * 64 + G : at * 128 + py * 64 + 2 * G, :]
                both = jnp.concatenate(
                    [
                        jnp.concatenate([even[:, y * X : (y + 1) * X], odd[:, y * X : (y + 1) * X]], axis=1)
                        for y in range(Y)
                    ],
                    axis=0,
                )
                woven = dot(both, weave)
                for y in range(Y):
                    place = pl.ds(depth * 16 + 2 * y + py, G, stride=64)
                    wide_out[0, place, :] = woven[y * G : (y + 1) * G, 0:X]
                    wide_out[1, place, :] = woven[y * G : (y + 1) * G, X : 2 * X]
    out_ref[:, 0:X] = wide_out[0].astype(BF16)
    out_ref[:, X : 2 * X] = wide_out[1].astype(BF16)


def call(body, name, args, outs, scratch, flops, smem=0):
    moved = sum(a.size * a.dtype.itemsize for a in args) + sum(o.size * o.dtype.itemsize for o in outs)
    return pl.pallas_call(
        body,
        name=name,
        out_shape=outs,
        in_specs=[pl.BlockSpec(memory_space=pltpu.SMEM)] * smem
        + [pl.BlockSpec(memory_space=pltpu.VMEM)] * (len(args) - smem),
        out_specs=[pl.BlockSpec(memory_space=pltpu.VMEM)] * len(outs),
        scratch_shapes=scratch,
        compiler_params=pltpu.CompilerParams(vmem_limit_bytes=48 * 1024 * 1024),
        cost_estimate=pl.CostEstimate(flops=flops, bytes_accessed=moved, transcendentals=0),
    )(*args)


def exchange(low, high):
    ends = lax.axis_size("slab") - 1
    before = lax.ppermute(high, "slab", [(i, i + 1) for i in range(ends)])
    after = lax.ppermute(low, "slab", [(i + 1, i) for i in range(ends)])
    return before, after


def local(latent, g_weight, bn_gain, bn_shift, real_crops, d_weight, cot_fake, cot_real):
    shape = jax.ShapeDtypeStruct
    taps_g = g_weight.transpose(0, 1, 2, 4, 3).reshape(64 * G, C)
    taps_d = d_weight.reshape(64 * G, C)
    weight = taps_d.T
    lat = latent[0]
    lat_prev, lat_next = exchange(lat[:, 0].reshape(C * Y, X), lat[:, 1].reshape(C * Y, X))
    real = real_crops[0]
    real_prev, real_next = exchange(
        real[:, 0].reshape(G * 2 * Y, 2 * X), real[:, 3].reshape(G * 2 * Y, 2 * X)
    )
    before, stats = call(
        generator_kernel,
        "generator",
        (lat.reshape(C * 2 * Y, X), lat_prev, lat_next, taps_g),
        [shape((768, CELLS), F32), shape((NDEV, 128), F32)],
        [
            pltpu.VMEM((256, 1152), BF16),
            pltpu.VMEM((4 * 576, CELLS), BF16),
            pltpu.VMEM((2048, X), F32),
        ],
        2 * 768 * 1152 * CELLS,
    )
    stats = lax.all_to_all(stats, AXES, 0, 0, tiled=True)
    working = [
        pltpu.VMEM((C * 2 * Y, X), F32),
        pltpu.VMEM((C * 2 * Y, X), F32),
        pltpu.VMEM((2 * C, CELLS), BF16),
    ]
    d_real, real_terms = call(
        real_kernel,
        "real_branch",
        (real.reshape(G * 64, 2 * X), real_prev, real_next, weight, cot_real.reshape(C * 2 * Y, X)),
        [shape((C * 2 * Y, X), BF16), shape((2048, C), F32)],
        [pltpu.VMEM((6 * 512, CELLS), BF16), pltpu.VMEM((4, 3072, X), F32)] + working,
        8 * 2048 * C * CELLS * 2,
    )
    at = lax.axis_index("slab")
    inside = jnp.stack([at > 0, at < lax.axis_size("slab") - 1]).astype(jnp.int32)
    d_fake, low, high, terms = call(
        fake_kernel,
        "fake_branch",
        (
            inside,
            before,
            stats,
            jnp.pad(bn_gain, (0, 128 - G)).reshape(1, 128),
            jnp.pad(bn_shift, (0, 128 - G)).reshape(1, 128),
            weight,
            cot_fake.reshape(C * 2 * Y, X),
            real_terms,
        ),
        [
            shape((C * 2 * Y, X), BF16),
            shape((C, CELLS), BF16),
            shape((C, CELLS), BF16),
            shape((NDEV, 8, 128), F32),
        ],
        [pltpu.VMEM((6 * 512, CELLS), BF16)] + working,
        8 * 2048 * C * CELLS * 2,
        smem=1,
    )
    grad_prev, grad_next = exchange(low, high)
    parts = lax.all_to_all(terms, AXES, 0, 0, tiled=True)
    (fake_grad,) = call(
        pullback_kernel,
        "pullback",
        (grad_prev, low, high, grad_next, taps_d),
        [shape((G * 64, 2 * X), BF16)],
        [
            pltpu.VMEM((256, 1152), BF16),
            pltpu.VMEM((4 * 576, CELLS), BF16),
            pltpu.VMEM((2, G * 64, X), F32),
        ],
        2 * 512 * 1152 * CELLS,
    )
    summed = jnp.broadcast_to(jnp.sum(parts, axis=0, keepdims=True), (NDEV, 8, 128))
    whole = lax.all_to_all(summed, AXES, 0, 0, tiled=True)
    weight_grad = whole.reshape(NDEV, 8, 2, C).transpose(0, 2, 1, 3).reshape(4, 4, 4, G, C)
    return (
        d_fake.reshape(1, C, 2, Y, X),
        d_real.reshape(1, C, 2, Y, X),
        fake_grad.reshape(1, G, 4, 2 * Y, 2 * X),
        weight_grad,
    )


def solution(mesh):
    split = P(("section", "rep"), None, "slab", None, None)
    in_specs = (split, P(), P(), P(), split, P(), split, split)
    out_specs = (split, split, split, P())
    return jax.shard_map(local, mesh=mesh, in_specs=in_specs, out_specs=out_specs, check_vma=False)
```

```python
import jax
import jax.numpy as jnp
from jax import lax
from jax.experimental import pallas as pl
from jax.experimental.pallas import tpu as pltpu
from jax.sharding import PartitionSpec as P

AXES = ("section", "slab", "rep")
NDEV = 128
C = 64
G = 32
Y = 8
X = 128
CELLS = Y * X
F32 = jnp.float32
BF16 = jnp.bfloat16

phase_taps = (((1, 0), (3, -1)), ((0, 1), (2, 0)))


def dot(a, b, dims=(1, 0)):
    return lax.dot_general(a, b, (((dims[0],), (dims[1],)), ((), ())), preferred_element_type=F32)


def lanes(shape):
    return lax.broadcasted_iota(jnp.int32, shape, len(shape) - 1)


def from_left(tile, lane):
    return jnp.where(lane == 0, 0.0, pltpu.roll(tile, 1, 1))


def from_right(tile, lane):
    return jnp.where(lane == X - 1, 0.0, pltpu.roll(tile, X - 1, 1))


def spread_weights(taps_ref, wide_ref):
    wide_ref[...] = jnp.zeros_like(wide_ref)
    for pz in range(2):
        for py in range(2):
            for px in range(2):
                row = ((1 - pz) * 4 + py * 2 + px) * G
                for kz, oz in phase_taps[pz]:
                    tz = oz if pz == 1 else oz + 1
                    for ky, oy in phase_taps[py]:
                        for kx, ox in phase_taps[px]:
                            col = tz * 576 + (oy + 1) * 192 + (ox + 1) * 64
                            tap = (kz * 16 + ky * 4 + kx) * G
                            wide_ref[row : row + G, col : col + C] = taps_ref[tap : tap + G, :]


def spread_cells(tile, depth, y, lane, patch_ref):
    for xi, moved in ((0, from_left(tile, lane)), (1, tile), (2, from_right(tile, lane))):
        piece = moved.astype(BF16)
        for yi in range(3):
            to = y - (yi - 1)
            if 0 <= to < Y:
                row = depth * 576 + yi * 192 + xi * 64
                patch_ref[row : row + C, to * X : (to + 1) * X] = piece


def clear_rims(depth, patch_ref):
    edge = jnp.zeros((192, X), BF16)
    patch_ref[depth * 576 : depth * 576 + 192, 0:X] = edge
    patch_ref[depth * 576 + 384 : depth * 576 + 576, CELLS - X : CELLS] = edge


def as_row(column, shift):
    sub = lax.broadcasted_iota(jnp.int32, (G, 128), 0)
    return jnp.sum(jnp.where(lanes((G, 128)) == sub + shift, column, 0.0), axis=0, keepdims=True)


def as_column(row, shift):
    sub = lax.broadcasted_iota(jnp.int32, (G, 128), 0)
    return jnp.sum(jnp.where(lanes((G, 128)) == sub + shift, row, 0.0), axis=1, keepdims=True)


def own_kernel(lat_ref, taps_ref, wide_ref, own_ref, first_ref, middle_ref, last_ref, wide_lat):
    spread_weights(taps_ref, wide_ref)
    wide_lat[...] = lat_ref[...].astype(F32)
    lane = lanes((C, X))
    for depth in range(2):
        clear_rims(depth, own_ref)
        for y in range(Y):
            spread_cells(wide_lat[pl.ds(depth * Y + y, C, stride=16), :], depth, y, lane, own_ref)
    first_ref[...] = dot(wide_ref[:, 576:1152], own_ref[0:576, :])
    middle_ref[...] = dot(wide_ref[...], own_ref[...])
    last_ref[...] = dot(wide_ref[:, 0:576], own_ref[576:1152, :])


def rim_kernel(prev_ref, next_ref, wide_ref, first_in, middle_ref, last_in, first_ref, last_ref, stats_ref, patch, wide_lat):
    wide_lat[0:512, :] = prev_ref[...].astype(F32)
    wide_lat[512:1024, :] = next_ref[...].astype(F32)
    lane = lanes((C, X))
    for side in range(2):
        clear_rims(side, patch)
        for y in range(Y):
            spread_cells(wide_lat[pl.ds(side * 512 + y, C, stride=8), :], side, y, lane, patch)
    first_ref[...] = first_in[...] + dot(wide_ref[:, 0:576], patch[0:576, :])
    last_ref[...] = last_in[...] + dot(wide_ref[:, 576:1152], patch[576:1152, :])
    count = 16.0 * CELLS
    blocks = [(first_ref, r) for r in range(4, 8)] + [(middle_ref, r) for r in range(8)]
    blocks += [(last_ref, r) for r in range(4)]
    total = jnp.zeros((G, CELLS), F32)
    for ref, block in blocks:
        total += ref[block * G : (block + 1) * G, :]
    mean = jnp.sum(total, axis=1, keepdims=True) * (1.0 / count)
    squares = jnp.zeros((G, CELLS), F32)
    for ref, block in blocks:
        off = ref[block * G : (block + 1) * G, :] - mean
        squares += off * off
    spread = jnp.sum(squares, axis=1, keepdims=True)
    stats_ref[...] = jnp.broadcast_to(as_row(mean, 0) + as_row(spread, G), (NDEV, 128))


def activate(before):
    squashed = jax.nn.sigmoid(4.0 * before)
    output = before * (0.2 + 0.8 * squashed)
    derivative = 0.2 + 0.8 * squashed + 3.2 * before * squashed * (1.0 - squashed)
    return (output, derivative)


def discriminate(patch, weight_ref, cot_ref, out_ref, wide_cot, wide_out, grad):
    wide_cot[...] = cot_ref[...].astype(F32)
    early = weight_ref[:, 0:1024]
    late = weight_ref[:, 1024:2048]
    shared = dot(jnp.concatenate([late, early], axis=0), patch[1024:2048, :])
    pre = (
        dot(early, patch[0:1024, :]) + shared[0:C, :],
        shared[C : 2 * C, :] + dot(late, patch[2048:3072, :]),
    )
    nothing = jnp.zeros((C, CELLS), BF16)
    grad[0:C, :] = nothing
    grad[3 * C : 4 * C, :] = nothing
    for m in range(2):
        for y in range(Y):
            output, slope = activate(pre[m][:, y * X : (y + 1) * X])
            wide_out[pl.ds(m * Y + y, C, stride=16), :] = output
            cot = wide_cot[pl.ds(m * Y + y, C, stride=16), :]
            grad[(2 - m) * C : (3 - m) * C, y * X : (y + 1) * X] = (cot * slope).astype(BF16)
    out_ref[...] = wide_out[...].astype(BF16)
    terms = dot(patch[0:1024, :], grad[128:256, :], (1, 1))
    terms += dot(patch[1024:2048, :], grad[64:192, :], (1, 1))
    return terms + dot(patch[2048:3072, :], grad[0:128, :], (1, 1))


def real_kernel(
    real_ref, prev_ref, next_ref, weight_ref, cot_ref, out_ref, terms_ref, patch, halves, rows, wide_cot, wide_out, grad
):
    for half in range(2):
        halves[half, 0:2048, :] = real_ref[:, half * X : (half + 1) * X].astype(F32)
        halves[half, 2048:2560, :] = prev_ref[:, half * X : (half + 1) * X].astype(F32)
        halves[half, 2560:3072, :] = next_ref[:, half * X : (half + 1) * X].astype(F32)
    column = lanes((2 * X, 4 * X))
    source = lax.broadcasted_iota(jnp.int32, (2 * X, 4 * X), 0)
    pick = jnp.where(source == 2 * (column % X) + column // X - 1, 1.0, 0.0).astype(BF16)
    edge = jnp.zeros((128, X), BF16)
    places = ((2048, 16), (0, 64), (16, 64), (32, 64), (48, 64), (2560, 16))
    for depth, (base, stride) in enumerate(places):
        patch[depth * 512 : depth * 512 + 128, 0:X] = edge
        patch[depth * 512 + 384 : depth * 512 + 512, CELLS - X : CELLS] = edge
        for row in range(2 * Y):
            for half in range(2):
                cells = halves[half, pl.ds(base + row, G, stride=stride), :].astype(BF16)
                rows[depth * 512 + row * G : depth * 512 + (row + 1) * G, half * X : (half + 1) * X] = cells
        split = dot(rows[depth * 512 : (depth + 1) * 512, :], pick).astype(BF16)
        for row in range(2 * Y):
            for kx in range(4):
                piece = split[row * G : (row + 1) * G, kx * X : (kx + 1) * X]
                for ky in range(4):
                    if (row + 1 - ky) % 2 == 0 and 0 <= (row + 1 - ky) // 2 < Y:
                        y = (row + 1 - ky) // 2
                        at = depth * 512 + ky * 128 + kx * G
                        patch[at : at + G, y * X : (y + 1) * X] = piece
    terms_ref[...] = discriminate(patch, weight_ref, cot_ref, out_ref, wide_cot, wide_out, grad)


def fake_kernel(
    inside_ref,
    first_ref,
    middle_ref,
    last_ref,
    stats_ref,
    gain_ref,
    shift_ref,
    weight_ref,
    cot_ref,
    real_terms_ref,
    out_ref,
    low_ref,
    high_ref,
    terms_ref,
    patch,
    wide_cot,
    wide_out,
    grad,
):
    stats = stats_ref[...]
    count = 16.0 * CELLS
    sums = jnp.sum(stats, axis=0, keepdims=True)
    mean_row = sums * (1.0 / NDEV)
    off = stats - mean_row
    between = as_column(jnp.sum(off * off, axis=0, keepdims=True), 0)
    center = as_column(mean_row, 0)
    variance = (as_column(sums, G) + count * between) * (1.0 / (count * NDEV))
    factor = as_column(gain_ref[...], 0) * lax.rsqrt(variance + 1e-05)
    shift = as_column(shift_ref[...], 0)
    lane = lanes((G, X))
    edge = jnp.zeros((128, X), BF16)
    for depth in range(6):
        before_ref = (first_ref, middle_ref, last_ref)[depth // 2]
        patch[depth * 512 : depth * 512 + 128, 0:X] = edge
        patch[depth * 512 + 384 : depth * 512 + 512, CELLS - X : CELLS] = edge
        for py in range(2):
            for px in range(2):
                block = (depth % 2 * 4 + py * 2 + px) * G
                for y in range(Y):
                    cells = before_ref[block : block + G, y * X : (y + 1) * X]
                    fake = jnp.maximum((cells - center) * factor + shift, 0.0)
                    if depth == 0:
                        fake = jnp.where(inside_ref[0] > 0, fake, 0.0)
                    if depth == 5:
                        fake = jnp.where(inside_ref[1] > 0, fake, 0.0)
                    if px == 1:
                        pieces = ((2, fake), (0, from_left(fake, lane)))
                    else:
                        pieces = ((1, fake), (3, from_right(fake, lane)))
                    for kx, piece in pieces:
                        piece = piece.astype(BF16)
                        for ky, to in ((2, y), (0, y + 1)) if py == 1 else ((1, y), (3, y - 1)):
                            if 0 <= to < Y:
                                at = depth * 512 + ky * 128 + kx * G
                                patch[at : at + G, to * X : (to + 1) * X] = piece
    terms = discriminate(patch, weight_ref, cot_ref, out_ref, wide_cot, wide_out, grad)
    low_ref[...] = grad[2 * C : 3 * C, :]
    high_ref[...] = grad[C : 2 * C, :]
    terms_ref[...] = terms + real_terms_ref[...]


def sum_kernel(parts_ref, prev_ref, next_ref, sums_ref):
    del prev_ref, next_ref
    total = jnp.sum(parts_ref[...].reshape(NDEV, 8, 128), axis=0, keepdims=True)
    sums_ref[...] = jnp.broadcast_to(total, (NDEV, 8, 128)).reshape(NDEV * 8, 128).astype(BF16)


def unpack_kernel(sums_ref, out_ref):
    sums = sums_ref[...].astype(F32)
    out_ref[0:1024, :] = sums[:, 0:C]
    out_ref[1024:2048, :] = sums[:, C : 2 * C]


def pullback_kernel(prev_ref, low_ref, high_ref, next_ref, taps_ref, sums_ref, out_ref, wide, patch, wide_out):
    del sums_ref
    spread_weights(taps_ref, wide)
    lane = lanes((C, X))
    for depth, ref in enumerate((prev_ref, low_ref, high_ref, next_ref)):
        clear_rims(depth, patch)
        for y in range(Y):
            spread_cells(ref[:, y * X : (y + 1) * X].astype(F32), depth, y, lane, patch)
    column = lax.broadcasted_iota(jnp.int32, (2 * X, 2 * X), 1)
    source = lax.broadcasted_iota(jnp.int32, (2 * X, 2 * X), 0)
    weave = jnp.where(source == (column % 2) * X + column // 2, 1.0, 0.0).astype(BF16)
    for pair, first, depths in ((0, 128, (0,)), (1, 0, (1, 2)), (2, 0, (3,))):
        rows = 128 * len(depths)
        result = dot(wide[first : first + rows, :], patch[pair * 576 : pair * 576 + 1152, :])
        result = result.astype(BF16)
        for at, depth in enumerate(depths):
            for py in range(2):
                even = result[at * 128 + py * 64 : at * 128 + py * 64 + G, :]
                odd = result[at * 128 + py * 64 + G : at * 128 + py * 64 + 2 * G, :]
                both = jnp.concatenate(
                    [
                        jnp.concatenate([even[:, y * X : (y + 1) * X], odd[:, y * X : (y + 1) * X]], axis=1)
                        for y in range(Y)
                    ],
                    axis=0,
                )
                woven = dot(both, weave)
                for y in range(Y):
                    place = pl.ds(depth * 16 + 2 * y + py, G, stride=64)
                    wide_out[0, place, :] = woven[y * G : (y + 1) * G, 0:X]
                    wide_out[1, place, :] = woven[y * G : (y + 1) * G, X : 2 * X]
    out_ref[:, 0:X] = wide_out[0].astype(BF16)
    out_ref[:, X : 2 * X] = wide_out[1].astype(BF16)


def call(body, name, args, outs, scratch, flops, mebibytes, smem=(), unread=()):
    moved = sum(a.size * a.dtype.itemsize for a in args) + sum(o.size * o.dtype.itemsize for o in outs)
    spaces = [
        pltpu.SMEM if i in smem else pl.ANY if i in unread else pltpu.VMEM for i in range(len(args))
    ]
    return pl.pallas_call(
        body,
        name=name,
        out_shape=outs,
        in_specs=[pl.BlockSpec(memory_space=space) for space in spaces],
        out_specs=[pl.BlockSpec(memory_space=pltpu.VMEM)] * len(outs),
        scratch_shapes=scratch,
        compiler_params=pltpu.CompilerParams(vmem_limit_bytes=mebibytes * 1024 * 1024),
        cost_estimate=pl.CostEstimate(flops=flops, bytes_accessed=moved, transcendentals=0),
    )(*args)


def exchange(low, high):
    ends = lax.axis_size("slab") - 1
    before = lax.ppermute(high, "slab", [(i, i + 1) for i in range(ends)])
    after = lax.ppermute(low, "slab", [(i + 1, i) for i in range(ends)])
    return before, after


def local(latent, g_weight, bn_gain, bn_shift, real_crops, d_weight, cot_fake, cot_real):
    shape = jax.ShapeDtypeStruct
    taps_g = g_weight.transpose(0, 1, 2, 4, 3).reshape(64 * G, C)
    taps_d = d_weight.reshape(64 * G, C)
    weight = taps_d.T
    lat = latent[0]
    lat_prev, lat_next = exchange(lat[:, 0].reshape(C * Y, X), lat[:, 1].reshape(C * Y, X))
    real = real_crops[0]
    real_prev, real_next = exchange(
        real[:, 0].reshape(G * 2 * Y, 2 * X), real[:, 3].reshape(G * 2 * Y, 2 * X)
    )
    wide, own, first, middle, last = call(
        own_kernel,
        "own_cells",
        (lat.reshape(C * 2 * Y, X), taps_g),
        [shape((256, 1152), BF16), shape((1152, CELLS), BF16)] + [shape((256, CELLS), F32)] * 3,
        [pltpu.VMEM((1024, X), F32)],
        4 * 256 * 1152 * CELLS,
        16,
    )
    first, last, stats = call(
        rim_kernel,
        "rim_cells",
        (lat_prev, lat_next, wide, first, middle, last),
        [shape((256, CELLS), F32), shape((256, CELLS), F32), shape((NDEV, 128), F32)],
        [pltpu.VMEM((1152, CELLS), BF16), pltpu.VMEM((1024, X), F32)],
        2 * 256 * 1152 * CELLS,
        20,
    )
    stats = lax.all_to_all(stats, AXES, 0, 0, tiled=True)
    working = [
        pltpu.VMEM((C * 2 * Y, X), F32),
        pltpu.VMEM((C * 2 * Y, X), F32),
        pltpu.VMEM((4 * C, CELLS), BF16),
    ]
    d_real, real_terms = call(
        real_kernel,
        "real_branch",
        (real.reshape(G * 64, 2 * X), real_prev, real_next, weight, cot_real.reshape(C * 2 * Y, X)),
        [shape((C * 2 * Y, X), BF16), shape((1024, 2 * C), F32)],
        [
            pltpu.VMEM((6 * 512, CELLS), BF16),
            pltpu.VMEM((2, 3072, X), F32),
            pltpu.VMEM((3072, 2 * X), BF16),
        ]
        + working,
        8 * 2048 * C * CELLS * 2,
        28,
    )
    at = lax.axis_index("slab")
    inside = jnp.stack([at > 0, at < lax.axis_size("slab") - 1]).astype(jnp.int32)
    d_fake, low, high, terms = call(
        fake_kernel,
        "fake_branch",
        (
            inside,
            first,
            middle,
            last,
            stats,
            jnp.pad(bn_gain, (0, 128 - G)).reshape(1, 128),
            jnp.pad(bn_shift, (0, 128 - G)).reshape(1, 128),
            weight,
            cot_fake.reshape(C * 2 * Y, X),
            real_terms,
        ),
        [
            shape((C * 2 * Y, X), BF16),
            shape((C, CELLS), BF16),
            shape((C, CELLS), BF16),
            shape((NDEV * 8, 128), F32),
        ],
        [pltpu.VMEM((6 * 512, CELLS), BF16)] + working,
        8 * 2048 * C * CELLS * 2,
        28,
        smem=(0,),
    )
    parts = lax.all_to_all(terms.reshape(NDEV, 8, 128), AXES, 0, 0, tiled=True)
    grad_prev, grad_next = exchange(low, high)
    (sums,) = call(
        sum_kernel,
        "sum_terms",
        (parts.reshape(NDEV * 8, 128), grad_prev, grad_next),
        [shape((NDEV * 8, 128), BF16)],
        [],
        NDEV * 1024,
        8,
        unread=(1, 2),
    )
    whole = lax.all_to_all(sums.reshape(NDEV, 8, 128), AXES, 0, 0, tiled=True)
    (fake_grad,) = call(
        pullback_kernel,
        "pullback",
        (grad_prev, low, high, grad_next, taps_d, sums),
        [shape((G * 64, 2 * X), BF16)],
        [
            pltpu.VMEM((256, 1152), BF16),
            pltpu.VMEM((4 * 576, CELLS), BF16),
            pltpu.VMEM((2, G * 64, X), F32),
        ],
        2 * 512 * 1152 * CELLS,
        24,
        unread=(5,),
    )
    (weight_grad,) = call(
        unpack_kernel,
        "unpack",
        (whole.reshape(NDEV * 8, 128),),
        [shape((2048, C), F32)],
        [],
        0,
        8,
    )
    return (
        d_fake.reshape(1, C, 2, Y, X),
        d_real.reshape(1, C, 2, Y, X),
        fake_grad.reshape(1, G, 4, 2 * Y, 2 * X),
        weight_grad.reshape(4, 4, 4, G, C),
    )


def solution(mesh):
    split = P(("section", "rep"), None, "slab", None, None)
    in_specs = (split, P(), P(), P(), split, P(), split, split)
    out_specs = (split, split, split, P())
    return jax.shard_map(local, mesh=mesh, in_specs=in_specs, out_specs=out_specs, check_vma=False)
```

```python
import jax
import jax.numpy as jnp
from jax import lax
from jax.experimental import pallas as pl
from jax.experimental.pallas import tpu as pltpu
from jax.sharding import PartitionSpec as P

AXES = ("section", "slab", "rep")
NDEV = 128
C = 64
G = 32
Y = 8
X = 128
CELLS = Y * X
F32 = jnp.float32
BF16 = jnp.bfloat16

phase_taps = (((1, 0), (3, -1)), ((0, 1), (2, 0)))


def dot(a, b, dims=(1, 0)):
    return lax.dot_general(a, b, (((dims[0],), (dims[1],)), ((), ())), preferred_element_type=F32)


def lanes(shape):
    return lax.broadcasted_iota(jnp.int32, shape, len(shape) - 1)


def from_left(tile, lane):
    return jnp.where(lane == 0, 0.0, pltpu.roll(tile, 1, 1))


def from_right(tile, lane):
    return jnp.where(lane == X - 1, 0.0, pltpu.roll(tile, X - 1, 1))


def spread_weights(taps_ref, wide_ref):
    wide_ref[...] = jnp.zeros_like(wide_ref)
    for pz in range(2):
        for py in range(2):
            for px in range(2):
                row = ((1 - pz) * 4 + py * 2 + px) * G
                for kz, oz in phase_taps[pz]:
                    tz = oz if pz == 1 else oz + 1
                    for ky, oy in phase_taps[py]:
                        for kx, ox in phase_taps[px]:
                            col = tz * 576 + (oy + 1) * 192 + (ox + 1) * 64
                            tap = (kz * 16 + ky * 4 + kx) * G
                            wide_ref[row : row + G, col : col + C] = taps_ref[tap : tap + G, :]


def spread_cells(tile, depth, y, lane, patch_ref):
    for xi, moved in ((0, from_left(tile, lane)), (1, tile), (2, from_right(tile, lane))):
        piece = moved.astype(BF16)
        for yi in range(3):
            to = y - (yi - 1)
            if 0 <= to < Y:
                row = depth * 576 + yi * 192 + xi * 64
                patch_ref[row : row + C, to * X : (to + 1) * X] = piece


def clear_rims(depth, patch_ref):
    edge = jnp.zeros((192, X), BF16)
    patch_ref[depth * 576 : depth * 576 + 192, 0:X] = edge
    patch_ref[depth * 576 + 384 : depth * 576 + 576, CELLS - X : CELLS] = edge


def fetch(source, target, sem):
    copy = pltpu.make_async_copy(source, target, sem)
    copy.start()
    return copy


def as_row(column, shift):
    sub = lax.broadcasted_iota(jnp.int32, (G, 128), 0)
    return jnp.sum(jnp.where(lanes((G, 128)) == sub + shift, column, 0.0), axis=0, keepdims=True)


def as_column(row, shift):
    shape = (G, row.shape[1])
    sub = lax.broadcasted_iota(jnp.int32, shape, 0)
    return jnp.sum(jnp.where(lanes(shape) == sub + shift, row, 0.0), axis=1, keepdims=True)


def own_kernel(lat_ref, taps_ref, taps_d_ref, wide_ref, first_ref, middle_ref, last_ref, weight_ref, patch, wide_lat):
    spread_weights(taps_ref, wide_ref)
    wide_lat[...] = lat_ref[...].astype(F32)
    lane = lanes((C, X))
    for depth in range(2):
        clear_rims(depth, patch)
        for y in range(Y):
            spread_cells(wide_lat[pl.ds(depth * Y + y, C, stride=16), :], depth, y, lane, patch)
    first_ref[...] = dot(wide_ref[:, 576:1152], patch[0:576, :])
    middle_ref[...] = dot(wide_ref[...], patch[...])
    last_ref[...] = dot(wide_ref[:, 0:576], patch[576:1152, :])
    same = lax.broadcasted_iota(jnp.int32, (C, C), 0) == lanes((C, C))
    unit = jnp.where(same, 1.0, 0.0).astype(BF16)
    weight_ref[...] = dot(unit, taps_d_ref[...], (1, 1)).astype(BF16)


def rim_kernel(
    prev_ref,
    next_ref,
    wide_ref,
    first_in,
    middle_in,
    last_in,
    real_ref,
    first_out,
    middle_out,
    last_out,
    stats_ref,
    low_out,
    high_out,
    patch,
    wide_lat,
    first,
    last,
    sems,
):
    copies = [
        fetch(real_ref.at[:, 0], low_out, sems.at[0]),
        fetch(real_ref.at[:, 3], high_out, sems.at[1]),
        fetch(middle_in, middle_out, sems.at[2]),
    ]
    wide_lat[0:512, :] = prev_ref[...].astype(F32)
    wide_lat[512:1024, :] = next_ref[...].astype(F32)
    lane = lanes((C, X))
    for side in range(2):
        clear_rims(side, patch)
        for y in range(Y):
            spread_cells(wide_lat[pl.ds(side * 512 + y, C, stride=8), :], side, y, lane, patch)
    first[...] = first_in[...] + dot(wide_ref[:, 0:576], patch[0:576, :])
    copies.append(fetch(first, first_out, sems.at[3]))
    last[...] = last_in[...] + dot(wide_ref[:, 576:1152], patch[576:1152, :])
    copies.append(fetch(last, last_out, sems.at[4]))
    count = 16.0 * CELLS
    blocks = [(first, r) for r in range(4, 8)] + [(middle_in, r) for r in range(8)]
    blocks += [(last, r) for r in range(4)]
    total = jnp.zeros((G, CELLS), F32)
    for ref, block in blocks:
        total += ref[block * G : (block + 1) * G, :]
    mean = jnp.sum(total, axis=1, keepdims=True) * (1.0 / count)
    squares = jnp.zeros((G, CELLS), F32)
    for ref, block in blocks:
        off = ref[block * G : (block + 1) * G, :] - mean
        squares += off * off
    spread = jnp.sum(squares, axis=1, keepdims=True)
    stats_ref[...] = jnp.broadcast_to(as_row(mean, 0) + as_row(spread, G), (NDEV, 128))
    for copy in copies:
        copy.wait()


def activate(before):
    squashed = jax.nn.sigmoid(4.0 * before)
    output = before * (0.2 + 0.8 * squashed)
    derivative = 0.2 + 0.8 * squashed + 3.2 * before * squashed * (1.0 - squashed)
    return (output, derivative)


def finish(pre, cot_ref, out_ref, wide_cot, wide_out, grad):
    wide_cot[...] = cot_ref[...].astype(F32)
    nothing = jnp.zeros((C, CELLS), BF16)
    grad[0:C, :] = nothing
    grad[3 * C : 4 * C, :] = nothing
    for m in range(2):
        for y in range(Y):
            output, slope = activate(pre[m][:, y * X : (y + 1) * X])
            wide_out[pl.ds(m * Y + y, C, stride=16), :] = output
            cot = wide_cot[pl.ds(m * Y + y, C, stride=16), :]
            grad[(2 - m) * C : (3 - m) * C, y * X : (y + 1) * X] = (cot * slope).astype(BF16)
    out_ref[...] = wide_out[...].astype(BF16)


def kernel_terms(planes, grad):
    halves = []
    for half in range(2):
        terms = dot(planes[half], grad[128:256, :], (1, 1))
        terms += dot(planes[half + 2], grad[64:192, :], (1, 1))
        halves.append(terms + dot(planes[half + 4], grad[0:128, :], (1, 1)))
    return halves


def split_depth(at, places, halves, rows, patch):
    base, stride = places
    column = lanes((2 * X, 4 * X))
    source = lax.broadcasted_iota(jnp.int32, (2 * X, 4 * X), 0)
    pick = jnp.where(source == 2 * (column % X) + column // X - 1, 1.0, 0.0).astype(BF16)
    edge = jnp.zeros((128, X), BF16)
    patch[at : at + 128, 0:X] = edge
    patch[at + 384 : at + 512, CELLS - X : CELLS] = edge
    for row in range(2 * Y):
        for half in range(2):
            cells = halves[half, pl.ds(base + row, G, stride=stride), :].astype(BF16)
            rows[at + row * G : at + (row + 1) * G, half * X : (half + 1) * X] = cells
    split = dot(rows[at : at + 512, :], pick).astype(BF16)
    for row in range(2 * Y):
        for kx in range(4):
            piece = split[row * G : (row + 1) * G, kx * X : (kx + 1) * X]
            for ky in range(4):
                if (row + 1 - ky) % 2 == 0 and 0 <= (row + 1 - ky) // 2 < Y:
                    y = (row + 1 - ky) // 2
                    place = at + ky * 128 + kx * G
                    patch[place : place + G, y * X : (y + 1) * X] = piece


def real_own_kernel(real_ref, weight_ref, low_ref, patch_ref, pre_ref, halves, rows):
    del low_ref
    for half in range(2):
        halves[half] = real_ref[:, half * X : (half + 1) * X].astype(F32)
    for depth in range(4):
        split_depth(depth * 512, (depth * 16, 64), halves, rows, patch_ref)
    late_early = jnp.concatenate([weight_ref[:, 1024:2048], weight_ref[:, 0:1024]], axis=0)
    both = dot(late_early, patch_ref[512:1536, :])
    pre_ref[0:C, :] = both[0:C, :] + dot(weight_ref[:, 512:1024], patch_ref[0:512, :])
    pre_ref[C : 2 * C, :] = both[C : 2 * C, :] + dot(weight_ref[:, 1024:1536], patch_ref[1536:2048, :])


def real_kernel(
    prev_ref,
    next_ref,
    own_ref,
    pre_ref,
    weight_ref,
    cot_ref,
    out_ref,
    terms_out,
    terms_ref,
    sem,
    patch,
    halves,
    rows,
    wide_cot,
    wide_out,
    grad,
):
    for half in range(2):
        halves[half, 0:512, :] = prev_ref[:, half * X : (half + 1) * X].astype(F32)
        halves[half, 512:1024, :] = next_ref[:, half * X : (half + 1) * X].astype(F32)
    for side in range(2):
        split_depth(side * 512, (side * 512, 16), halves, rows, patch)
    pre = (
        pre_ref[0:C, :] + dot(weight_ref[:, 0:512], patch[0:512, :]),
        pre_ref[C : 2 * C, :] + dot(weight_ref[:, 1536:2048], patch[512:1024, :]),
    )
    finish(pre, cot_ref, out_ref, wide_cot, wide_out, grad)
    own = [own_ref[depth * 512 : (depth + 1) * 512, :] for depth in range(4)]
    planes = [patch[0:512, :]] + own + [patch[512:1024, :]]
    for half, terms in enumerate(kernel_terms(planes, grad)):
        terms_ref[half * 512 : (half + 1) * 512, :] = terms
    fetch(terms_ref, terms_out, sem).wait()


def fake_kernel(
    inside_ref,
    first_in,
    middle_in,
    last_in,
    stats_ref,
    gain_ref,
    shift_ref,
    weight_ref,
    cot_ref,
    real_terms_in,
    out_ref,
    low_ref,
    high_ref,
    terms_ref,
    before,
    real_terms,
    sems,
    patch,
    wide_cot,
    wide_out,
    grad,
):
    befores = [
        fetch(ref, before.at[i], sems.at[i]) for i, ref in enumerate((first_in, middle_in, last_in))
    ]
    real_copy = fetch(real_terms_in, real_terms, sems.at[3])
    stats = stats_ref[...]
    count = 16.0 * CELLS
    sums = jnp.sum(stats, axis=0, keepdims=True)
    mean_row = sums * (1.0 / NDEV)
    off = stats - mean_row
    between = as_column(jnp.sum(off * off, axis=0, keepdims=True), 0)
    center = as_column(mean_row, 0)
    variance = (as_column(sums, G) + count * between) * (1.0 / (count * NDEV))
    factor = as_column(gain_ref[...], 0) * lax.rsqrt(variance + 1e-05)
    shift = as_column(shift_ref[...], 0)
    lane = lanes((G, X))
    edge = jnp.zeros((128, X), BF16)
    for depth in range(6):
        if depth % 2 == 0:
            befores[depth // 2].wait()
        patch[depth * 512 : depth * 512 + 128, 0:X] = edge
        patch[depth * 512 + 384 : depth * 512 + 512, CELLS - X : CELLS] = edge
        for py in range(2):
            for px in range(2):
                block = (depth % 2 * 4 + py * 2 + px) * G
                for y in range(Y):
                    cells = before[depth // 2, block : block + G, y * X : (y + 1) * X]
                    fake = jnp.maximum((cells - center) * factor + shift, 0.0)
                    if depth == 0:
                        fake = jnp.where(inside_ref[0] > 0, fake, 0.0)
                    if depth == 5:
                        fake = jnp.where(inside_ref[1] > 0, fake, 0.0)
                    if px == 1:
                        pieces = ((2, fake), (0, from_left(fake, lane)))
                    else:
                        pieces = ((1, fake), (3, from_right(fake, lane)))
                    for kx, piece in pieces:
                        piece = piece.astype(BF16)
                        for ky, to in ((2, y), (0, y + 1)) if py == 1 else ((1, y), (3, y - 1)):
                            if 0 <= to < Y:
                                at = depth * 512 + ky * 128 + kx * G
                                patch[at : at + G, to * X : (to + 1) * X] = piece
    early = weight_ref[:, 0:1024]
    late = weight_ref[:, 1024:2048]
    shared = dot(jnp.concatenate([late, early], axis=0), patch[1024:2048, :])
    pre = (
        dot(early, patch[0:1024, :]) + shared[0:C, :],
        shared[C : 2 * C, :] + dot(late, patch[2048:3072, :]),
    )
    finish(pre, cot_ref, out_ref, wide_cot, wide_out, grad)
    low_ref[...] = grad[2 * C : 3 * C, :]
    high_ref[...] = grad[C : 2 * C, :]
    planes = [patch[depth * 512 : (depth + 1) * 512, :] for depth in range(6)]
    real_copy.wait()
    for half, terms in enumerate(kernel_terms(planes, grad)):
        rows = slice(half * 512, (half + 1) * 512)
        terms_ref[rows, :] = terms + real_terms[rows, :]


def sum_kernel(parts_ref, edge_ref, sums_ref):
    del edge_ref
    total = jnp.sum(parts_ref[...].reshape(NDEV, 8, 128), axis=0, keepdims=True)
    sums_ref[...] = jnp.broadcast_to(total, (NDEV, 8, 128)).reshape(NDEV * 8, 128).astype(BF16)


def unpack_kernel(sums_ref, out_ref):
    sums = sums_ref[...].astype(F32)
    out_ref[0:1024, :] = sums[:, 0:C]
    out_ref[1024:2048, :] = sums[:, C : 2 * C]


def pullback_kernel(prev_ref, low_ref, high_ref, next_ref, taps_ref, sums_ref, out_ref, wide, patch, wide_out):
    del sums_ref
    spread_weights(taps_ref, wide)
    lane = lanes((C, X))
    for depth, ref in enumerate((prev_ref, low_ref, high_ref, next_ref)):
        clear_rims(depth, patch)
        for y in range(Y):
            spread_cells(ref[:, y * X : (y + 1) * X].astype(F32), depth, y, lane, patch)
    column = lax.broadcasted_iota(jnp.int32, (2 * X, 2 * X), 1)
    source = lax.broadcasted_iota(jnp.int32, (2 * X, 2 * X), 0)
    weave = jnp.where(source == (column % 2) * X + column // 2, 1.0, 0.0).astype(BF16)
    for pair, first, depths in ((0, 128, (0,)), (1, 0, (1, 2)), (2, 0, (3,))):
        rows = 128 * len(depths)
        result = dot(wide[first : first + rows, :], patch[pair * 576 : pair * 576 + 1152, :])
        result = result.astype(BF16)
        for at, depth in enumerate(depths):
            for py in range(2):
                even = result[at * 128 + py * 64 : at * 128 + py * 64 + G, :]
                odd = result[at * 128 + py * 64 + G : at * 128 + py * 64 + 2 * G, :]
                both = jnp.concatenate(
                    [
                        jnp.concatenate([even[:, y * X : (y + 1) * X], odd[:, y * X : (y + 1) * X]], axis=1)
                        for y in range(Y)
                    ],
                    axis=0,
                )
                woven = dot(both, weave)
                for y in range(Y):
                    place = pl.ds(depth * 16 + 2 * y + py, G, stride=64)
                    wide_out[0, place, :] = woven[y * G : (y + 1) * G, 0:X]
                    wide_out[1, place, :] = woven[y * G : (y + 1) * G, X : 2 * X]
    out_ref[:, 0:X] = wide_out[0].astype(BF16)
    out_ref[:, X : 2 * X] = wide_out[1].astype(BF16)


def call(body, name, args, outs, scratch, flops, mebibytes, smem=(), far=(), far_outs=()):
    moved = sum(a.size * a.dtype.itemsize for a in args) + sum(o.size * o.dtype.itemsize for o in outs)
    spaces = [
        pltpu.SMEM if i in smem else pl.ANY if i in far else pltpu.VMEM for i in range(len(args))
    ]
    out_spaces = [pltpu.HBM if i in far_outs else pltpu.VMEM for i in range(len(outs))]
    outs = [pltpu.HBM(o.shape, o.dtype) if i in far_outs else o for i, o in enumerate(outs)]
    args = [
        pltpu.with_memory_space_constraint(a, pltpu.HBM) if i in far else a for i, a in enumerate(args)
    ]
    return pl.pallas_call(
        body,
        name=name,
        out_shape=outs,
        in_specs=[pl.BlockSpec(memory_space=space) for space in spaces],
        out_specs=[pl.BlockSpec(memory_space=space) for space in out_spaces],
        scratch_shapes=scratch,
        compiler_params=pltpu.CompilerParams(vmem_limit_bytes=mebibytes * 1024 * 1024),
        cost_estimate=pl.CostEstimate(flops=flops, bytes_accessed=moved, transcendentals=0),
    )(*args)


def exchange(low, high):
    ends = lax.axis_size("slab") - 1
    before = lax.ppermute(high, "slab", [(i, i + 1) for i in range(ends)])
    after = lax.ppermute(low, "slab", [(i + 1, i) for i in range(ends)])
    return before, after


def local(latent, g_weight, bn_gain, bn_shift, real_crops, d_weight, cot_fake, cot_real):
    shape = jax.ShapeDtypeStruct
    taps_g = g_weight.transpose(0, 1, 2, 4, 3).reshape(64 * G, C)
    taps_d = d_weight.reshape(64 * G, C)
    lat = latent[0]
    lat_prev, lat_next = exchange(lat[:, 0].reshape(C * Y, X), lat[:, 1].reshape(C * Y, X))
    real = real_crops[0]
    wide, first, middle, last, weight = call(
        own_kernel,
        "own_cells",
        (lat.reshape(C * 2 * Y, X), taps_g, taps_d),
        [shape((256, 1152), BF16)] + [shape((256, CELLS), F32)] * 3 + [shape((C, 2048), BF16)],
        [pltpu.VMEM((1152, CELLS), BF16), pltpu.VMEM((1024, X), F32)],
        4 * 256 * 1152 * CELLS,
        16,
    )
    first, middle, last, stats, real_low, real_high = call(
        rim_kernel,
        "rim_cells",
        (lat_prev, lat_next, wide, first, middle, last, real),
        [shape((256, CELLS), F32)] * 3
        + [shape((NDEV, 128), F32)]
        + [shape((G, 2 * Y, 2 * X), BF16)] * 2,
        [
            pltpu.VMEM((1152, CELLS), BF16),
            pltpu.VMEM((1024, X), F32),
            pltpu.VMEM((256, CELLS), F32),
            pltpu.VMEM((256, CELLS), F32),
            pltpu.SemaphoreType.DMA((5,)),
        ],
        2 * 256 * 1152 * CELLS,
        20,
        far=(6,),
        far_outs=(0, 1, 2, 4, 5),
    )
    stats = lax.all_to_all(stats, AXES, 0, 0, tiled=True)
    real_prev, real_next = exchange(real_low, real_high)
    real_patch, real_pre = call(
        real_own_kernel,
        "real_own",
        (real.reshape(G * 64, 2 * X), weight, real_low),
        [shape((2048, CELLS), BF16), shape((2 * C, CELLS), F32)],
        [pltpu.VMEM((2, 2048, X), F32), pltpu.VMEM((2048, 2 * X), BF16)],
        4 * 2048 * C * CELLS,
        16,
        far=(2,),
    )
    working = [
        pltpu.VMEM((C * 2 * Y, X), F32),
        pltpu.VMEM((C * 2 * Y, X), F32),
        pltpu.VMEM((4 * C, CELLS), BF16),
    ]
    d_real, real_terms = call(
        real_kernel,
        "real_branch",
        (
            real_prev.reshape(G * 16, 2 * X),
            real_next.reshape(G * 16, 2 * X),
            real_patch,
            real_pre,
            weight,
            cot_real.reshape(C * 2 * Y, X),
        ),
        [shape((C * 2 * Y, X), BF16), shape((1024, 2 * C), F32)],
        [
            pltpu.VMEM((1024, 2 * C), F32),
            pltpu.SemaphoreType.DMA,
            pltpu.VMEM((1024, CELLS), BF16),
            pltpu.VMEM((2, 1024, X), F32),
            pltpu.VMEM((1024, 2 * X), BF16),
        ]
        + working,
        8 * 2048 * C * CELLS,
        20,
        far_outs=(1,),
    )
    at = lax.axis_index("slab")
    inside = jnp.stack([at > 0, at < lax.axis_size("slab") - 1]).astype(jnp.int32)
    d_fake, low, high, terms = call(
        fake_kernel,
        "fake_branch",
        (
            inside,
            first,
            middle,
            last,
            stats,
            bn_gain.reshape(1, G),
            bn_shift.reshape(1, G),
            weight,
            cot_fake.reshape(C * 2 * Y, X),
            real_terms,
        ),
        [
            shape((C * 2 * Y, X), BF16),
            shape((C, CELLS), BF16),
            shape((C, CELLS), BF16),
            shape((NDEV * 8, 128), F32),
        ],
        [
            pltpu.VMEM((3, 256, CELLS), F32),
            pltpu.VMEM((NDEV * 8, 128), F32),
            pltpu.SemaphoreType.DMA((4,)),
            pltpu.VMEM((6 * 512, CELLS), BF16),
        ]
        + working,
        8 * 2048 * C * CELLS * 2,
        28,
        smem=(0,),
        far=(1, 2, 3, 9),
    )
    parts = lax.all_to_all(terms.reshape(NDEV, 8, 128), AXES, 0, 0, tiled=True)
    grad_prev, grad_next = exchange(low, high)
    (sums,) = call(
        sum_kernel,
        "sum_terms",
        (parts.reshape(NDEV * 8, 128), grad_prev),
        [shape((NDEV * 8, 128), BF16)],
        [],
        NDEV * 1024,
        8,
        far=(1,),
    )
    whole = lax.all_to_all(sums.reshape(NDEV, 8, 128), AXES, 0, 0, tiled=True)
    (fake_grad,) = call(
        pullback_kernel,
        "pullback",
        (grad_prev, low, high, grad_next, taps_d, sums),
        [shape((G * 64, 2 * X), BF16)],
        [
            pltpu.VMEM((256, 1152), BF16),
            pltpu.VMEM((4 * 576, CELLS), BF16),
            pltpu.VMEM((2, G * 64, X), F32),
        ],
        2 * 512 * 1152 * CELLS,
        24,
        far=(5,),
    )
    (weight_grad,) = call(
        unpack_kernel,
        "unpack",
        (whole.reshape(NDEV * 8, 128),),
        [shape((2048, C), F32)],
        [],
        0,
        8,
    )
    return (
        d_fake.reshape(1, C, 2, Y, X),
        d_real.reshape(1, C, 2, Y, X),
        fake_grad.reshape(1, G, 4, 2 * Y, 2 * X),
        weight_grad.reshape(4, 4, 4, G, C),
    )


def solution(mesh):
    split = P(("section", "rep"), None, "slab", None, None)
    in_specs = (split, P(), P(), P(), split, P(), split, split)
    out_specs = (split, split, split, P())
    return jax.shard_map(local, mesh=mesh, in_specs=in_specs, out_specs=out_specs, check_vma=False)
```

```python
import jax
import jax.numpy as jnp
from jax import lax
from jax.experimental import pallas as pl
from jax.experimental.pallas import tpu as pltpu
from jax.sharding import PartitionSpec as P

AXES = ("section", "slab", "rep")
NDEV = 128
C = 64
G = 32
Y = 8
X = 128
CELLS = Y * X
F32 = jnp.float32
BF16 = jnp.bfloat16

phase_taps = (((1, 0), (3, -1)), ((0, 1), (2, 0)))


def dot(a, b, dims=(1, 0)):
    return lax.dot_general(a, b, (((dims[0],), (dims[1],)), ((), ())), preferred_element_type=F32)


def lanes(shape):
    return lax.broadcasted_iota(jnp.int32, shape, len(shape) - 1)


def from_left(tile, lane):
    return jnp.where(lane == 0, 0.0, pltpu.roll(tile, 1, 1))


def from_right(tile, lane):
    return jnp.where(lane == X - 1, 0.0, pltpu.roll(tile, X - 1, 1))


def spread_weights(taps_ref, wide_ref):
    wide_ref[...] = jnp.zeros_like(wide_ref)
    for pz in range(2):
        for py in range(2):
            for px in range(2):
                row = ((1 - pz) * 4 + py * 2 + px) * G
                for kz, oz in phase_taps[pz]:
                    tz = oz if pz == 1 else oz + 1
                    for ky, oy in phase_taps[py]:
                        for kx, ox in phase_taps[px]:
                            col = tz * 576 + (oy + 1) * 192 + (ox + 1) * 64
                            tap = (kz * 16 + ky * 4 + kx) * G
                            wide_ref[row : row + G, col : col + C] = taps_ref[tap : tap + G, :]


def spread_cells(tile, depth, y, lane, patch_ref):
    for xi, moved in ((0, from_left(tile, lane)), (1, tile), (2, from_right(tile, lane))):
        piece = moved.astype(BF16)
        for yi in range(3):
            to = y - (yi - 1)
            if 0 <= to < Y:
                row = depth * 576 + yi * 192 + xi * 64
                patch_ref[row : row + C, to * X : (to + 1) * X] = piece


def clear_rims(depth, patch_ref):
    edge = jnp.zeros((192, X), BF16)
    patch_ref[depth * 576 : depth * 576 + 192, 0:X] = edge
    patch_ref[depth * 576 + 384 : depth * 576 + 576, CELLS - X : CELLS] = edge


def fetch(source, target, sem):
    copy = pltpu.make_async_copy(source, target, sem)
    copy.start()
    return copy


def as_row(column, shift):
    sub = lax.broadcasted_iota(jnp.int32, (G, 128), 0)
    return jnp.sum(jnp.where(lanes((G, 128)) == sub + shift, column, 0.0), axis=0, keepdims=True)


def as_column(row, shift):
    shape = (G, row.shape[1])
    sub = lax.broadcasted_iota(jnp.int32, shape, 0)
    return jnp.sum(jnp.where(lanes(shape) == sub + shift, row, 0.0), axis=1, keepdims=True)


def edge_kernel(lat_ref, real_ref, low_ref, high_ref, lat_edge, real_edge, sems):
    copies = []
    for side in range(2):
        copies.append(fetch(lat_ref.at[:, side], lat_edge.at[side], sems.at[2 * side]))
        copies.append(fetch(real_ref.at[:, 3 * side], real_edge.at[side], sems.at[2 * side + 1]))
    for side, ref in enumerate((low_ref, high_ref)):
        copies[2 * side].wait()
        ref[0:512, :] = lat_edge[side].reshape(512, X)
        copies[2 * side + 1].wait()
        edge = real_edge[side].reshape(512, 2 * X)
        ref[512:1024, :] = edge[:, 0:X]
        ref[1024:1536, :] = edge[:, X : 2 * X]


def own_kernel(
    lat_in,
    taps_in,
    taps_d_in,
    wide_ref,
    first_ref,
    middle_ref,
    last_ref,
    weight_out,
    lat,
    taps,
    taps_d,
    weight,
    sems,
    patch,
    wide_lat,
):
    copies = [
        fetch(lat_in, lat, sems.at[0]),
        fetch(taps_in, taps, sems.at[1]),
        fetch(taps_d_in, taps_d, sems.at[2]),
    ]
    copies[0].wait()
    wide_lat[...] = lat[...].astype(F32)
    lane = lanes((C, X))
    for depth in range(2):
        clear_rims(depth, patch)
        for y in range(Y):
            spread_cells(wide_lat[pl.ds(depth * Y + y, C, stride=16), :], depth, y, lane, patch)
    copies[2].wait()
    same = lax.broadcasted_iota(jnp.int32, (C, C), 0) == lanes((C, C))
    unit = jnp.where(same, 1.0, 0.0).astype(BF16)
    weight[...] = dot(unit, taps_d[...], (1, 1)).astype(BF16)
    weight_copy = fetch(weight, weight_out, sems.at[3])
    copies[1].wait()
    spread_weights(taps, wide_ref)
    first_ref[...] = dot(wide_ref[:, 576:1152], patch[0:576, :])
    middle_ref[...] = dot(wide_ref[...], patch[...])
    last_ref[...] = dot(wide_ref[:, 0:576], patch[576:1152, :])
    weight_copy.wait()


def rim_kernel(
    prev_ref,
    next_ref,
    wide_ref,
    first_in,
    middle_in,
    last_in,
    pre_ref,
    first_out,
    middle_out,
    last_out,
    stats_ref,
    real_prev_out,
    real_next_out,
    patch,
    wide_lat,
    first,
    last,
    sems,
):
    del pre_ref
    copies = [
        fetch(prev_ref.at[512:1536], real_prev_out, sems.at[0]),
        fetch(next_ref.at[512:1536], real_next_out, sems.at[1]),
        fetch(middle_in, middle_out, sems.at[2]),
    ]
    wide_lat[0:512, :] = prev_ref[0:512, :].astype(F32)
    wide_lat[512:1024, :] = next_ref[0:512, :].astype(F32)
    lane = lanes((C, X))
    for side in range(2):
        clear_rims(side, patch)
        for y in range(Y):
            spread_cells(wide_lat[pl.ds(side * 512 + y, C, stride=8), :], side, y, lane, patch)
    first[...] = first_in[...] + dot(wide_ref[:, 0:576], patch[0:576, :])
    copies.append(fetch(first, first_out, sems.at[3]))
    last[...] = last_in[...] + dot(wide_ref[:, 576:1152], patch[576:1152, :])
    copies.append(fetch(last, last_out, sems.at[4]))
    count = 16.0 * CELLS
    blocks = [(first, r) for r in range(4, 8)] + [(middle_in, r) for r in range(8)]
    blocks += [(last, r) for r in range(4)]
    total = jnp.zeros((G, CELLS), F32)
    for ref, block in blocks:
        total += ref[block * G : (block + 1) * G, :]
    mean = jnp.sum(total, axis=1, keepdims=True) * (1.0 / count)
    squares = jnp.zeros((G, CELLS), F32)
    for ref, block in blocks:
        off = ref[block * G : (block + 1) * G, :] - mean
        squares += off * off
    spread = jnp.sum(squares, axis=1, keepdims=True)
    stats_ref[...] = jnp.broadcast_to(as_row(mean, 0) + as_row(spread, G), (NDEV, 128))
    for copy in copies:
        copy.wait()


def activate(before):
    squashed = jax.nn.sigmoid(4.0 * before)
    output = before * (0.2 + 0.8 * squashed)
    derivative = 0.2 + 0.8 * squashed + 3.2 * before * squashed * (1.0 - squashed)
    return (output, derivative)


def finish(pre, cot_ref, out_ref, wide_cot, wide_out, grad):
    wide_cot[...] = cot_ref[...].astype(F32)
    nothing = jnp.zeros((C, CELLS), BF16)
    grad[0:C, :] = nothing
    grad[3 * C : 4 * C, :] = nothing
    for m in range(2):
        for y in range(Y):
            output, slope = activate(pre[m][:, y * X : (y + 1) * X])
            wide_out[pl.ds(m * Y + y, C, stride=16), :] = output
            cot = wide_cot[pl.ds(m * Y + y, C, stride=16), :]
            grad[(2 - m) * C : (3 - m) * C, y * X : (y + 1) * X] = (cot * slope).astype(BF16)
    out_ref[...] = wide_out[...].astype(BF16)


def kernel_terms(planes, grad):
    halves = []
    for half in range(2):
        terms = dot(planes[half], grad[128:256, :], (1, 1))
        terms += dot(planes[half + 2], grad[64:192, :], (1, 1))
        halves.append(terms + dot(planes[half + 4], grad[0:128, :], (1, 1)))
    return halves


def split_depth(at, places, halves, rows, patch):
    base, stride = places
    column = lanes((2 * X, 4 * X))
    source = lax.broadcasted_iota(jnp.int32, (2 * X, 4 * X), 0)
    pick = jnp.where(source == 2 * (column % X) + column // X - 1, 1.0, 0.0).astype(BF16)
    edge = jnp.zeros((128, X), BF16)
    patch[at : at + 128, 0:X] = edge
    patch[at + 384 : at + 512, CELLS - X : CELLS] = edge
    for row in range(2 * Y):
        for half in range(2):
            cells = halves[half, pl.ds(base + row, G, stride=stride), :].astype(BF16)
            rows[at + row * G : at + (row + 1) * G, half * X : (half + 1) * X] = cells
    split = dot(rows[at : at + 512, :], pick).astype(BF16)
    for row in range(2 * Y):
        for kx in range(4):
            piece = split[row * G : (row + 1) * G, kx * X : (kx + 1) * X]
            for ky in range(4):
                if (row + 1 - ky) % 2 == 0 and 0 <= (row + 1 - ky) // 2 < Y:
                    y = (row + 1 - ky) // 2
                    place = at + ky * 128 + kx * G
                    patch[place : place + G, y * X : (y + 1) * X] = piece


def real_own_kernel(real_in, weight_in, patch_out, pre_out, real, weight, patch, pre, sems, halves, rows):
    real_copies = []
    for part in range(4):
        piece = pl.ds(part * 512, 512)
        real_copies.append(fetch(real_in.at[piece], real.at[piece], sems.at[part]))
    weight_copy = fetch(weight_in, weight, sems.at[4])
    for part in range(4):
        real_copies[part].wait()
        for half in range(2):
            piece = slice(part * 512, (part + 1) * 512)
            halves[half, piece, :] = real[piece, half * X : (half + 1) * X].astype(F32)
    copies = []
    for depth in range(4):
        split_depth(depth * 512, (depth * 16, 64), halves, rows, patch)
        piece = pl.ds(depth * 512, 512)
        copies.append(fetch(patch.at[piece], patch_out.at[piece], sems.at[5 + depth]))
    weight_copy.wait()
    late_early = jnp.concatenate([weight[:, 1024:2048], weight[:, 0:1024]], axis=0)
    both = dot(late_early, patch[512:1536, :])
    pre[0:C, :] = both[0:C, :] + dot(weight[:, 512:1024], patch[0:512, :])
    pre[C : 2 * C, :] = both[C : 2 * C, :] + dot(weight[:, 1024:1536], patch[1536:2048, :])
    copies.append(fetch(pre, pre_out, sems.at[9]))
    for copy in copies:
        copy.wait()


def real_kernel(
    prev_in,
    next_in,
    own_in,
    pre_in,
    weight_in,
    cot_ref,
    out_ref,
    terms_out,
    terms_ref,
    sems,
    edges,
    own,
    pre_own,
    weight,
    patch,
    halves,
    rows,
    wide_cot,
    wide_out,
    grad,
):
    edge_copies = [
        fetch(prev_in, edges.at[0], sems.at[0]),
        fetch(next_in, edges.at[1], sems.at[1]),
    ]
    copies = [
        fetch(weight_in, weight, sems.at[2]),
        fetch(pre_in, pre_own, sems.at[3]),
    ]
    own_copy = fetch(own_in, own, sems.at[4])
    for side in range(2):
        edge_copies[side].wait()
        for half in range(2):
            cells = edges[side, half * 512 : (half + 1) * 512, :]
            halves[half, side * 512 : (side + 1) * 512, :] = cells.astype(F32)
        split_depth(side * 512, (side * 512, 16), halves, rows, patch)
    for copy in copies:
        copy.wait()
    pre = (
        pre_own[0:C, :] + dot(weight[:, 0:512], patch[0:512, :]),
        pre_own[C : 2 * C, :] + dot(weight[:, 1536:2048], patch[512:1024, :]),
    )
    finish(pre, cot_ref, out_ref, wide_cot, wide_out, grad)
    own_copy.wait()
    own_planes = [own[depth * 512 : (depth + 1) * 512, :] for depth in range(4)]
    planes = [patch[0:512, :]] + own_planes + [patch[512:1024, :]]
    for half, terms in enumerate(kernel_terms(planes, grad)):
        terms_ref[half * 512 : (half + 1) * 512, :] = terms
    fetch(terms_ref, terms_out, sems.at[5]).wait()


def fake_kernel(
    inside_ref,
    first_in,
    middle_in,
    last_in,
    stats_ref,
    gain_ref,
    shift_ref,
    weight_in,
    cot_ref,
    real_terms_in,
    out_ref,
    low_out,
    high_out,
    terms_ref,
    before,
    real_terms,
    weight_ref,
    sems,
    patch,
    wide_cot,
    wide_out,
    grad,
):
    befores = []
    for depth in range(6):
        ref = (first_in, middle_in, last_in)[depth // 2]
        half = pl.ds(depth % 2 * 128, 128)
        befores.append(fetch(ref.at[half], before.at[depth], sems.at[depth]))
    weight_copy = fetch(weight_in, weight_ref, sems.at[6])
    real_copy = fetch(real_terms_in, real_terms, sems.at[7])
    stats = stats_ref[...]
    count = 16.0 * CELLS
    sums = jnp.sum(stats, axis=0, keepdims=True)
    mean_row = sums * (1.0 / NDEV)
    off = stats - mean_row
    between = as_column(jnp.sum(off * off, axis=0, keepdims=True), 0)
    center = as_column(mean_row, 0)
    variance = (as_column(sums, G) + count * between) * (1.0 / (count * NDEV))
    factor = as_column(gain_ref[...], 0) * lax.rsqrt(variance + 1e-05)
    shift = as_column(shift_ref[...], 0)
    lane = lanes((G, X))
    edge = jnp.zeros((128, X), BF16)
    for depth in range(6):
        befores[depth].wait()
        patch[depth * 512 : depth * 512 + 128, 0:X] = edge
        patch[depth * 512 + 384 : depth * 512 + 512, CELLS - X : CELLS] = edge
        for py in range(2):
            for px in range(2):
                block = (py * 2 + px) * G
                for y in range(Y):
                    cells = before[depth, block : block + G, y * X : (y + 1) * X]
                    fake = jnp.maximum((cells - center) * factor + shift, 0.0)
                    if depth == 0:
                        fake = jnp.where(inside_ref[0] > 0, fake, 0.0)
                    if depth == 5:
                        fake = jnp.where(inside_ref[1] > 0, fake, 0.0)
                    if px == 1:
                        pieces = ((2, fake), (0, from_left(fake, lane)))
                    else:
                        pieces = ((1, fake), (3, from_right(fake, lane)))
                    for kx, piece in pieces:
                        piece = piece.astype(BF16)
                        for ky, to in ((2, y), (0, y + 1)) if py == 1 else ((1, y), (3, y - 1)):
                            if 0 <= to < Y:
                                at = depth * 512 + ky * 128 + kx * G
                                patch[at : at + G, to * X : (to + 1) * X] = piece
    weight_copy.wait()
    early = weight_ref[:, 0:1024]
    late = weight_ref[:, 1024:2048]
    shared = dot(jnp.concatenate([late, early], axis=0), patch[1024:2048, :])
    pre = (
        dot(early, patch[0:1024, :]) + shared[0:C, :],
        shared[C : 2 * C, :] + dot(late, patch[2048:3072, :]),
    )
    finish(pre, cot_ref, out_ref, wide_cot, wide_out, grad)
    edge_copies = [
        fetch(grad.at[2 * C : 3 * C], low_out, sems.at[8]),
        fetch(grad.at[C : 2 * C], high_out, sems.at[9]),
    ]
    planes = [patch[depth * 512 : (depth + 1) * 512, :] for depth in range(6)]
    real_copy.wait()
    for half, terms in enumerate(kernel_terms(planes, grad)):
        rows = slice(half * 512, (half + 1) * 512)
        terms_ref[rows, :] = terms + real_terms[rows, :]
    for copy in edge_copies:
        copy.wait()


def sum_kernel(parts_ref, prev_ref, next_ref, middle_ref, sums_ref):
    del prev_ref, next_ref, middle_ref
    total = jnp.sum(parts_ref[...].reshape(NDEV, 8, 128), axis=0, keepdims=True)
    sums_ref[...] = jnp.broadcast_to(total, (NDEV, 8, 128)).reshape(NDEV * 8, 128).astype(BF16)


def unpack_kernel(sums_ref, out_ref):
    sums = sums_ref[...].astype(F32)
    out_ref[0:1024, :] = sums[:, 0:C]
    out_ref[1024:2048, :] = sums[:, C : 2 * C]


def pull_own_kernel(
    low_in,
    high_in,
    taps_in,
    wide_out,
    first_out,
    middle_out,
    last_out,
    cells,
    taps,
    wide,
    first,
    middle,
    last,
    patch,
    sems,
):
    edges = [fetch(ref, cells.at[i], sems.at[i]) for i, ref in enumerate((low_in, high_in))]
    taps_copy = fetch(taps_in, taps, sems.at[2])
    lane = lanes((C, X))
    for depth in range(2):
        edges[depth].wait()
        clear_rims(depth, patch)
        for y in range(Y):
            spread_cells(cells[depth, :, y * X : (y + 1) * X].astype(F32), depth, y, lane, patch)
    taps_copy.wait()
    spread_weights(taps, wide)
    copies = [fetch(wide, wide_out, sems.at[3])]
    first[...] = dot(wide[128:256, 576:1152], patch[0:576, :])
    copies.append(fetch(first, first_out, sems.at[4]))
    middle[...] = dot(wide[...], patch[...]).astype(BF16)
    copies.append(fetch(middle, middle_out, sems.at[5]))
    last[...] = dot(wide[0:128, 0:576], patch[576:1152, :])
    copies.append(fetch(last, last_out, sems.at[6]))
    for copy in copies:
        copy.wait()


def pullback_kernel(
    prev_in,
    next_in,
    wide_in,
    first_in,
    middle_in,
    last_in,
    sums_ref,
    out_ref,
    cells,
    wide,
    first,
    middle,
    last,
    patch,
    wide_out,
    sems,
):
    del sums_ref
    middle_copy = fetch(middle_in, middle, sems.at[2])
    edges = [fetch(ref, cells.at[i], sems.at[i]) for i, ref in enumerate((prev_in, next_in))]
    copies = [
        fetch(wide_in, wide, sems.at[3]),
        fetch(first_in, first, sems.at[4]),
        fetch(last_in, last, sems.at[5]),
    ]
    column = lanes((2 * X, 2 * X))
    source = lax.broadcasted_iota(jnp.int32, (2 * X, 2 * X), 0)
    weave = jnp.where(source == (column % 2) * X + column // 2, 1.0, 0.0).astype(BF16)

    def place(result, depth):
        for py in range(2):
            even = result[py * 64 : py * 64 + G, :]
            odd = result[py * 64 + G : py * 64 + 2 * G, :]
            both = jnp.concatenate(
                [
                    jnp.concatenate([even[:, y * X : (y + 1) * X], odd[:, y * X : (y + 1) * X]], axis=1)
                    for y in range(Y)
                ],
                axis=0,
            )
            woven = dot(both, weave)
            for y in range(Y):
                rows = pl.ds(depth * 16 + 2 * y + py, G, stride=64)
                wide_out[0, rows, :] = woven[y * G : (y + 1) * G, 0:X]
                wide_out[1, rows, :] = woven[y * G : (y + 1) * G, X : 2 * X]

    middle_copy.wait()
    place(middle[0:128, :], 1)
    place(middle[128:256, :], 2)
    lane = lanes((C, X))
    for side in range(2):
        edges[side].wait()
        clear_rims(side, patch)
        for y in range(Y):
            spread_cells(cells[side, :, y * X : (y + 1) * X].astype(F32), side, y, lane, patch)
    for copy in copies:
        copy.wait()
    place((first[...] + dot(wide[128:256, 0:576], patch[0:576, :])).astype(BF16), 0)
    place((last[...] + dot(wide[0:128, 576:1152], patch[576:1152, :])).astype(BF16), 3)
    out_ref[:, 0:X] = wide_out[0].astype(BF16)
    out_ref[:, X : 2 * X] = wide_out[1].astype(BF16)


def call(body, name, args, outs, scratch, flops, mebibytes, smem=(), far=(), far_outs=()):
    moved = sum(a.size * a.dtype.itemsize for a in args) + sum(o.size * o.dtype.itemsize for o in outs)
    spaces = [
        pltpu.SMEM if i in smem else pl.ANY if i in far else pltpu.VMEM for i in range(len(args))
    ]
    out_spaces = [pltpu.HBM if i in far_outs else pltpu.VMEM for i in range(len(outs))]
    outs = [pltpu.HBM(o.shape, o.dtype) if i in far_outs else o for i, o in enumerate(outs)]
    args = [
        pltpu.with_memory_space_constraint(a, pltpu.HBM) if i in far else a for i, a in enumerate(args)
    ]
    return pl.pallas_call(
        body,
        name=name,
        out_shape=outs,
        in_specs=[pl.BlockSpec(memory_space=space) for space in spaces],
        out_specs=[pl.BlockSpec(memory_space=space) for space in out_spaces],
        scratch_shapes=scratch,
        compiler_params=pltpu.CompilerParams(vmem_limit_bytes=mebibytes * 1024 * 1024),
        cost_estimate=pl.CostEstimate(flops=flops, bytes_accessed=moved, transcendentals=0),
    )(*args)


def exchange(low, high):
    ends = lax.axis_size("slab") - 1
    before = lax.ppermute(high, "slab", [(i, i + 1) for i in range(ends)])
    after = lax.ppermute(low, "slab", [(i + 1, i) for i in range(ends)])
    return before, after


def local(latent, g_weight, bn_gain, bn_shift, real_crops, d_weight, cot_fake, cot_real):
    shape = jax.ShapeDtypeStruct
    taps_g = g_weight.transpose(0, 1, 2, 4, 3).reshape(64 * G, C)
    taps_d = d_weight.reshape(64 * G, C)
    lat = latent[0]
    real = real_crops[0]
    low, high = call(
        edge_kernel,
        "edges",
        (lat, real),
        [shape((1536, X), BF16)] * 2,
        [
            pltpu.VMEM((2, C, Y, X), BF16),
            pltpu.VMEM((2, G, 2 * Y, 2 * X), BF16),
            pltpu.SemaphoreType.DMA((4,)),
        ],
        0,
        8,
        far=(0, 1),
    )
    prev, next_ = exchange(low, high)
    wide, first, middle, last, weight = call(
        own_kernel,
        "own_cells",
        (lat.reshape(C * 2 * Y, X), taps_g, taps_d),
        [shape((256, 1152), BF16)] + [shape((256, CELLS), F32)] * 3 + [shape((C, 2048), BF16)],
        [
            pltpu.VMEM((1024, X), BF16),
            pltpu.VMEM((2048, C), BF16),
            pltpu.VMEM((2048, C), BF16),
            pltpu.VMEM((C, 2048), BF16),
            pltpu.SemaphoreType.DMA((4,)),
            pltpu.VMEM((1152, CELLS), BF16),
            pltpu.VMEM((1024, X), F32),
        ],
        4 * 256 * 1152 * CELLS,
        16,
        far=(0, 1, 2),
        far_outs=(4,),
    )
    real_patch, real_pre = call(
        real_own_kernel,
        "real_own",
        (real.reshape(G * 64, 2 * X), weight),
        [shape((2048, CELLS), BF16), shape((2 * C, CELLS), F32)],
        [
            pltpu.VMEM((2048, 2 * X), BF16),
            pltpu.VMEM((C, 2048), BF16),
            pltpu.VMEM((2048, CELLS), BF16),
            pltpu.VMEM((2 * C, CELLS), F32),
            pltpu.SemaphoreType.DMA((10,)),
            pltpu.VMEM((2, 2048, X), F32),
            pltpu.VMEM((2048, 2 * X), BF16),
        ],
        4 * 2048 * C * CELLS,
        20,
        far=(0, 1),
        far_outs=(0, 1),
    )
    first, middle, last, stats, real_prev, real_next = call(
        rim_kernel,
        "rim_cells",
        (prev, next_, wide, first, middle, last, real_pre),
        [shape((256, CELLS), F32)] * 3 + [shape((NDEV, 128), F32)] + [shape((1024, X), BF16)] * 2,
        [
            pltpu.VMEM((1152, CELLS), BF16),
            pltpu.VMEM((1024, X), F32),
            pltpu.VMEM((256, CELLS), F32),
            pltpu.VMEM((256, CELLS), F32),
            pltpu.SemaphoreType.DMA((5,)),
        ],
        2 * 256 * 1152 * CELLS,
        20,
        far=(6,),
        far_outs=(0, 1, 2, 4, 5),
    )
    stats = lax.all_to_all(stats, AXES, 0, 0, tiled=True)
    working = [
        pltpu.VMEM((C * 2 * Y, X), F32),
        pltpu.VMEM((C * 2 * Y, X), F32),
        pltpu.VMEM((4 * C, CELLS), BF16),
    ]
    d_real, real_terms = call(
        real_kernel,
        "real_branch",
        (real_prev, real_next, real_patch, real_pre, weight, cot_real.reshape(C * 2 * Y, X)),
        [shape((C * 2 * Y, X), BF16), shape((1024, 2 * C), F32)],
        [
            pltpu.VMEM((1024, 2 * C), F32),
            pltpu.SemaphoreType.DMA((6,)),
            pltpu.VMEM((2, 1024, X), BF16),
            pltpu.VMEM((2048, CELLS), BF16),
            pltpu.VMEM((2 * C, CELLS), F32),
            pltpu.VMEM((C, 2048), BF16),
            pltpu.VMEM((1024, CELLS), BF16),
            pltpu.VMEM((2, 1024, X), F32),
            pltpu.VMEM((1024, 2 * X), BF16),
        ]
        + working,
        8 * 2048 * C * CELLS,
        24,
        far=(0, 1, 2, 3, 4),
        far_outs=(1,),
    )
    at = lax.axis_index("slab")
    inside = jnp.stack([at > 0, at < lax.axis_size("slab") - 1]).astype(jnp.int32)
    d_fake, low, high, terms = call(
        fake_kernel,
        "fake_branch",
        (
            inside,
            first,
            middle,
            last,
            stats,
            bn_gain.reshape(1, G),
            bn_shift.reshape(1, G),
            weight,
            cot_fake.reshape(C * 2 * Y, X),
            real_terms,
        ),
        [
            shape((C * 2 * Y, X), BF16),
            shape((C, CELLS), BF16),
            shape((C, CELLS), BF16),
            shape((NDEV * 8, 128), F32),
        ],
        [
            pltpu.VMEM((6, 128, CELLS), F32),
            pltpu.VMEM((NDEV * 8, 128), F32),
            pltpu.VMEM((C, 2048), BF16),
            pltpu.SemaphoreType.DMA((10,)),
            pltpu.VMEM((6 * 512, CELLS), BF16),
        ]
        + working,
        8 * 2048 * C * CELLS * 2,
        28,
        smem=(0,),
        far=(1, 2, 3, 7, 9),
        far_outs=(1, 2),
    )
    parts = lax.all_to_all(terms.reshape(NDEV, 8, 128), AXES, 0, 0, tiled=True)
    grad_prev, grad_next = exchange(low, high)
    pull_wide, pull_first, pull_middle, pull_last = call(
        pull_own_kernel,
        "pull_own",
        (low, high, taps_d),
        [
            shape((256, 1152), BF16),
            shape((128, CELLS), F32),
            shape((256, CELLS), BF16),
            shape((128, CELLS), F32),
        ],
        [
            pltpu.VMEM((2, C, CELLS), BF16),
            pltpu.VMEM((2048, C), BF16),
            pltpu.VMEM((256, 1152), BF16),
            pltpu.VMEM((128, CELLS), F32),
            pltpu.VMEM((256, CELLS), BF16),
            pltpu.VMEM((128, CELLS), F32),
            pltpu.VMEM((1152, CELLS), BF16),
            pltpu.SemaphoreType.DMA((7,)),
        ],
        2 * 384 * 1152 * CELLS,
        16,
        far=(0, 1, 2),
        far_outs=(0, 1, 2, 3),
    )
    (sums,) = call(
        sum_kernel,
        "sum_terms",
        (parts.reshape(NDEV * 8, 128), grad_prev, grad_next, pull_middle),
        [shape((NDEV * 8, 128), BF16)],
        [],
        NDEV * 1024,
        8,
        far=(1, 2, 3),
    )
    whole = lax.all_to_all(sums.reshape(NDEV, 8, 128), AXES, 0, 0, tiled=True)
    (fake_grad,) = call(
        pullback_kernel,
        "pullback",
        (grad_prev, grad_next, pull_wide, pull_first, pull_middle, pull_last, sums),
        [shape((G * 64, 2 * X), BF16)],
        [
            pltpu.VMEM((2, C, CELLS), BF16),
            pltpu.VMEM((256, 1152), BF16),
            pltpu.VMEM((128, CELLS), F32),
            pltpu.VMEM((256, CELLS), BF16),
            pltpu.VMEM((128, CELLS), F32),
            pltpu.VMEM((1152, CELLS), BF16),
            pltpu.VMEM((2, G * 64, X), F32),
            pltpu.SemaphoreType.DMA((6,)),
        ],
        2 * 128 * 1152 * CELLS,
        16,
        far=(0, 1, 2, 3, 4, 5, 6),
    )
    (weight_grad,) = call(
        unpack_kernel,
        "unpack",
        (whole.reshape(NDEV * 8, 128),),
        [shape((2048, C), F32)],
        [],
        0,
        8,
    )
    return (
        d_fake.reshape(1, C, 2, Y, X),
        d_real.reshape(1, C, 2, Y, X),
        fake_grad.reshape(1, G, 4, 2 * Y, 2 * X),
        weight_grad.reshape(4, 4, 4, G, C),
    )


def solution(mesh):
    split = P(("section", "rep"), None, "slab", None, None)
    in_specs = (split, P(), P(), P(), split, P(), split, split)
    out_specs = (split, split, split, P())
    return jax.shard_map(local, mesh=mesh, in_specs=in_specs, out_specs=out_specs, check_vma=False)
```

```python
import jax
import jax.numpy as jnp
from jax import lax
from jax.experimental import pallas as pl
from jax.experimental.pallas import tpu as pltpu
from jax.sharding import PartitionSpec as P

AXES = ("section", "slab", "rep")
NDEV = 128
C = 64
G = 32
Y = 8
X = 128
CELLS = Y * X
F32 = jnp.float32
BF16 = jnp.bfloat16

phase_taps = (((1, 0), (3, -1)), ((0, 1), (2, 0)))


def dot(a, b, dims=(1, 0)):
    return lax.dot_general(a, b, (((dims[0],), (dims[1],)), ((), ())), preferred_element_type=F32)


def lanes(shape):
    return lax.broadcasted_iota(jnp.int32, shape, len(shape) - 1)


def from_left(tile, lane):
    return jnp.where(lane == 0, 0.0, pltpu.roll(tile, 1, 1))


def from_right(tile, lane):
    return jnp.where(lane == X - 1, 0.0, pltpu.roll(tile, X - 1, 1))


def spread_weights(taps_ref, wide_ref):
    wide_ref[...] = jnp.zeros_like(wide_ref)
    for pz in range(2):
        for py in range(2):
            for px in range(2):
                row = ((1 - pz) * 4 + py * 2 + px) * G
                for kz, oz in phase_taps[pz]:
                    tz = oz if pz == 1 else oz + 1
                    for ky, oy in phase_taps[py]:
                        for kx, ox in phase_taps[px]:
                            col = tz * 576 + (oy + 1) * 192 + (ox + 1) * 64
                            tap = (kz * 16 + ky * 4 + kx) * G
                            wide_ref[row : row + G, col : col + C] = taps_ref[tap : tap + G, :]


def spread_cells(tile, depth, y, lane, patch_ref):
    for xi, moved in ((0, from_left(tile, lane)), (1, tile), (2, from_right(tile, lane))):
        piece = moved.astype(BF16)
        for yi in range(3):
            to = y - (yi - 1)
            if 0 <= to < Y:
                row = depth * 576 + yi * 192 + xi * 64
                patch_ref[row : row + C, to * X : (to + 1) * X] = piece


def clear_rims(depth, patch_ref):
    edge = jnp.zeros((192, X), BF16)
    patch_ref[depth * 576 : depth * 576 + 192, 0:X] = edge
    patch_ref[depth * 576 + 384 : depth * 576 + 576, CELLS - X : CELLS] = edge


def fetch(source, target, sem):
    copy = pltpu.make_async_copy(source, target, sem)
    copy.start()
    return copy


def as_row(column, shift):
    sub = lax.broadcasted_iota(jnp.int32, (G, 128), 0)
    return jnp.sum(jnp.where(lanes((G, 128)) == sub + shift, column, 0.0), axis=0, keepdims=True)


def as_column(row, shift):
    shape = (G, row.shape[1])
    sub = lax.broadcasted_iota(jnp.int32, shape, 0)
    return jnp.sum(jnp.where(lanes(shape) == sub + shift, row, 0.0), axis=1, keepdims=True)


def edge_kernel(lat_in, real_in, edge_ref, lat_edge, real_edge, sems):
    copies = [
        fetch(lat_in.at[:, 0], lat_edge, sems.at[0]),
        fetch(real_in.at[:, 0], real_edge, sems.at[1]),
    ]
    join_edge(copies, lat_edge, real_edge, edge_ref)


def join_edge(copies, lat_edge, real_edge, edge_ref):
    copies[0].wait()
    edge_ref[0:512, :] = lat_edge[...].reshape(512, X)
    copies[1].wait()
    edge = real_edge[...].reshape(512, 2 * X)
    edge_ref[512:1024, :] = edge[:, 0:X]
    edge_ref[1024:1536, :] = edge[:, X : 2 * X]


def cell_stats(ref, first, count):
    blocks = range(first, first + count)
    total = jnp.zeros((G, CELLS), F32)
    for block in blocks:
        total += ref[block * G : (block + 1) * G, :]
    mean = jnp.sum(total, axis=1, keepdims=True) * (1.0 / (count * CELLS))
    squares = jnp.zeros((G, CELLS), F32)
    for block in blocks:
        off = ref[block * G : (block + 1) * G, :] - mean
        squares += off * off
    return mean, jnp.sum(squares, axis=1, keepdims=True)


def own_kernel(
    lat_in,
    real_in,
    taps_in,
    taps_d_in,
    wide_out,
    first_out,
    middle_out,
    last_out,
    sums_ref,
    edge_ref,
    weight_out,
    lat_edge,
    real_edge,
    lat,
    taps,
    taps_d,
    weight,
    wide,
    first,
    middle,
    last,
    sems,
    patch,
    wide_lat,
):
    edge_copies = [
        fetch(lat_in.at[:, 1], lat_edge, sems.at[0]),
        fetch(real_in.at[:, 3], real_edge, sems.at[1]),
    ]
    lat_copy = fetch(lat_in, lat, sems.at[2])
    taps_copy = fetch(taps_in, taps, sems.at[3])
    taps_d_copy = fetch(taps_d_in, taps_d, sems.at[4])
    lat_copy.wait()
    wide_lat[...] = lat[...].reshape(1024, X).astype(F32)
    lane = lanes((C, X))
    for depth in range(2):
        clear_rims(depth, patch)
        for y in range(Y):
            spread_cells(wide_lat[pl.ds(depth * Y + y, C, stride=16), :], depth, y, lane, patch)
    taps_copy.wait()
    spread_weights(taps, wide)
    copies = [fetch(wide, wide_out, sems.at[5])]
    last[...] = dot(wide[:, 0:576], patch[576:1152, :])
    copies.append(fetch(last, last_out, sems.at[6]))
    middle[...] = dot(wide[...], patch[...])
    copies.append(fetch(middle, middle_out, sems.at[7]))
    first[...] = dot(wide[:, 576:1152], patch[0:576, :])
    copies.append(fetch(first, first_out, sems.at[8]))
    taps_d_copy.wait()
    same = lax.broadcasted_iota(jnp.int32, (C, C), 0) == lanes((C, C))
    unit = jnp.where(same, 1.0, 0.0).astype(BF16)
    weight[...] = dot(unit, taps_d[...], (1, 1)).astype(BF16)
    copies.append(fetch(weight, weight_out, sems.at[9]))
    join_edge(edge_copies, lat_edge, real_edge, edge_ref)
    place = lanes((G, 128))
    sums = jnp.zeros((G, 128), F32)
    for at, column in enumerate(cell_stats(middle, 0, 8) + cell_stats(first, 4, 4)):
        sums = jnp.where(place == at, column, sums)
    sums_ref[...] = sums
    for copy in copies:
        copy.wait()


def rim_kernel(
    inside_ref,
    next_ref,
    sums_ref,
    wide_in,
    last_in,
    last_out,
    stats_out,
    real_next_out,
    patch,
    wide_lat,
    wide,
    last,
    stats,
    sems,
):
    wide_copy = fetch(wide_in, wide, sems.at[0])
    last_copy = fetch(last_in, last, sems.at[1])
    copies = [fetch(next_ref.at[512:1536], real_next_out, sems.at[2])]
    wide_lat[...] = next_ref[0:512, :].astype(F32)
    lane = lanes((C, X))
    clear_rims(0, patch)
    for y in range(Y):
        spread_cells(wide_lat[pl.ds(y, C, stride=8), :], 0, y, lane, patch)
    wide_copy.wait()
    last_copy.wait()
    last[...] += dot(wide[:, 576:1152], patch[...])
    copies.append(fetch(last, last_out, sems.at[3]))
    groups = [(2.0, sums_ref[:, 0:1], sums_ref[:, 1:2])]
    groups.append((jnp.where(inside_ref[0] > 0, 0.0, 1.0), sums_ref[:, 2:3], sums_ref[:, 3:4]))
    groups.append((1.0,) + cell_stats(last, 0, 4))
    groups.append((jnp.where(inside_ref[1] > 0, 1.0, 0.0),) + cell_stats(last, 4, 4))
    depths = jnp.zeros((G, 1), F32)
    mean = jnp.zeros((G, 1), F32)
    for weight, one, _ in groups:
        depths += weight
        mean += weight * one
    mean /= depths
    spread = jnp.zeros((G, 1), F32)
    for weight, one, squares in groups:
        own = squares if isinstance(weight, float) else weight * squares
        spread += own + weight * (4.0 * CELLS) * (one - mean) * (one - mean)
    stats[...] = jnp.broadcast_to(as_row(mean, 0) + as_row(spread, G), (NDEV, 128))
    copies.append(fetch(stats, stats_out, sems.at[4]))
    for copy in copies:
        copy.wait()


def activate(before):
    squashed = jax.nn.sigmoid(4.0 * before)
    output = before * (0.2 + 0.8 * squashed)
    derivative = 0.2 + 0.8 * squashed + 3.2 * before * squashed * (1.0 - squashed)
    return (output, derivative)


def convolve(weight_ref, patch):
    early = weight_ref[:, 0:1024]
    late = weight_ref[:, 1024:2048]
    shared = dot(jnp.concatenate([late, early], axis=0), patch[1024:2048, :])
    return (
        dot(early, patch[0:1024, :]) + shared[0:C, :],
        shared[C : 2 * C, :] + dot(late, patch[2048:3072, :]),
    )


def finish(pre, cot_ref, out_ref, wide_cot, wide_out, grad):
    wide_cot[...] = cot_ref[...].astype(F32)
    nothing = jnp.zeros((C, CELLS), BF16)
    grad[0:C, :] = nothing
    grad[3 * C : 4 * C, :] = nothing
    for m in range(2):
        for y in range(Y):
            output, slope = activate(pre[m][:, y * X : (y + 1) * X])
            wide_out[pl.ds(m * Y + y, C, stride=16), :] = output
            cot = wide_cot[pl.ds(m * Y + y, C, stride=16), :]
            grad[(2 - m) * C : (3 - m) * C, y * X : (y + 1) * X] = (cot * slope).astype(BF16)
    out_ref[...] = wide_out[...].astype(BF16)


def kernel_terms(planes, grad):
    halves = []
    for half in range(2):
        terms = dot(planes[half], grad[128:256, :], (1, 1))
        terms += dot(planes[half + 2], grad[64:192, :], (1, 1))
        halves.append(terms + dot(planes[half + 4], grad[0:128, :], (1, 1)))
    return halves


def split_depth(at, places, halves, rows, patch):
    base, stride = places
    column = lanes((2 * X, 4 * X))
    source = lax.broadcasted_iota(jnp.int32, (2 * X, 4 * X), 0)
    pick = jnp.where(source == 2 * (column % X) + column // X - 1, 1.0, 0.0).astype(BF16)
    edge = jnp.zeros((128, X), BF16)
    patch[at : at + 128, 0:X] = edge
    patch[at + 384 : at + 512, CELLS - X : CELLS] = edge
    for row in range(2 * Y):
        for half in range(2):
            cells = halves[half, pl.ds(base + row, G, stride=stride), :].astype(BF16)
            rows[at + row * G : at + (row + 1) * G, half * X : (half + 1) * X] = cells
    split = dot(rows[at : at + 512, :], pick).astype(BF16)
    for row in range(2 * Y):
        for kx in range(4):
            piece = split[row * G : (row + 1) * G, kx * X : (kx + 1) * X]
            for ky in range(4):
                if (row + 1 - ky) % 2 == 0 and 0 <= (row + 1 - ky) // 2 < Y:
                    y = (row + 1 - ky) // 2
                    place = at + ky * 128 + kx * G
                    patch[place : place + G, y * X : (y + 1) * X] = piece


def real_kernel(
    real_ref,
    prev_ref,
    next_in,
    weight_in,
    cot_ref,
    wide_in,
    first_in,
    out_ref,
    terms_out,
    first_out,
    edge,
    weight,
    wide,
    first,
    terms_ref,
    sems,
    patch,
    lat_patch,
    halves,
    rows,
    wide_cot,
    wide_out,
    grad,
):
    copies = [
        fetch(wide_in, wide, sems.at[0]),
        fetch(first_in, first, sems.at[1]),
        fetch(next_in, edge, sems.at[2]),
        fetch(weight_in, weight, sems.at[3]),
    ]
    halves[0, 0:512, :] = prev_ref[0:512, :].astype(F32)
    lane = lanes((C, X))
    clear_rims(0, lat_patch)
    for y in range(Y):
        spread_cells(halves[0, pl.ds(y, C, stride=8), :], 0, y, lane, lat_patch)
    copies[0].wait()
    copies[1].wait()
    first[...] += dot(wide[:, 0:576], lat_patch[...])
    first_copy = fetch(first, first_out, sems.at[4])
    copies[2].wait()
    for half in range(2):
        part = slice(512 + half * 512, 1024 + half * 512)
        halves[half, 0:2048, :] = real_ref[:, half * X : (half + 1) * X].astype(F32)
        halves[half, 2048:2560, :] = prev_ref[part, :].astype(F32)
        halves[half, 2560:3072, :] = edge[half * 512 : (half + 1) * 512, :].astype(F32)
    places = ((2048, 16), (0, 64), (16, 64), (32, 64), (48, 64), (2560, 16))
    for depth in range(6):
        split_depth(depth * 512, places[depth], halves, rows, patch)
    copies[3].wait()
    finish(convolve(weight, patch), cot_ref, out_ref, wide_cot, wide_out, grad)
    planes = [patch[depth * 512 : (depth + 1) * 512, :] for depth in range(6)]
    for half, terms in enumerate(kernel_terms(planes, grad)):
        terms_ref[half * 512 : (half + 1) * 512, :] = terms
    fetch(terms_ref, terms_out, sems.at[5]).wait()
    first_copy.wait()


def fake_kernel(
    inside_ref,
    first_in,
    middle_in,
    last_in,
    stats_ref,
    gain_ref,
    shift_ref,
    weight_in,
    cot_ref,
    real_terms_in,
    out_ref,
    low_out,
    high_out,
    terms_ref,
    before,
    real_terms,
    weight_ref,
    sems,
    patch,
    wide_cot,
    wide_out,
    grad,
):
    befores = []
    for depth in range(6):
        ref = (first_in, middle_in, last_in)[depth // 2]
        half = pl.ds(depth % 2 * 128, 128)
        befores.append(fetch(ref.at[half], before.at[depth], sems.at[depth]))
    weight_copy = fetch(weight_in, weight_ref, sems.at[6])
    real_copy = fetch(real_terms_in, real_terms, sems.at[7])
    stats = stats_ref[...]
    slab = lax.broadcasted_iota(jnp.int32, (NDEV, 128), 0) // 2 % 32
    depths = jnp.where(slab == 0, 5.0, jnp.where(slab == 31, 3.0, 4.0))
    mean_row = jnp.sum(stats * depths, axis=0, keepdims=True) * (1.0 / (4.0 * NDEV))
    off = stats - mean_row
    between = as_column(jnp.sum(off * off * depths, axis=0, keepdims=True), 0)
    center = as_column(mean_row, 0)
    within = as_column(jnp.sum(stats, axis=0, keepdims=True), G)
    variance = (within + 4.0 * CELLS * between) * (1.0 / (16.0 * CELLS * NDEV))
    factor = as_column(gain_ref[...], 0) * lax.rsqrt(variance + 1e-05)
    shift = as_column(shift_ref[...], 0)
    lane = lanes((G, X))
    edge = jnp.zeros((128, X), BF16)
    for depth in range(6):
        befores[depth].wait()
        patch[depth * 512 : depth * 512 + 128, 0:X] = edge
        patch[depth * 512 + 384 : depth * 512 + 512, CELLS - X : CELLS] = edge
        for py in range(2):
            for px in range(2):
                block = (py * 2 + px) * G
                for y in range(Y):
                    cells = before[depth, block : block + G, y * X : (y + 1) * X]
                    fake = jnp.maximum((cells - center) * factor + shift, 0.0)
                    if depth == 0:
                        fake = jnp.where(inside_ref[0] > 0, fake, 0.0)
                    if depth == 5:
                        fake = jnp.where(inside_ref[1] > 0, fake, 0.0)
                    if px == 1:
                        pieces = ((2, fake), (0, from_left(fake, lane)))
                    else:
                        pieces = ((1, fake), (3, from_right(fake, lane)))
                    for kx, piece in pieces:
                        piece = piece.astype(BF16)
                        for ky, to in ((2, y), (0, y + 1)) if py == 1 else ((1, y), (3, y - 1)):
                            if 0 <= to < Y:
                                at = depth * 512 + ky * 128 + kx * G
                                patch[at : at + G, to * X : (to + 1) * X] = piece
    weight_copy.wait()
    pre = convolve(weight_ref, patch)
    finish(pre, cot_ref, out_ref, wide_cot, wide_out, grad)
    edge_copies = [
        fetch(grad.at[2 * C : 3 * C], low_out, sems.at[8]),
        fetch(grad.at[C : 2 * C], high_out, sems.at[9]),
    ]
    planes = [patch[depth * 512 : (depth + 1) * 512, :] for depth in range(6)]
    real_copy.wait()
    for half, terms in enumerate(kernel_terms(planes, grad)):
        rows = slice(half * 512, (half + 1) * 512)
        terms_ref[rows, :] = terms + real_terms[rows, :]
    for copy in edge_copies:
        copy.wait()


def sum_kernel(parts_ref, prev_ref, middle_ref, sums_ref):
    del prev_ref, middle_ref
    total = jnp.sum(parts_ref[...].reshape(NDEV, 8, 128), axis=0, keepdims=True)
    sums_ref[...] = jnp.broadcast_to(total, (NDEV, 8, 128)).reshape(NDEV * 8, 128).astype(BF16)


def unpack_kernel(sums_ref, out_ref):
    sums = sums_ref[...].astype(F32)
    out_ref[0:1024, :] = sums[:, 0:C]
    out_ref[1024:2048, :] = sums[:, C : 2 * C]


def pull_own_kernel(
    low_in,
    high_in,
    taps_in,
    wide_out,
    first_out,
    middle_out,
    last_out,
    cells,
    taps,
    wide,
    first,
    middle,
    last,
    patch,
    sems,
):
    edges = [fetch(ref, cells.at[i], sems.at[i]) for i, ref in enumerate((low_in, high_in))]
    taps_copy = fetch(taps_in, taps, sems.at[2])
    lane = lanes((C, X))
    for depth in range(2):
        edges[depth].wait()
        clear_rims(depth, patch)
        for y in range(Y):
            spread_cells(cells[depth, :, y * X : (y + 1) * X].astype(F32), depth, y, lane, patch)
    taps_copy.wait()
    spread_weights(taps, wide)
    copies = [fetch(wide, wide_out, sems.at[3])]
    first[...] = dot(wide[128:256, 576:1152], patch[0:576, :])
    copies.append(fetch(first, first_out, sems.at[4]))
    middle[...] = dot(wide[...], patch[...]).astype(BF16)
    copies.append(fetch(middle, middle_out, sems.at[5]))
    last[...] = dot(wide[0:128, 0:576], patch[576:1152, :])
    copies.append(fetch(last, last_out, sems.at[6]))
    for copy in copies:
        copy.wait()


def weave_into(result, depth, wide_out):
    column = lanes((2 * X, 2 * X))
    source = lax.broadcasted_iota(jnp.int32, (2 * X, 2 * X), 0)
    weave = jnp.where(source == (column % 2) * X + column // 2, 1.0, 0.0).astype(BF16)
    for py in range(2):
        even = result[py * 64 : py * 64 + G, :]
        odd = result[py * 64 + G : py * 64 + 2 * G, :]
        both = jnp.concatenate(
            [
                jnp.concatenate([even[:, y * X : (y + 1) * X], odd[:, y * X : (y + 1) * X]], axis=1)
                for y in range(Y)
            ],
            axis=0,
        )
        woven = dot(both, weave)
        for y in range(Y):
            rows = pl.ds(depth * 16 + 2 * y + py, G, stride=64)
            wide_out[0, rows, :] = woven[y * G : (y + 1) * G, 0:X]
            wide_out[1, rows, :] = woven[y * G : (y + 1) * G, X : 2 * X]


def spread_edge(cells, patch):
    lane = lanes((C, X))
    clear_rims(0, patch)
    for y in range(Y):
        spread_cells(cells[:, y * X : (y + 1) * X].astype(F32), 0, y, lane, patch)


def pull_prev_kernel(
    prev_in, wide_in, first_in, middle_in, sums_ref, rows_ref, cells, wide, first, middle, patch, sems
):
    del sums_ref
    copies = [
        fetch(middle_in, middle, sems.at[0]),
        fetch(prev_in, cells, sems.at[1]),
        fetch(wide_in, wide, sems.at[2]),
        fetch(first_in, first, sems.at[3]),
    ]
    rows_ref[...] = jnp.zeros_like(rows_ref)
    copies[0].wait()
    weave_into(middle[0:128, :], 1, rows_ref)
    weave_into(middle[128:256, :], 2, rows_ref)
    copies[1].wait()
    spread_edge(cells, patch)
    copies[2].wait()
    copies[3].wait()
    weave_into((first[...] + dot(wide[128:256, 0:576], patch[...])).astype(BF16), 0, rows_ref)


def pull_next_kernel(next_ref, wide_in, last_in, rows_ref, out_ref, wide, last, patch, wide_out, sems):
    copies = [fetch(wide_in, wide, sems.at[0]), fetch(last_in, last, sems.at[1])]
    spread_edge(next_ref, patch)
    wide_out[...] = rows_ref[...]
    copies[0].wait()
    copies[1].wait()
    weave_into((last[...] + dot(wide[0:128, 576:1152], patch[...])).astype(BF16), 3, wide_out)
    out_ref[:, 0:X] = wide_out[0].astype(BF16)
    out_ref[:, X : 2 * X] = wide_out[1].astype(BF16)


def call(body, name, args, outs, scratch, flops, mebibytes, smem=(), far=(), far_outs=()):
    moved = sum(a.size * a.dtype.itemsize for a in args) + sum(o.size * o.dtype.itemsize for o in outs)
    spaces = [
        pltpu.SMEM if i in smem else pl.ANY if i in far else pltpu.VMEM for i in range(len(args))
    ]
    out_spaces = [pltpu.HBM if i in far_outs else pltpu.VMEM for i in range(len(outs))]
    outs = [pltpu.HBM(o.shape, o.dtype) if i in far_outs else o for i, o in enumerate(outs)]
    args = [
        pltpu.with_memory_space_constraint(a, pltpu.HBM) if i in far else a for i, a in enumerate(args)
    ]
    return pl.pallas_call(
        body,
        name=name,
        out_shape=outs,
        in_specs=[pl.BlockSpec(memory_space=space) for space in spaces],
        out_specs=[pl.BlockSpec(memory_space=space) for space in out_spaces],
        scratch_shapes=scratch,
        compiler_params=pltpu.CompilerParams(vmem_limit_bytes=mebibytes * 1024 * 1024),
        cost_estimate=pl.CostEstimate(flops=flops, bytes_accessed=moved, transcendentals=0),
    )(*args)


def to_next(edge):
    ends = lax.axis_size("slab") - 1
    return lax.ppermute(edge, "slab", [(i, i + 1) for i in range(ends)])


def to_prev(edge):
    ends = lax.axis_size("slab") - 1
    return lax.ppermute(edge, "slab", [(i + 1, i) for i in range(ends)])


def local(latent, g_weight, bn_gain, bn_shift, real_crops, d_weight, cot_fake, cot_real):
    shape = jax.ShapeDtypeStruct
    taps_g = g_weight.transpose(0, 1, 2, 4, 3).reshape(64 * G, C)
    taps_d = d_weight.reshape(64 * G, C)
    lat = latent[0]
    real = real_crops[0]
    at = lax.axis_index("slab")
    inside = jnp.stack([at > 0, at < lax.axis_size("slab") - 1]).astype(jnp.int32)
    (low,) = call(
        edge_kernel,
        "edges",
        (lat, real),
        [shape((1536, X), BF16)],
        [
            pltpu.VMEM((C, Y, X), BF16),
            pltpu.VMEM((G, 2 * Y, 2 * X), BF16),
            pltpu.SemaphoreType.DMA((2,)),
        ],
        0,
        4,
        far=(0, 1),
    )
    next_ = to_prev(low)
    wide, first, middle, last, sums, high, weight = call(
        own_kernel,
        "own_cells",
        (lat, real, taps_g, taps_d),
        [shape((256, 1152), BF16)]
        + [shape((256, CELLS), F32)] * 3
        + [shape((G, 128), F32), shape((1536, X), BF16), shape((C, 2048), BF16)],
        [
            pltpu.VMEM((C, Y, X), BF16),
            pltpu.VMEM((G, 2 * Y, 2 * X), BF16),
            pltpu.VMEM((C, 2, Y, X), BF16),
            pltpu.VMEM((2048, C), BF16),
            pltpu.VMEM((2048, C), BF16),
            pltpu.VMEM((C, 2048), BF16),
            pltpu.VMEM((256, 1152), BF16),
            pltpu.VMEM((256, CELLS), F32),
            pltpu.VMEM((256, CELLS), F32),
            pltpu.VMEM((256, CELLS), F32),
            pltpu.SemaphoreType.DMA((10,)),
            pltpu.VMEM((1152, CELLS), BF16),
            pltpu.VMEM((1024, X), F32),
        ],
        4 * 256 * 1152 * CELLS,
        16,
        far=(0, 1, 2, 3),
        far_outs=(0, 1, 2, 3, 6),
    )
    prev = to_next(high)
    last, stats, real_next = call(
        rim_kernel,
        "rim_cells",
        (inside, next_, sums, wide, last),
        [shape((256, CELLS), F32), shape((NDEV, 128), F32), shape((1024, X), BF16)],
        [
            pltpu.VMEM((576, CELLS), BF16),
            pltpu.VMEM((512, X), F32),
            pltpu.VMEM((256, 1152), BF16),
            pltpu.VMEM((256, CELLS), F32),
            pltpu.VMEM((NDEV, 128), F32),
            pltpu.SemaphoreType.DMA((5,)),
        ],
        256 * 1152 * CELLS,
        12,
        smem=(0,),
        far=(3, 4),
        far_outs=(0, 1, 2),
    )
    stats = lax.all_to_all(stats, AXES, 0, 0, tiled=True)
    working = [
        pltpu.VMEM((C * 2 * Y, X), F32),
        pltpu.VMEM((C * 2 * Y, X), F32),
        pltpu.VMEM((4 * C, CELLS), BF16),
    ]
    d_real, real_terms, first = call(
        real_kernel,
        "real_branch",
        (
            real.reshape(G * 64, 2 * X),
            prev,
            real_next,
            weight,
            cot_real.reshape(C * 2 * Y, X),
            wide,
            first,
        ),
        [shape((C * 2 * Y, X), BF16), shape((1024, 2 * C), F32), shape((256, CELLS), F32)],
        [
            pltpu.VMEM((1024, X), BF16),
            pltpu.VMEM((C, 2048), BF16),
            pltpu.VMEM((256, 1152), BF16),
            pltpu.VMEM((256, CELLS), F32),
            pltpu.VMEM((1024, 2 * C), F32),
            pltpu.SemaphoreType.DMA((6,)),
            pltpu.VMEM((6 * 512, CELLS), BF16),
            pltpu.VMEM((576, CELLS), BF16),
            pltpu.VMEM((2, 3072, X), F32),
            pltpu.VMEM((3072, 2 * X), BF16),
        ]
        + working,
        16 * 2048 * C * CELLS,
        26,
        far=(2, 3, 5, 6),
        far_outs=(1, 2),
    )
    d_fake, low, high, terms = call(
        fake_kernel,
        "fake_branch",
        (
            inside,
            first,
            middle,
            last,
            stats,
            bn_gain.reshape(1, G),
            bn_shift.reshape(1, G),
            weight,
            cot_fake.reshape(C * 2 * Y, X),
            real_terms,
        ),
        [
            shape((C * 2 * Y, X), BF16),
            shape((C, CELLS), BF16),
            shape((C, CELLS), BF16),
            shape((NDEV * 8, 128), F32),
        ],
        [
            pltpu.VMEM((6, 128, CELLS), F32),
            pltpu.VMEM((NDEV * 8, 128), F32),
            pltpu.VMEM((C, 2048), BF16),
            pltpu.SemaphoreType.DMA((10,)),
            pltpu.VMEM((6 * 512, CELLS), BF16),
        ]
        + working,
        8 * 2048 * C * CELLS * 2,
        26,
        smem=(0,),
        far=(1, 2, 3, 7, 9),
        far_outs=(1, 2),
    )
    parts = lax.all_to_all(terms.reshape(NDEV, 8, 128), AXES, 0, 0, tiled=True)
    grad_prev = to_next(high)
    grad_next = to_prev(low)
    pull_wide, pull_first, pull_middle, pull_last = call(
        pull_own_kernel,
        "pull_own",
        (low, high, taps_d),
        [
            shape((256, 1152), BF16),
            shape((128, CELLS), F32),
            shape((256, CELLS), BF16),
            shape((128, CELLS), F32),
        ],
        [
            pltpu.VMEM((2, C, CELLS), BF16),
            pltpu.VMEM((2048, C), BF16),
            pltpu.VMEM((256, 1152), BF16),
            pltpu.VMEM((128, CELLS), F32),
            pltpu.VMEM((256, CELLS), BF16),
            pltpu.VMEM((128, CELLS), F32),
            pltpu.VMEM((1152, CELLS), BF16),
            pltpu.SemaphoreType.DMA((7,)),
        ],
        2 * 384 * 1152 * CELLS,
        8,
        far=(0, 1, 2),
        far_outs=(0, 1, 2, 3),
    )
    (sums,) = call(
        sum_kernel,
        "sum_terms",
        (parts.reshape(NDEV * 8, 128), grad_prev, pull_middle),
        [shape((NDEV * 8, 128), BF16)],
        [],
        NDEV * 1024,
        4,
        far=(1, 2),
    )
    whole = lax.all_to_all(sums.reshape(NDEV, 8, 128), AXES, 0, 0, tiled=True)
    (pull_rows,) = call(
        pull_prev_kernel,
        "pull_prev",
        (grad_prev, pull_wide, pull_first, pull_middle, sums),
        [shape((2, G * 64, X), F32)],
        [
            pltpu.VMEM((C, CELLS), BF16),
            pltpu.VMEM((256, 1152), BF16),
            pltpu.VMEM((128, CELLS), F32),
            pltpu.VMEM((256, CELLS), BF16),
            pltpu.VMEM((576, CELLS), BF16),
            pltpu.SemaphoreType.DMA((4,)),
        ],
        2 * 128 * 1152 * CELLS,
        8,
        far=(0, 1, 2, 3, 4),
    )
    (fake_grad,) = call(
        pull_next_kernel,
        "pull_next",
        (grad_next, pull_wide, pull_last, pull_rows),
        [shape((G * 64, 2 * X), BF16)],
        [
            pltpu.VMEM((256, 1152), BF16),
            pltpu.VMEM((128, CELLS), F32),
            pltpu.VMEM((576, CELLS), BF16),
            pltpu.VMEM((2, G * 64, X), F32),
            pltpu.SemaphoreType.DMA((2,)),
        ],
        2 * 128 * 576 * CELLS,
        8,
        far=(1, 2),
    )
    (weight_grad,) = call(
        unpack_kernel,
        "unpack",
        (whole.reshape(NDEV * 8, 128),),
        [shape((2048, C), F32)],
        [],
        0,
        4,
    )
    return (
        d_fake.reshape(1, C, 2, Y, X),
        d_real.reshape(1, C, 2, Y, X),
        fake_grad.reshape(1, G, 4, 2 * Y, 2 * X),
        weight_grad.reshape(4, 4, 4, G, C),
    )


def solution(mesh):
    split = P(("section", "rep"), None, "slab", None, None)
    in_specs = (split, P(), P(), P(), split, P(), split, split)
    out_specs = (split, split, split, P())
    return jax.shard_map(local, mesh=mesh, in_specs=in_specs, out_specs=out_specs, check_vma=False)
```

```python
import jax
import jax.numpy as jnp
from jax import lax
from jax.experimental import pallas as pl
from jax.experimental.pallas import tpu as pltpu
from jax.sharding import PartitionSpec as P

AXES = ("section", "slab", "rep")
NDEV = 128
C = 64
G = 32
Y = 8
X = 128
CELLS = Y * X
F32 = jnp.float32
BF16 = jnp.bfloat16

phase_taps = (((1, 0), (3, -1)), ((0, 1), (2, 0)))


def dot(a, b, dims=(1, 0)):
    return lax.dot_general(a, b, (((dims[0],), (dims[1],)), ((), ())), preferred_element_type=F32)


def lanes(shape):
    return lax.broadcasted_iota(jnp.int32, shape, len(shape) - 1)


def from_left(tile, lane):
    return jnp.where(lane == 0, 0.0, pltpu.roll(tile, 1, 1))


def from_right(tile, lane):
    return jnp.where(lane == X - 1, 0.0, pltpu.roll(tile, X - 1, 1))


def spread_weights(taps_ref, wide_ref):
    wide_ref[...] = jnp.zeros_like(wide_ref)
    for pz in range(2):
        for py in range(2):
            for px in range(2):
                row = ((1 - pz) * 4 + py * 2 + px) * G
                for kz, oz in phase_taps[pz]:
                    tz = oz if pz == 1 else oz + 1
                    for ky, oy in phase_taps[py]:
                        for kx, ox in phase_taps[px]:
                            col = (oy + 1) * 192 + (ox + 1) * 64
                            tap = (kz * 16 + ky * 4 + kx) * G
                            wide_ref[tz, row : row + G, col : col + C] = taps_ref[tap : tap + G, :]


def spread_cells(tile, depth, y, lane, patch_ref):
    for xi, moved in ((0, from_left(tile, lane)), (1, tile), (2, from_right(tile, lane))):
        piece = moved.astype(BF16)
        for yi in range(3):
            to = y - (yi - 1)
            if 0 <= to < Y:
                row = depth * 576 + yi * 192 + xi * 64
                patch_ref[row : row + C, to * X : (to + 1) * X] = piece


def clear_rims(depth, patch_ref):
    edge = jnp.zeros((192, X), BF16)
    patch_ref[depth * 576 : depth * 576 + 192, 0:X] = edge
    patch_ref[depth * 576 + 384 : depth * 576 + 576, CELLS - X : CELLS] = edge


def fetch(source, target, sem):
    copy = pltpu.make_async_copy(source, target, sem)
    copy.start()
    return copy


def as_row(column, shift):
    sub = lax.broadcasted_iota(jnp.int32, (G, 128), 0)
    return jnp.sum(jnp.where(lanes((G, 128)) == sub + shift, column, 0.0), axis=0, keepdims=True)


def as_column(row, shift):
    shape = (G, row.shape[1])
    sub = lax.broadcasted_iota(jnp.int32, shape, 0)
    return jnp.sum(jnp.where(lanes(shape) == sub + shift, row, 0.0), axis=1, keepdims=True)


def edge_kernel(lat_in, real_in, edge_ref, lat_edge, real_edge, sems):
    copies = [
        fetch(lat_in.at[:, 0], lat_edge, sems.at[0]),
        fetch(real_in.at[:, 0], real_edge, sems.at[1]),
    ]
    join_edge(copies, lat_edge, real_edge, edge_ref)


def join_edge(copies, lat_edge, real_edge, edge_ref):
    copies[0].wait()
    edge_ref[0:512, :] = lat_edge[...].reshape(512, X)
    copies[1].wait()
    edge = real_edge[...].reshape(512, 2 * X)
    edge_ref[512:1024, :] = edge[:, 0:X]
    edge_ref[1024:1536, :] = edge[:, X : 2 * X]


def cell_stats(ref, first, count):
    blocks = range(first, first + count)
    total = jnp.zeros((G, CELLS), F32)
    for block in blocks:
        total += ref[block * G : (block + 1) * G, :]
    mean = jnp.sum(total, axis=1, keepdims=True) * (1.0 / (count * CELLS))
    squares = jnp.zeros((G, CELLS), F32)
    for block in blocks:
        off = ref[block * G : (block + 1) * G, :] - mean
        squares += off * off
    return mean, jnp.sum(squares, axis=1, keepdims=True)


def own_kernel(
    lat_in,
    real_in,
    taps_in,
    taps_d_in,
    wide_out,
    first_out,
    middle_out,
    last_out,
    sums_ref,
    edge_ref,
    weight_out,
    lat_edge,
    real_edge,
    lat,
    taps,
    taps_d,
    weight,
    wide,
    first,
    middle,
    last,
    sems,
    patch,
    wide_lat,
):
    edge_copies = [
        fetch(lat_in.at[:, 1], lat_edge, sems.at[0]),
        fetch(real_in.at[:, 3], real_edge, sems.at[1]),
    ]
    lat_copy = fetch(lat_in, lat, sems.at[2])
    taps_copy = fetch(taps_in, taps, sems.at[3])
    taps_d_copy = fetch(taps_d_in, taps_d, sems.at[4])
    lat_copy.wait()
    wide_lat[...] = lat[...].reshape(1024, X).astype(F32)
    lane = lanes((C, X))
    for depth in range(2):
        clear_rims(depth, patch)
        for y in range(Y):
            spread_cells(wide_lat[pl.ds(depth * Y + y, C, stride=16), :], depth, y, lane, patch)
    taps_copy.wait()
    spread_weights(taps, wide)
    copies = [fetch(wide, wide_out, sems.at[5])]
    last[...] = dot(wide[0], patch[576:1152, :])
    copies.append(fetch(last, last_out, sems.at[6]))
    middle[...] = dot(wide[0], patch[0:576, :]) + dot(wide[1], patch[576:1152, :])
    copies.append(fetch(middle, middle_out, sems.at[7]))
    first[...] = dot(wide[1], patch[0:576, :])
    copies.append(fetch(first, first_out, sems.at[8]))
    taps_d_copy.wait()
    same = lax.broadcasted_iota(jnp.int32, (C, C), 0) == lanes((C, C))
    unit = jnp.where(same, 1.0, 0.0).astype(BF16)
    weight[...] = dot(unit, taps_d[...], (1, 1)).astype(BF16)
    copies.append(fetch(weight, weight_out, sems.at[9]))
    join_edge(edge_copies, lat_edge, real_edge, edge_ref)
    place = lanes((G, 128))
    sums = jnp.zeros((G, 128), F32)
    for at, column in enumerate(cell_stats(middle, 0, 8) + cell_stats(first, 4, 4)):
        sums = jnp.where(place == at, column, sums)
    sums_ref[...] = sums
    for copy in copies:
        copy.wait()


def rim_kernel(
    inside_ref,
    next_ref,
    sums_ref,
    gain_ref,
    shift_ref,
    wide_in,
    last_in,
    last_out,
    stats_out,
    real_next_out,
    patch,
    wide_lat,
    wide,
    last,
    stats,
    sems,
):
    wide_copy = fetch(wide_in.at[1], wide, sems.at[0])
    last_copy = fetch(last_in, last, sems.at[1])
    copies = [fetch(next_ref.at[512:1536], real_next_out, sems.at[2])]
    wide_lat[...] = next_ref[0:512, :].astype(F32)
    lane = lanes((C, X))
    clear_rims(0, patch)
    for y in range(Y):
        spread_cells(wide_lat[pl.ds(y, C, stride=8), :], 0, y, lane, patch)
    wide_copy.wait()
    added = dot(wide[...], patch[...])
    last_copy.wait()
    last[...] += added
    copies.append(fetch(last, last_out, sems.at[3]))
    groups = [(2.0, sums_ref[:, 0:1], sums_ref[:, 1:2])]
    groups.append((jnp.where(inside_ref[0] > 0, 0.0, 1.0), sums_ref[:, 2:3], sums_ref[:, 3:4]))
    groups.append((1.0,) + cell_stats(last, 0, 4))
    groups.append((jnp.where(inside_ref[1] > 0, 1.0, 0.0),) + cell_stats(last, 4, 4))
    depths = jnp.zeros((G, 1), F32)
    mean = jnp.zeros((G, 1), F32)
    for weight, one, _ in groups:
        depths += weight
        mean += weight * one
    mean /= depths
    spread = jnp.zeros((G, 1), F32)
    for weight, one, squares in groups:
        own = squares if isinstance(weight, float) else weight * squares
        spread += own + weight * (4.0 * CELLS) * (one - mean) * (one - mean)
    row = as_row(mean, 0) + as_row(spread, G)
    row += as_row(as_column(gain_ref[...], 0), 2 * G) + as_row(as_column(shift_ref[...], 0), 3 * G)
    stats[...] = jnp.broadcast_to(row, (NDEV, 128))
    copies.append(fetch(stats, stats_out, sems.at[4]))
    for copy in copies:
        copy.wait()


def activate(before):
    squashed = jax.nn.sigmoid(4.0 * before)
    output = before * (0.2 + 0.8 * squashed)
    derivative = 0.2 + 0.8 * squashed + 3.2 * before * squashed * (1.0 - squashed)
    return (output, derivative)


def convolve(weight_ref, patch):
    early = weight_ref[:, 0:1024]
    late = weight_ref[:, 1024:2048]
    shared = dot(jnp.concatenate([late, early], axis=0), patch[1024:2048, :])
    return (
        dot(early, patch[0:1024, :]) + shared[0:C, :],
        shared[C : 2 * C, :] + dot(late, patch[2048:3072, :]),
    )


def finish(pre, cot_ref, out_ref, wide_cot, wide_out, grad):
    wide_cot[...] = cot_ref[...].astype(F32)
    nothing = jnp.zeros((C, CELLS), BF16)
    grad[0:C, :] = nothing
    grad[3 * C : 4 * C, :] = nothing
    for m in range(2):
        for y in range(Y):
            output, slope = activate(pre[m][:, y * X : (y + 1) * X])
            wide_out[pl.ds(m * Y + y, C, stride=16), :] = output
            cot = wide_cot[pl.ds(m * Y + y, C, stride=16), :]
            grad[(2 - m) * C : (3 - m) * C, y * X : (y + 1) * X] = (cot * slope).astype(BF16)
    out_ref[...] = wide_out[...].astype(BF16)


def kernel_terms(planes, grad):
    halves = []
    for half in range(2):
        terms = dot(planes[half], grad[128:256, :], (1, 1))
        terms += dot(planes[half + 2], grad[64:192, :], (1, 1))
        halves.append(terms + dot(planes[half + 4], grad[0:128, :], (1, 1)))
    return halves


def split_depth(at, places, halves, rows, patch):
    base, stride = places
    column = lanes((2 * X, 4 * X))
    source = lax.broadcasted_iota(jnp.int32, (2 * X, 4 * X), 0)
    pick = jnp.where(source == 2 * (column % X) + column // X - 1, 1.0, 0.0).astype(BF16)
    edge = jnp.zeros((128, X), BF16)
    patch[at : at + 128, 0:X] = edge
    patch[at + 384 : at + 512, CELLS - X : CELLS] = edge
    for row in range(2 * Y):
        for half in range(2):
            cells = halves[half, pl.ds(base + row, G, stride=stride), :].astype(BF16)
            rows[at + row * G : at + (row + 1) * G, half * X : (half + 1) * X] = cells
    split = dot(rows[at : at + 512, :], pick).astype(BF16)
    for row in range(2 * Y):
        for kx in range(4):
            piece = split[row * G : (row + 1) * G, kx * X : (kx + 1) * X]
            for ky in range(4):
                if (row + 1 - ky) % 2 == 0 and 0 <= (row + 1 - ky) // 2 < Y:
                    y = (row + 1 - ky) // 2
                    place = at + ky * 128 + kx * G
                    patch[place : place + G, y * X : (y + 1) * X] = piece


def real_kernel(
    real_ref,
    prev_ref,
    next_in,
    weight_in,
    cot_ref,
    wide_in,
    first_in,
    out_ref,
    terms_out,
    first_out,
    edge,
    weight,
    wide,
    first,
    terms_ref,
    sems,
    patch,
    lat_patch,
    halves,
    rows,
    wide_cot,
    wide_out,
    grad,
):
    edge_copy = fetch(next_in, edge, sems.at[0])
    for half in range(2):
        part = slice(512 + half * 512, 1024 + half * 512)
        halves[half, 0:2048, :] = real_ref[:, half * X : (half + 1) * X].astype(F32)
        halves[half, 2048:2560, :] = prev_ref[part, :].astype(F32)
    places = ((2048, 16), (0, 64), (16, 64), (32, 64), (48, 64), (2560, 16))
    for depth in range(2):
        split_depth(depth * 512, places[depth], halves, rows, patch)
    edge_copy.wait()
    copies = [
        fetch(weight_in, weight, sems.at[1]),
        fetch(wide_in.at[0], wide, sems.at[2]),
        fetch(first_in, first, sems.at[3]),
    ]
    for half in range(2):
        halves[half, 2560:3072, :] = edge[half * 512 : (half + 1) * 512, :].astype(F32)
    for depth in range(2, 6):
        split_depth(depth * 512, places[depth], halves, rows, patch)
    halves[0, 0:512, :] = prev_ref[0:512, :].astype(F32)
    lane = lanes((C, X))
    clear_rims(0, lat_patch)
    for y in range(Y):
        spread_cells(halves[0, pl.ds(y, C, stride=8), :], 0, y, lane, lat_patch)
    for copy in copies:
        copy.wait()
    first[...] += dot(wide[...], lat_patch[...])
    first_copy = fetch(first, first_out, sems.at[4])
    finish(convolve(weight, patch), cot_ref, out_ref, wide_cot, wide_out, grad)
    planes = [patch[depth * 512 : (depth + 1) * 512, :] for depth in range(6)]
    for half, terms in enumerate(kernel_terms(planes, grad)):
        terms_ref[half * 512 : (half + 1) * 512, :] = terms
    fetch(terms_ref, terms_out, sems.at[5]).wait()
    first_copy.wait()


def fake_kernel(
    inside_ref,
    first_in,
    middle_in,
    last_in,
    stats_ref,
    weight_in,
    cot_ref,
    real_terms_in,
    out_ref,
    low_out,
    high_out,
    terms_ref,
    before,
    real_terms,
    weight_ref,
    sems,
    patch,
    wide_cot,
    wide_out,
    grad,
):
    def fetch_before(depth):
        ref = (first_in, middle_in, last_in)[depth // 2]
        half = pl.ds(depth % 2 * 128, 128)
        return fetch(ref.at[half], before.at[depth], sems.at[depth])

    befores = [fetch_before(depth) for depth in range(3)]
    stats = stats_ref[...]
    slab = lax.broadcasted_iota(jnp.int32, (NDEV, 128), 0) // 2 % 32
    depths = jnp.where(slab == 0, 5.0, jnp.where(slab == 31, 3.0, 4.0))
    mean_row = jnp.sum(stats * depths, axis=0, keepdims=True) * (1.0 / (4.0 * NDEV))
    off = stats - mean_row
    between = as_column(jnp.sum(off * off * depths, axis=0, keepdims=True), 0)
    center = as_column(mean_row, 0)
    within = as_column(jnp.sum(stats, axis=0, keepdims=True), G)
    variance = (within + 4.0 * CELLS * between) * (1.0 / (16.0 * CELLS * NDEV))
    factor = as_column(stats[0:1, :], 2 * G) * lax.rsqrt(variance + 1e-05)
    shift = as_column(stats[0:1, :], 3 * G)
    lane = lanes((G, X))
    edge = jnp.zeros((128, X), BF16)
    for depth in range(6):
        befores[depth].wait()
        if depth < 3:
            befores.append(fetch_before(depth + 3))
        elif depth == 3:
            weight_copy = fetch(weight_in, weight_ref, sems.at[6])
        elif depth == 4:
            real_copy = fetch(real_terms_in, real_terms, sems.at[7])
        patch[depth * 512 : depth * 512 + 128, 0:X] = edge
        patch[depth * 512 + 384 : depth * 512 + 512, CELLS - X : CELLS] = edge
        for py in range(2):
            for px in range(2):
                block = (py * 2 + px) * G
                for y in range(Y):
                    cells = before[depth, block : block + G, y * X : (y + 1) * X]
                    fake = jnp.maximum((cells - center) * factor + shift, 0.0)
                    if depth == 0:
                        fake = jnp.where(inside_ref[0] > 0, fake, 0.0)
                    if depth == 5:
                        fake = jnp.where(inside_ref[1] > 0, fake, 0.0)
                    if px == 1:
                        pieces = ((2, fake), (0, from_left(fake, lane)))
                    else:
                        pieces = ((1, fake), (3, from_right(fake, lane)))
                    for kx, piece in pieces:
                        piece = piece.astype(BF16)
                        for ky, to in ((2, y), (0, y + 1)) if py == 1 else ((1, y), (3, y - 1)):
                            if 0 <= to < Y:
                                at = depth * 512 + ky * 128 + kx * G
                                patch[at : at + G, to * X : (to + 1) * X] = piece
    weight_copy.wait()
    pre = convolve(weight_ref, patch)
    finish(pre, cot_ref, out_ref, wide_cot, wide_out, grad)
    edge_copies = [
        fetch(grad.at[2 * C : 3 * C], low_out, sems.at[8]),
        fetch(grad.at[C : 2 * C], high_out, sems.at[9]),
    ]
    planes = [patch[depth * 512 : (depth + 1) * 512, :] for depth in range(6)]
    real_copy.wait()
    for half, terms in enumerate(kernel_terms(planes, grad)):
        rows = slice(half * 512, (half + 1) * 512)
        terms_ref[rows, :] = terms + real_terms[rows, :]
    for copy in edge_copies:
        copy.wait()


def sum_kernel(parts_ref, prev_ref, next_ref, first_ref, sums_ref):
    del prev_ref, next_ref, first_ref
    total = jnp.sum(parts_ref[...].reshape(NDEV, 8, 128), axis=0, keepdims=True)
    sums_ref[...] = jnp.broadcast_to(total, (NDEV, 8, 128)).reshape(NDEV * 8, 128).astype(BF16)


def unpack_kernel(sums_ref, out, whole, sems):
    copies = []
    for part in range(4):
        rows = slice(part * 256, (part + 1) * 256)
        sums = sums_ref[rows, :].astype(F32)
        whole[0, rows, :] = sums[:, 0:C]
        whole[1, rows, :] = sums[:, C : 2 * C]
        for half in range(2):
            piece = pl.ds(part * 256, 256)
            copies.append(fetch(whole.at[half, piece], out.at[half, piece], sems.at[2 * part + half]))
    for copy in copies:
        copy.wait()


def weave_into(result, first_row, stride, wide_out):
    column = lanes((2 * X, 2 * X))
    source = lax.broadcasted_iota(jnp.int32, (2 * X, 2 * X), 0)
    weave = jnp.where(source == (column % 2) * X + column // 2, 1.0, 0.0).astype(BF16)
    for py in range(2):
        even = result[py * 64 : py * 64 + G, :]
        odd = result[py * 64 + G : py * 64 + 2 * G, :]
        both = jnp.concatenate(
            [
                jnp.concatenate([even[:, y * X : (y + 1) * X], odd[:, y * X : (y + 1) * X]], axis=1)
                for y in range(Y)
            ],
            axis=0,
        )
        woven = dot(both, weave)
        for y in range(Y):
            rows = pl.ds(first_row + 2 * y + py, G, stride=stride)
            wide_out[0, rows, :] = woven[y * G : (y + 1) * G, 0:X]
            wide_out[1, rows, :] = woven[y * G : (y + 1) * G, X : 2 * X]


def spread_edge(cells, depth, patch):
    lane = lanes((C, X))
    clear_rims(depth, patch)
    for y in range(Y):
        spread_cells(cells[:, y * X : (y + 1) * X].astype(F32), depth, y, lane, patch)


def pull_own_kernel(
    low_in,
    high_in,
    taps_in,
    wide_out,
    first_out,
    last_out,
    image_out,
    cells,
    taps,
    wide,
    first,
    last,
    patch,
    wide_rows,
    image,
    sems,
):
    edges = [fetch(ref, cells.at[i], sems.at[i]) for i, ref in enumerate((low_in, high_in))]
    taps_copy = fetch(taps_in, taps, sems.at[2])
    for depth in range(2):
        edges[depth].wait()
        spread_edge(cells[depth], depth, patch)
    taps_copy.wait()
    spread_weights(taps, wide)
    copies = [fetch(wide, wide_out, sems.at[3])]
    first[...] = dot(wide[1, 128:256, :], patch[0:576, :])
    copies.append(fetch(first, first_out, sems.at[4]))
    last[...] = dot(wide[0, 0:128, :], patch[576:1152, :])
    copies.append(fetch(last, last_out, sems.at[5]))
    middle = dot(wide[0], patch[0:576, :]) + dot(wide[1], patch[576:1152, :])
    middle = middle.astype(BF16)
    weave_into(middle[0:128, :], 0, 32, wide_rows)
    weave_into(middle[128:256, :], 16, 32, wide_rows)
    for half in range(2):
        image[:, :, half * X : (half + 1) * X] = wide_rows[half].reshape(G, 32, X).astype(BF16)
    copies.append(fetch(image, image_out.at[:, 16:48], sems.at[6]))
    for copy in copies:
        copy.wait()


def pullback_kernel(
    prev_in,
    next_in,
    wide_in,
    first_in,
    last_in,
    sums_ref,
    image_in,
    image_out,
    cells,
    wide,
    outer,
    patch,
    wide_rows,
    image,
    sems,
):
    del sums_ref, image_in
    edges = [fetch(ref, cells.at[i], sems.at[i]) for i, ref in enumerate((prev_in, next_in))]
    copies = [
        fetch(wide_in, wide, sems.at[2]),
        fetch(first_in, outer.at[0], sems.at[3]),
        fetch(last_in, outer.at[1], sems.at[4]),
    ]
    for side in range(2):
        edges[side].wait()
        spread_edge(cells[side], side, patch)
    for copy in copies:
        copy.wait()
    stores = []
    for side in range(2):
        rows = slice(128 - side * 128, 256 - side * 128)
        added = dot(wide[side, rows, :], patch[side * 576 : (side + 1) * 576, :])
        weave_into((outer[side] + added).astype(BF16), 0, 16, wide_rows.at[side])
        for half in range(2):
            columns = slice(half * X, (half + 1) * X)
            image[side, :, :, columns] = wide_rows[side, half].reshape(G, 16, X).astype(BF16)
        place = pl.ds(side * 48, 16)
        stores.append(fetch(image.at[side], image_out.at[:, place], sems.at[5 + side]))
    for copy in stores:
        copy.wait()


def call(body, name, args, outs, scratch, flops, mebibytes, smem=(), far=(), far_outs=(), aliases=()):
    moved = sum(a.size * a.dtype.itemsize for a in args) + sum(o.size * o.dtype.itemsize for o in outs)
    spaces = [
        pltpu.SMEM if i in smem else pl.ANY if i in far else pltpu.VMEM for i in range(len(args))
    ]
    out_spaces = [pltpu.HBM if i in far_outs else pltpu.VMEM for i in range(len(outs))]
    outs = [pltpu.HBM(o.shape, o.dtype) if i in far_outs else o for i, o in enumerate(outs)]
    args = [
        pltpu.with_memory_space_constraint(a, pltpu.HBM) if i in far else a for i, a in enumerate(args)
    ]
    return pl.pallas_call(
        body,
        name=name,
        out_shape=outs,
        in_specs=[pl.BlockSpec(memory_space=space) for space in spaces],
        out_specs=[pl.BlockSpec(memory_space=space) for space in out_spaces],
        scratch_shapes=scratch,
        input_output_aliases=dict(aliases),
        compiler_params=pltpu.CompilerParams(vmem_limit_bytes=mebibytes * 1024 * 1024),
        cost_estimate=pl.CostEstimate(flops=flops, bytes_accessed=moved, transcendentals=0),
    )(*args)


def to_next(edge):
    ends = lax.axis_size("slab") - 1
    return lax.ppermute(edge, "slab", [(i, i + 1) for i in range(ends)])


def to_prev(edge):
    ends = lax.axis_size("slab") - 1
    return lax.ppermute(edge, "slab", [(i + 1, i) for i in range(ends)])


def local(latent, g_weight, bn_gain, bn_shift, real_crops, d_weight, cot_fake, cot_real):
    shape = jax.ShapeDtypeStruct
    taps_g = g_weight.transpose(0, 1, 2, 4, 3).reshape(64 * G, C)
    taps_d = d_weight.reshape(64 * G, C)
    lat = latent[0]
    real = real_crops[0]
    at = lax.axis_index("slab")
    inside = jnp.stack([at > 0, at < lax.axis_size("slab") - 1]).astype(jnp.int32)
    (low,) = call(
        edge_kernel,
        "edges",
        (lat, real),
        [shape((1536, X), BF16)],
        [
            pltpu.VMEM((C, Y, X), BF16),
            pltpu.VMEM((G, 2 * Y, 2 * X), BF16),
            pltpu.SemaphoreType.DMA((2,)),
        ],
        0,
        4,
        far=(0, 1),
    )
    next_ = to_prev(low)
    wide, first, middle, last, sums, high, weight = call(
        own_kernel,
        "own_cells",
        (lat, real, taps_g, taps_d),
        [shape((2, 256, 576), BF16)]
        + [shape((256, CELLS), F32)] * 3
        + [shape((G, 128), F32), shape((1536, X), BF16), shape((C, 2048), BF16)],
        [
            pltpu.VMEM((C, Y, X), BF16),
            pltpu.VMEM((G, 2 * Y, 2 * X), BF16),
            pltpu.VMEM((C, 2, Y, X), BF16),
            pltpu.VMEM((2048, C), BF16),
            pltpu.VMEM((2048, C), BF16),
            pltpu.VMEM((C, 2048), BF16),
            pltpu.VMEM((2, 256, 576), BF16),
            pltpu.VMEM((256, CELLS), F32),
            pltpu.VMEM((256, CELLS), F32),
            pltpu.VMEM((256, CELLS), F32),
            pltpu.SemaphoreType.DMA((10,)),
            pltpu.VMEM((1152, CELLS), BF16),
            pltpu.VMEM((1024, X), F32),
        ],
        4 * 256 * 1152 * CELLS,
        16,
        far=(0, 1, 2, 3),
        far_outs=(0, 1, 2, 3, 6),
    )
    prev = to_next(high)
    last, stats, real_next = call(
        rim_kernel,
        "rim_cells",
        (inside, next_, sums, bn_gain.reshape(1, G), bn_shift.reshape(1, G), wide, last),
        [shape((256, CELLS), F32), shape((NDEV, 128), F32), shape((1024, X), BF16)],
        [
            pltpu.VMEM((576, CELLS), BF16),
            pltpu.VMEM((512, X), F32),
            pltpu.VMEM((256, 576), BF16),
            pltpu.VMEM((256, CELLS), F32),
            pltpu.VMEM((NDEV, 128), F32),
            pltpu.SemaphoreType.DMA((5,)),
        ],
        256 * 1152 * CELLS,
        12,
        smem=(0,),
        far=(5, 6),
        far_outs=(0, 1, 2),
    )
    stats = lax.all_to_all(stats, AXES, 0, 0, tiled=True)
    working = [
        pltpu.VMEM((C * 2 * Y, X), F32),
        pltpu.VMEM((C * 2 * Y, X), F32),
        pltpu.VMEM((4 * C, CELLS), BF16),
    ]
    d_real, real_terms, first = call(
        real_kernel,
        "real_branch",
        (
            real.reshape(G * 64, 2 * X),
            prev,
            real_next,
            weight,
            cot_real.reshape(C * 2 * Y, X),
            wide,
            first,
        ),
        [shape((C * 2 * Y, X), BF16), shape((1024, 2 * C), F32), shape((256, CELLS), F32)],
        [
            pltpu.VMEM((1024, X), BF16),
            pltpu.VMEM((C, 2048), BF16),
            pltpu.VMEM((256, 576), BF16),
            pltpu.VMEM((256, CELLS), F32),
            pltpu.VMEM((1024, 2 * C), F32),
            pltpu.SemaphoreType.DMA((6,)),
            pltpu.VMEM((6 * 512, CELLS), BF16),
            pltpu.VMEM((576, CELLS), BF16),
            pltpu.VMEM((2, 3072, X), F32),
            pltpu.VMEM((3072, 2 * X), BF16),
        ]
        + working,
        16 * 2048 * C * CELLS,
        26,
        far=(2, 3, 5, 6),
        far_outs=(1, 2),
    )
    d_fake, low, high, terms = call(
        fake_kernel,
        "fake_branch",
        (
            inside,
            first,
            middle,
            last,
            stats,
            weight,
            cot_fake.reshape(C * 2 * Y, X),
            real_terms,
        ),
        [
            shape((C * 2 * Y, X), BF16),
            shape((C, CELLS), BF16),
            shape((C, CELLS), BF16),
            shape((NDEV * 8, 128), F32),
        ],
        [
            pltpu.VMEM((6, 128, CELLS), F32),
            pltpu.VMEM((NDEV * 8, 128), F32),
            pltpu.VMEM((C, 2048), BF16),
            pltpu.SemaphoreType.DMA((10,)),
            pltpu.VMEM((6 * 512, CELLS), BF16),
        ]
        + working,
        8 * 2048 * C * CELLS * 2,
        26,
        smem=(0,),
        far=(1, 2, 3, 5, 7),
        far_outs=(1, 2),
    )
    parts = lax.all_to_all(terms.reshape(NDEV, 8, 128), AXES, 0, 0, tiled=True)
    grad_prev = to_next(high)
    grad_next = to_prev(low)
    pull_wide, pull_first, pull_last, image = call(
        pull_own_kernel,
        "pull_own",
        (low, high, taps_d),
        [
            shape((2, 256, 576), BF16),
            shape((128, CELLS), F32),
            shape((128, CELLS), F32),
            shape((G, 64, 2 * X), BF16),
        ],
        [
            pltpu.VMEM((2, C, CELLS), BF16),
            pltpu.VMEM((2048, C), BF16),
            pltpu.VMEM((2, 256, 576), BF16),
            pltpu.VMEM((128, CELLS), F32),
            pltpu.VMEM((128, CELLS), F32),
            pltpu.VMEM((1152, CELLS), BF16),
            pltpu.VMEM((2, G * 32, X), F32),
            pltpu.VMEM((G, 32, 2 * X), BF16),
            pltpu.SemaphoreType.DMA((7,)),
        ],
        2 * 384 * 1152 * CELLS,
        16,
        far=(0, 1, 2),
        far_outs=(0, 1, 2, 3),
    )
    (sums,) = call(
        sum_kernel,
        "sum_terms",
        (parts.reshape(NDEV * 8, 128), grad_prev, grad_next, pull_first),
        [shape((NDEV * 8, 128), BF16)],
        [],
        NDEV * 1024,
        6,
        far=(1, 2, 3),
    )
    whole = lax.all_to_all(sums.reshape(NDEV, 8, 128), AXES, 0, 0, tiled=True)
    (fake_grad,) = call(
        pullback_kernel,
        "pullback",
        (grad_prev, grad_next, pull_wide, pull_first, pull_last, sums, image),
        [shape((G, 64, 2 * X), BF16)],
        [
            pltpu.VMEM((2, C, CELLS), BF16),
            pltpu.VMEM((2, 256, 576), BF16),
            pltpu.VMEM((2, 128, CELLS), F32),
            pltpu.VMEM((1152, CELLS), BF16),
            pltpu.VMEM((2, 2, G * 16, X), F32),
            pltpu.VMEM((2, G, 16, 2 * X), BF16),
            pltpu.SemaphoreType.DMA((7,)),
        ],
        2 * 128 * 1152 * CELLS,
        16,
        far=(0, 1, 2, 3, 4, 5, 6),
        far_outs=(0,),
        aliases=((6, 0),),
    )
    (weight_grad,) = call(
        unpack_kernel,
        "unpack",
        (whole.reshape(NDEV * 8, 128),),
        [shape((2, 1024, C), F32)],
        [pltpu.VMEM((2, 1024, C), F32), pltpu.SemaphoreType.DMA((8,))],
        0,
        6,
        far_outs=(0,),
    )
    return (
        d_fake.reshape(1, C, 2, Y, X),
        d_real.reshape(1, C, 2, Y, X),
        fake_grad.reshape(1, G, 4, 2 * Y, 2 * X),
        weight_grad.reshape(4, 4, 4, G, C),
    )


def solution(mesh):
    split = P(("section", "rep"), None, "slab", None, None)
    in_specs = (split, P(), P(), P(), split, P(), split, split)
    out_specs = (split, split, split, P())
    return jax.shard_map(local, mesh=mesh, in_specs=in_specs, out_specs=out_specs, check_vma=False)
```

```python
import functools

import jax
import jax.numpy as jnp
from jax import lax
from jax.experimental import pallas as pl
from jax.experimental.pallas import tpu as pltpu
from jax.sharding import PartitionSpec as P

AXES = ("section", "slab", "rep")
NDEV = 128
C = 64
G = 32
Y = 8
X = 128
CELLS = Y * X
F32 = jnp.float32
BF16 = jnp.bfloat16

phase_taps = (((1, 0), (3, -1)), ((0, 1), (2, 0)))


def dot(a, b, dims=(1, 0)):
    return lax.dot_general(a, b, (((dims[0],), (dims[1],)), ((), ())), preferred_element_type=F32)


def lanes(shape):
    return lax.broadcasted_iota(jnp.int32, shape, len(shape) - 1)


def from_left(tile, lane):
    return jnp.where(lane == 0, 0.0, pltpu.roll(tile, 1, 1))


def from_right(tile, lane):
    return jnp.where(lane == X - 1, 0.0, pltpu.roll(tile, X - 1, 1))


def spread_weights(taps_ref, wide_ref):
    wide_ref[...] = jnp.zeros_like(wide_ref)
    for pz in range(2):
        for py in range(2):
            for px in range(2):
                row = ((1 - pz) * 4 + py * 2 + px) * G
                for kz, oz in phase_taps[pz]:
                    tz = oz if pz == 1 else oz + 1
                    for ky, oy in phase_taps[py]:
                        for kx, ox in phase_taps[px]:
                            col = (oy + 1) * 192 + (ox + 1) * 64
                            tap = (kz * 16 + ky * 4 + kx) * G
                            wide_ref[tz, row : row + G, col : col + C] = taps_ref[tap : tap + G, :]


def spread_cells(tile, depth, y, lane, patch_ref):
    for xi, moved in ((0, from_left(tile, lane)), (1, tile), (2, from_right(tile, lane))):
        piece = moved.astype(BF16)
        for yi in range(3):
            to = y - (yi - 1)
            if 0 <= to < Y:
                row = depth * 576 + yi * 192 + xi * 64
                patch_ref[row : row + C, to * X : (to + 1) * X] = piece


def clear_rims(depth, patch_ref):
    edge = jnp.zeros((192, X), BF16)
    patch_ref[depth * 576 : depth * 576 + 192, 0:X] = edge
    patch_ref[depth * 576 + 384 : depth * 576 + 576, CELLS - X : CELLS] = edge


def fetch(source, target, sem):
    copy = pltpu.make_async_copy(source, target, sem)
    copy.start()
    return copy


def as_row(column, shift):
    sub = lax.broadcasted_iota(jnp.int32, (G, 128), 0)
    return jnp.sum(jnp.where(lanes((G, 128)) == sub + shift, column, 0.0), axis=0, keepdims=True)


def as_column(row, shift):
    shape = (G, row.shape[1])
    sub = lax.broadcasted_iota(jnp.int32, shape, 0)
    return jnp.sum(jnp.where(lanes(shape) == sub + shift, row, 0.0), axis=1, keepdims=True)


def edge_kernel(lat_in, real_in, edge_ref, lat_edge, real_edge, sems):
    copies = [
        fetch(lat_in.at[:, 0], lat_edge, sems.at[0]),
        fetch(real_in.at[:, 0], real_edge, sems.at[1]),
    ]
    join_edge(copies, lat_edge, real_edge, edge_ref)


def join_edge(copies, lat_edge, real_edge, edge_ref):
    copies[0].wait()
    edge_ref[0:512, :] = lat_edge[...].reshape(512, X)
    copies[1].wait()
    edge = real_edge[...].reshape(512, 2 * X)
    edge_ref[512:1024, :] = edge[:, 0:X]
    edge_ref[1024:1536, :] = edge[:, X : 2 * X]


def cell_stats(ref, first, count):
    blocks = range(first, first + count)
    total = jnp.zeros((G, CELLS), F32)
    for block in blocks:
        total += ref[block * G : (block + 1) * G, :]
    mean = jnp.sum(total, axis=1, keepdims=True) * (1.0 / (count * CELLS))
    squares = jnp.zeros((G, CELLS), F32)
    for block in blocks:
        off = ref[block * G : (block + 1) * G, :] - mean
        squares += off * off
    return mean, jnp.sum(squares, axis=1, keepdims=True)


def own_kernel(
    lat_in,
    real_in,
    taps_in,
    taps_d_in,
    wide_out,
    first_out,
    middle_out,
    last_out,
    sums_ref,
    edge_ref,
    weight_out,
    lat_edge,
    real_edge,
    lat,
    taps,
    taps_d,
    weight,
    wide,
    first,
    middle,
    last,
    sems,
    patch,
    wide_lat,
):
    edge_copies = [
        fetch(lat_in.at[:, 1], lat_edge, sems.at[0]),
        fetch(real_in.at[:, 3], real_edge, sems.at[1]),
    ]
    lat_copy = fetch(lat_in, lat, sems.at[2])
    taps_copy = fetch(taps_in, taps, sems.at[3])
    taps_d_copy = fetch(taps_d_in, taps_d, sems.at[4])
    lat_copy.wait()
    wide_lat[...] = lat[...].reshape(1024, X).astype(F32)
    lane = lanes((C, X))
    for depth in range(2):
        clear_rims(depth, patch)
        for y in range(Y):
            spread_cells(wide_lat[pl.ds(depth * Y + y, C, stride=16), :], depth, y, lane, patch)
    taps_copy.wait()
    spread_weights(taps, wide)
    copies = [fetch(wide, wide_out, sems.at[5])]
    last[...] = dot(wide[0], patch[576:1152, :])
    copies.append(fetch(last, last_out, sems.at[6]))
    middle[...] = dot(wide[0], patch[0:576, :]) + dot(wide[1], patch[576:1152, :])
    copies.append(fetch(middle, middle_out, sems.at[7]))
    first[...] = dot(wide[1], patch[0:576, :])
    copies.append(fetch(first, first_out, sems.at[8]))
    taps_d_copy.wait()
    same = lax.broadcasted_iota(jnp.int32, (C, C), 0) == lanes((C, C))
    unit = jnp.where(same, 1.0, 0.0).astype(BF16)
    weight[...] = dot(unit, taps_d[...], (1, 1)).astype(BF16)
    copies.append(fetch(weight, weight_out, sems.at[9]))
    join_edge(edge_copies, lat_edge, real_edge, edge_ref)
    place = lanes((G, 128))
    sums = jnp.zeros((G, 128), F32)
    for at, column in enumerate(cell_stats(middle, 0, 8) + cell_stats(first, 4, 4)):
        sums = jnp.where(place == at, column, sums)
    sums_ref[...] = sums
    for copy in copies:
        copy.wait()


def rim_kernel(
    inside_ref,
    next_ref,
    sums_ref,
    gain_in,
    shift_in,
    wide_in,
    last_in,
    last_out,
    stats_out,
    real_next_out,
    patch,
    wide_lat,
    wide,
    last,
    stats,
    gain,
    shift,
    sems,
):
    wide_copy = fetch(wide_in.at[1], wide, sems.at[0])
    last_copy = fetch(last_in, last, sems.at[1])
    affine_copies = [fetch(gain_in, gain, sems.at[5]), fetch(shift_in, shift, sems.at[6])]
    copies = [fetch(next_ref.at[512:1536], real_next_out, sems.at[2])]
    wide_lat[...] = next_ref[0:512, :].astype(F32)
    lane = lanes((C, X))
    clear_rims(0, patch)
    for y in range(Y):
        spread_cells(wide_lat[pl.ds(y, C, stride=8), :], 0, y, lane, patch)
    wide_copy.wait()
    added = dot(wide[...], patch[...])
    last_copy.wait()
    last[...] += added
    copies.append(fetch(last, last_out, sems.at[3]))
    groups = [(2.0, sums_ref[:, 0:1], sums_ref[:, 1:2])]
    groups.append((jnp.where(inside_ref[0] > 0, 0.0, 1.0), sums_ref[:, 2:3], sums_ref[:, 3:4]))
    groups.append((1.0,) + cell_stats(last, 0, 4))
    groups.append((jnp.where(inside_ref[1] > 0, 1.0, 0.0),) + cell_stats(last, 4, 4))
    depths = jnp.zeros((G, 1), F32)
    mean = jnp.zeros((G, 1), F32)
    for weight, one, _ in groups:
        depths += weight
        mean += weight * one
    mean /= depths
    spread = jnp.zeros((G, 1), F32)
    for weight, one, squares in groups:
        own = squares if isinstance(weight, float) else weight * squares
        spread += own + weight * (4.0 * CELLS) * (one - mean) * (one - mean)
    row = as_row(mean, 0) + as_row(spread, G)
    for copy in affine_copies:
        copy.wait()
    row += as_row(as_column(gain[...], 0), 2 * G) + as_row(as_column(shift[...], 0), 3 * G)
    stats[...] = jnp.broadcast_to(row, (NDEV, 128))
    copies.append(fetch(stats, stats_out, sems.at[4]))
    for copy in copies:
        copy.wait()


def activate(before):
    squashed = jax.nn.sigmoid(4.0 * before)
    output = before * (0.2 + 0.8 * squashed)
    derivative = 0.2 + 0.8 * squashed + 3.2 * before * squashed * (1.0 - squashed)
    return (output, derivative)


def convolve(weight_ref, patch):
    early = weight_ref[:, 0:1024]
    late = weight_ref[:, 1024:2048]
    shared = dot(jnp.concatenate([late, early], axis=0), patch[1024:2048, :])
    return (
        dot(early, patch[0:1024, :]) + shared[0:C, :],
        shared[C : 2 * C, :] + dot(late, patch[2048:3072, :]),
    )


def finish(pre, cot_ref, out_ref, wide_cot, wide_out, grad):
    wide_cot[...] = cot_ref[...].astype(F32)
    nothing = jnp.zeros((C, CELLS), BF16)
    grad[0:C, :] = nothing
    grad[3 * C : 4 * C, :] = nothing
    for m in range(2):
        for y in range(Y):
            output, slope = activate(pre[m][:, y * X : (y + 1) * X])
            wide_out[pl.ds(m * Y + y, C, stride=16), :] = output
            cot = wide_cot[pl.ds(m * Y + y, C, stride=16), :]
            grad[(2 - m) * C : (3 - m) * C, y * X : (y + 1) * X] = (cot * slope).astype(BF16)
    out_ref[...] = wide_out[...].astype(BF16)


def kernel_terms(planes, grad):
    halves = []
    for half in range(2):
        terms = dot(planes[half], grad[128:256, :], (1, 1))
        terms += dot(planes[half + 2], grad[64:192, :], (1, 1))
        halves.append(terms + dot(planes[half + 4], grad[0:128, :], (1, 1)))
    return halves


def split_depth(at, places, halves, rows, patch):
    base, stride = places
    column = lanes((2 * X, 4 * X))
    source = lax.broadcasted_iota(jnp.int32, (2 * X, 4 * X), 0)
    pick = jnp.where(source == 2 * (column % X) + column // X - 1, 1.0, 0.0).astype(BF16)
    edge = jnp.zeros((128, X), BF16)
    patch[at : at + 128, 0:X] = edge
    patch[at + 384 : at + 512, CELLS - X : CELLS] = edge
    for row in range(2 * Y):
        for half in range(2):
            cells = halves[half, pl.ds(base + row, G, stride=stride), :].astype(BF16)
            rows[at + row * G : at + (row + 1) * G, half * X : (half + 1) * X] = cells
    split = dot(rows[at : at + 512, :], pick).astype(BF16)
    for row in range(2 * Y):
        for kx in range(4):
            piece = split[row * G : (row + 1) * G, kx * X : (kx + 1) * X]
            for ky in range(4):
                if (row + 1 - ky) % 2 == 0 and 0 <= (row + 1 - ky) // 2 < Y:
                    y = (row + 1 - ky) // 2
                    place = at + ky * 128 + kx * G
                    patch[place : place + G, y * X : (y + 1) * X] = piece


def real_kernel(
    real_ref,
    prev_ref,
    next_in,
    weight_in,
    cot_ref,
    wide_in,
    first_in,
    out_ref,
    terms_out,
    first_out,
    edge,
    weight,
    wide,
    first,
    terms_ref,
    sems,
    patch,
    lat_patch,
    halves,
    rows,
    wide_cot,
    wide_out,
    grad,
):
    edge_copy = fetch(next_in, edge, sems.at[0])
    for half in range(2):
        part = slice(512 + half * 512, 1024 + half * 512)
        halves[half, 0:2048, :] = real_ref[:, half * X : (half + 1) * X].astype(F32)
        halves[half, 2048:2560, :] = prev_ref[part, :].astype(F32)
    places = ((2048, 16), (0, 64), (16, 64), (32, 64), (48, 64), (2560, 16))
    for depth in range(2):
        split_depth(depth * 512, places[depth], halves, rows, patch)
    edge_copy.wait()
    copies = [
        fetch(weight_in, weight, sems.at[1]),
        fetch(wide_in.at[0], wide, sems.at[2]),
        fetch(first_in, first, sems.at[3]),
    ]
    for half in range(2):
        halves[half, 2560:3072, :] = edge[half * 512 : (half + 1) * 512, :].astype(F32)
    for depth in range(2, 6):
        split_depth(depth * 512, places[depth], halves, rows, patch)
    halves[0, 0:512, :] = prev_ref[0:512, :].astype(F32)
    lane = lanes((C, X))
    clear_rims(0, lat_patch)
    for y in range(Y):
        spread_cells(halves[0, pl.ds(y, C, stride=8), :], 0, y, lane, lat_patch)
    for copy in copies:
        copy.wait()
    first[...] += dot(wide[...], lat_patch[...])
    first_copy = fetch(first, first_out, sems.at[4])
    finish(convolve(weight, patch), cot_ref, out_ref, wide_cot, wide_out, grad)
    planes = [patch[depth * 512 : (depth + 1) * 512, :] for depth in range(6)]
    for half, terms in enumerate(kernel_terms(planes, grad)):
        terms_ref[half * 512 : (half + 1) * 512, :] = terms
    fetch(terms_ref, terms_out, sems.at[5]).wait()
    first_copy.wait()


def fake_kernel(
    inside_ref,
    first_in,
    middle_in,
    last_ref,
    stats_ref,
    weight_in,
    cot_ref,
    real_terms_in,
    out_ref,
    low_out,
    high_out,
    terms_ref,
    first_ref,
    middle_ref,
    real_terms,
    weight_ref,
    sems,
    patch,
    wide_cot,
    wide_out,
    grad,
):
    middle_copy = fetch(middle_in, middle_ref, sems.at[4])
    first_copy = fetch(first_in, first_ref, sems.at[0])
    weight_copy = fetch(weight_in, weight_ref, sems.at[5])
    real_copy = fetch(real_terms_in, real_terms, sems.at[1])
    stats = stats_ref[...]
    slab = lax.broadcasted_iota(jnp.int32, (NDEV, 128), 0) // 2 % 32
    depths = jnp.where(slab == 0, 5.0, jnp.where(slab == 31, 3.0, 4.0))
    mean_row = jnp.sum(stats * depths, axis=0, keepdims=True) * (1.0 / (4.0 * NDEV))
    off = stats - mean_row
    between = as_column(jnp.sum(off * off * depths, axis=0, keepdims=True), 0)
    center = as_column(mean_row, 0)
    within = as_column(jnp.sum(stats, axis=0, keepdims=True), G)
    variance = (within + 4.0 * CELLS * between) * (1.0 / (16.0 * CELLS * NDEV))
    factor = as_column(stats[0:1, :], 2 * G) * lax.rsqrt(variance + 1e-05)
    shift = as_column(stats[0:1, :], 3 * G)
    lane = lanes((G, X))
    edge = jnp.zeros((128, X), BF16)
    for depth in (4, 5, 2, 3, 0, 1):
        if depth == 2:
            middle_copy.wait()
        elif depth == 0:
            first_copy.wait()
        before_ref = (first_ref, middle_ref, last_ref)[depth // 2]
        patch[depth * 512 : depth * 512 + 128, 0:X] = edge
        patch[depth * 512 + 384 : depth * 512 + 512, CELLS - X : CELLS] = edge
        for py in range(2):
            for px in range(2):
                block = (depth % 2 * 4 + py * 2 + px) * G
                for y in range(Y):
                    cells = before_ref[block : block + G, y * X : (y + 1) * X]
                    fake = jnp.maximum((cells - center) * factor + shift, 0.0)
                    if depth == 0:
                        fake = jnp.where(inside_ref[0] > 0, fake, 0.0)
                    if depth == 5:
                        fake = jnp.where(inside_ref[1] > 0, fake, 0.0)
                    if px == 1:
                        pieces = ((2, fake), (0, from_left(fake, lane)))
                    else:
                        pieces = ((1, fake), (3, from_right(fake, lane)))
                    for kx, piece in pieces:
                        piece = piece.astype(BF16)
                        for ky, to in ((2, y), (0, y + 1)) if py == 1 else ((1, y), (3, y - 1)):
                            if 0 <= to < Y:
                                at = depth * 512 + ky * 128 + kx * G
                                patch[at : at + G, to * X : (to + 1) * X] = piece
    weight_copy.wait()
    pre = convolve(weight_ref, patch)
    finish(pre, cot_ref, out_ref, wide_cot, wide_out, grad)
    edge_copies = [
        fetch(grad.at[2 * C : 3 * C], low_out, sems.at[2]),
        fetch(grad.at[C : 2 * C], high_out, sems.at[3]),
    ]
    planes = [patch[depth * 512 : (depth + 1) * 512, :] for depth in range(6)]
    real_copy.wait()
    for half, terms in enumerate(kernel_terms(planes, grad)):
        rows = slice(half * 512, (half + 1) * 512)
        terms_ref[rows, :] = terms + real_terms[rows, :]
    for copy in edge_copies:
        copy.wait()


def sum_kernel(parts_ref, prev_ref, first_ref, sums_ref):
    del prev_ref, first_ref
    total = jnp.sum(parts_ref[...].reshape(NDEV, 8, 128), axis=0, keepdims=True)
    sums_ref[...] = jnp.broadcast_to(total, (NDEV, 8, 128)).reshape(NDEV * 8, 128).astype(BF16)


def unpack_kernel(sums_ref, out, whole, sems):
    copies = []
    for part in range(4):
        rows = slice(part * 256, (part + 1) * 256)
        sums = sums_ref[rows, :].astype(F32)
        whole[0, rows, :] = sums[:, 0:C]
        whole[1, rows, :] = sums[:, C : 2 * C]
        for half in range(2):
            piece = pl.ds(part * 256, 256)
            copies.append(fetch(whole.at[half, piece], out.at[half, piece], sems.at[2 * part + half]))
    for copy in copies:
        copy.wait()


def weave_into(result, first_row, stride, wide_out):
    column = lanes((2 * X, 2 * X))
    source = lax.broadcasted_iota(jnp.int32, (2 * X, 2 * X), 0)
    weave = jnp.where(source == (column % 2) * X + column // 2, 1.0, 0.0).astype(BF16)
    for py in range(2):
        even = result[py * 64 : py * 64 + G, :]
        odd = result[py * 64 + G : py * 64 + 2 * G, :]
        both = jnp.concatenate(
            [
                jnp.concatenate([even[:, y * X : (y + 1) * X], odd[:, y * X : (y + 1) * X]], axis=1)
                for y in range(Y)
            ],
            axis=0,
        )
        woven = dot(both, weave)
        for y in range(Y):
            rows = pl.ds(first_row + 2 * y + py, G, stride=stride)
            wide_out[0, rows, :] = woven[y * G : (y + 1) * G, 0:X]
            wide_out[1, rows, :] = woven[y * G : (y + 1) * G, X : 2 * X]


def spread_edge(cells, depth, patch):
    lane = lanes((C, X))
    clear_rims(depth, patch)
    for y in range(Y):
        spread_cells(cells[:, y * X : (y + 1) * X].astype(F32), depth, y, lane, patch)


def pull_own_kernel(
    low_in,
    high_in,
    taps_in,
    wide_out,
    first_out,
    last_out,
    image_out,
    cells,
    taps,
    wide,
    first,
    last,
    patch,
    wide_rows,
    image,
    sems,
):
    edges = [fetch(ref, cells.at[i], sems.at[i]) for i, ref in enumerate((low_in, high_in))]
    taps_copy = fetch(taps_in, taps, sems.at[2])
    for depth in range(2):
        edges[depth].wait()
        spread_edge(cells[depth], depth, patch)
    taps_copy.wait()
    spread_weights(taps, wide)
    copies = [fetch(wide, wide_out, sems.at[3])]
    first[...] = dot(wide[1, 128:256, :], patch[0:576, :])
    copies.append(fetch(first, first_out, sems.at[4]))
    last[...] = dot(wide[0, 0:128, :], patch[576:1152, :])
    copies.append(fetch(last, last_out, sems.at[5]))
    middle = dot(wide[0], patch[0:576, :]) + dot(wide[1], patch[576:1152, :])
    middle = middle.astype(BF16)
    weave_into(middle[0:128, :], 0, 32, wide_rows)
    weave_into(middle[128:256, :], 16, 32, wide_rows)
    for half in range(2):
        image[:, :, half * X : (half + 1) * X] = wide_rows[half].reshape(G, 32, X).astype(BF16)
    copies.append(fetch(image, image_out.at[:, 16:48], sems.at[6]))
    for copy in copies:
        copy.wait()


def pull_outer_kernel(
    side, edge_in, wide_in, share_in, after_ref, image_in, image_out, cells, wide, share, patch, wide_rows, image, sems
):
    del after_ref, image_in
    edge_copy = fetch(edge_in, cells, sems.at[0])
    copies = [
        fetch(wide_in.at[side], wide, sems.at[1]),
        fetch(share_in, share, sems.at[2]),
    ]
    edge_copy.wait()
    spread_edge(cells, 0, patch)
    for copy in copies:
        copy.wait()
    rows = slice(128 - side * 128, 256 - side * 128)
    weave_into((share[...] + dot(wide[rows, :], patch[...])).astype(BF16), 0, 16, wide_rows)
    for half in range(2):
        image[:, :, half * X : (half + 1) * X] = wide_rows[half].reshape(G, 16, X).astype(BF16)
    fetch(image, image_out.at[:, pl.ds(side * 48, 16)], sems.at[3]).wait()


def call(body, name, args, outs, scratch, flops, mebibytes, smem=(), far=(), far_outs=(), aliases=()):
    moved = sum(a.size * a.dtype.itemsize for a in args) + sum(o.size * o.dtype.itemsize for o in outs)
    spaces = [
        pltpu.SMEM if i in smem else pl.ANY if i in far else pltpu.VMEM for i in range(len(args))
    ]
    out_spaces = [pltpu.HBM if i in far_outs else pltpu.VMEM for i in range(len(outs))]
    outs = [pltpu.HBM(o.shape, o.dtype) if i in far_outs else o for i, o in enumerate(outs)]
    args = [
        pltpu.with_memory_space_constraint(a, pltpu.HBM) if i in far else a for i, a in enumerate(args)
    ]
    return pl.pallas_call(
        body,
        name=name,
        out_shape=outs,
        in_specs=[pl.BlockSpec(memory_space=space) for space in spaces],
        out_specs=[pl.BlockSpec(memory_space=space) for space in out_spaces],
        scratch_shapes=scratch,
        input_output_aliases=dict(aliases),
        compiler_params=pltpu.CompilerParams(vmem_limit_bytes=mebibytes * 1024 * 1024),
        cost_estimate=pl.CostEstimate(flops=flops, bytes_accessed=moved, transcendentals=0),
    )(*args)


def to_next(edge):
    ends = lax.axis_size("slab") - 1
    return lax.ppermute(edge, "slab", [(i, i + 1) for i in range(ends)])


def to_prev(edge):
    ends = lax.axis_size("slab") - 1
    return lax.ppermute(edge, "slab", [(i + 1, i) for i in range(ends)])


def local(latent, g_weight, bn_gain, bn_shift, real_crops, d_weight, cot_fake, cot_real):
    shape = jax.ShapeDtypeStruct
    taps_g = g_weight.transpose(0, 1, 2, 4, 3).reshape(64 * G, C)
    taps_d = d_weight.reshape(64 * G, C)
    lat = latent[0]
    real = real_crops[0]
    at = lax.axis_index("slab")
    inside = jnp.stack([at > 0, at < lax.axis_size("slab") - 1]).astype(jnp.int32)
    (low,) = call(
        edge_kernel,
        "edges",
        (lat, real),
        [shape((1536, X), BF16)],
        [
            pltpu.VMEM((C, Y, X), BF16),
            pltpu.VMEM((G, 2 * Y, 2 * X), BF16),
            pltpu.SemaphoreType.DMA((2,)),
        ],
        0,
        4,
        far=(0, 1),
    )
    next_ = to_prev(low)
    wide, first, middle, last, sums, high, weight = call(
        own_kernel,
        "own_cells",
        (lat, real, taps_g, taps_d),
        [shape((2, 256, 576), BF16)]
        + [shape((256, CELLS), F32)] * 3
        + [shape((G, 128), F32), shape((1536, X), BF16), shape((C, 2048), BF16)],
        [
            pltpu.VMEM((C, Y, X), BF16),
            pltpu.VMEM((G, 2 * Y, 2 * X), BF16),
            pltpu.VMEM((C, 2, Y, X), BF16),
            pltpu.VMEM((2048, C), BF16),
            pltpu.VMEM((2048, C), BF16),
            pltpu.VMEM((C, 2048), BF16),
            pltpu.VMEM((2, 256, 576), BF16),
            pltpu.VMEM((256, CELLS), F32),
            pltpu.VMEM((256, CELLS), F32),
            pltpu.VMEM((256, CELLS), F32),
            pltpu.SemaphoreType.DMA((10,)),
            pltpu.VMEM((1152, CELLS), BF16),
            pltpu.VMEM((1024, X), F32),
        ],
        4 * 256 * 1152 * CELLS,
        16,
        far=(0, 1, 2, 3),
        far_outs=(0, 1, 2, 3, 6),
    )
    prev = to_next(high)
    last, stats, real_next = call(
        rim_kernel,
        "rim_cells",
        (inside, next_, sums, bn_gain.reshape(1, G), bn_shift.reshape(1, G), wide, last),
        [shape((256, CELLS), F32), shape((NDEV, 128), F32), shape((1024, X), BF16)],
        [
            pltpu.VMEM((576, CELLS), BF16),
            pltpu.VMEM((512, X), F32),
            pltpu.VMEM((256, 576), BF16),
            pltpu.VMEM((256, CELLS), F32),
            pltpu.VMEM((NDEV, 128), F32),
            pltpu.VMEM((1, G), F32),
            pltpu.VMEM((1, G), F32),
            pltpu.SemaphoreType.DMA((7,)),
        ],
        256 * 1152 * CELLS,
        12,
        smem=(0,),
        far=(3, 4, 5, 6),
        far_outs=(0, 1, 2),
    )
    stats = lax.all_to_all(stats, AXES, 0, 0, tiled=True)
    working = [
        pltpu.VMEM((C * 2 * Y, X), F32),
        pltpu.VMEM((C * 2 * Y, X), F32),
        pltpu.VMEM((4 * C, CELLS), BF16),
    ]
    d_real, real_terms, first = call(
        real_kernel,
        "real_branch",
        (
            real.reshape(G * 64, 2 * X),
            prev,
            real_next,
            weight,
            cot_real.reshape(C * 2 * Y, X),
            wide,
            first,
        ),
        [shape((C * 2 * Y, X), BF16), shape((1024, 2 * C), F32), shape((256, CELLS), F32)],
        [
            pltpu.VMEM((1024, X), BF16),
            pltpu.VMEM((C, 2048), BF16),
            pltpu.VMEM((256, 576), BF16),
            pltpu.VMEM((256, CELLS), F32),
            pltpu.VMEM((1024, 2 * C), F32),
            pltpu.SemaphoreType.DMA((6,)),
            pltpu.VMEM((6 * 512, CELLS), BF16),
            pltpu.VMEM((576, CELLS), BF16),
            pltpu.VMEM((2, 3072, X), F32),
            pltpu.VMEM((3072, 2 * X), BF16),
        ]
        + working,
        16 * 2048 * C * CELLS,
        26,
        far=(2, 3, 5, 6),
        far_outs=(1, 2),
    )
    d_fake, low, high, terms = call(
        fake_kernel,
        "fake_branch",
        (
            inside,
            first,
            middle,
            last,
            stats,
            weight,
            cot_fake.reshape(C * 2 * Y, X),
            real_terms,
        ),
        [
            shape((C * 2 * Y, X), BF16),
            shape((C, CELLS), BF16),
            shape((C, CELLS), BF16),
            shape((NDEV * 8, 128), F32),
        ],
        [
            pltpu.VMEM((256, CELLS), F32),
            pltpu.VMEM((256, CELLS), F32),
            pltpu.VMEM((NDEV * 8, 128), F32),
            pltpu.VMEM((C, 2048), BF16),
            pltpu.SemaphoreType.DMA((6,)),
            pltpu.VMEM((6 * 512, CELLS), BF16),
        ]
        + working,
        8 * 2048 * C * CELLS * 2,
        26,
        smem=(0,),
        far=(1, 2, 5, 7),
        far_outs=(1, 2),
    )
    parts = lax.all_to_all(terms.reshape(NDEV, 8, 128), AXES, 0, 0, tiled=True)
    grad_prev = to_next(high)
    grad_next = to_prev(low)
    pull_wide, pull_first, pull_last, image = call(
        pull_own_kernel,
        "pull_own",
        (low, high, taps_d),
        [
            shape((2, 256, 576), BF16),
            shape((128, CELLS), F32),
            shape((128, CELLS), F32),
            shape((G, 64, 2 * X), BF16),
        ],
        [
            pltpu.VMEM((2, C, CELLS), BF16),
            pltpu.VMEM((2048, C), BF16),
            pltpu.VMEM((2, 256, 576), BF16),
            pltpu.VMEM((128, CELLS), F32),
            pltpu.VMEM((128, CELLS), F32),
            pltpu.VMEM((1152, CELLS), BF16),
            pltpu.VMEM((2, G * 32, X), F32),
            pltpu.VMEM((G, 32, 2 * X), BF16),
            pltpu.SemaphoreType.DMA((7,)),
        ],
        2 * 384 * 1152 * CELLS,
        16,
        far=(0, 1, 2),
        far_outs=(0, 1, 2, 3),
    )
    (sums,) = call(
        sum_kernel,
        "sum_terms",
        (parts.reshape(NDEV * 8, 128), grad_prev, pull_first),
        [shape((NDEV * 8, 128), BF16)],
        [],
        NDEV * 1024,
        6,
        far=(1, 2),
    )
    whole = lax.all_to_all(sums.reshape(NDEV, 8, 128), AXES, 0, 0, tiled=True)
    for side, edge, share in ((0, grad_prev, pull_first), (1, grad_next, pull_last)):
        (image,) = call(
            functools.partial(pull_outer_kernel, side),
            "pull_prev" if side == 0 else "pull_next",
            (edge, pull_wide, share, sums, image),
            [shape((G, 64, 2 * X), BF16)],
            [
                pltpu.VMEM((C, CELLS), BF16),
                pltpu.VMEM((256, 576), BF16),
                pltpu.VMEM((128, CELLS), F32),
                pltpu.VMEM((576, CELLS), BF16),
                pltpu.VMEM((2, G * 16, X), F32),
                pltpu.VMEM((G, 16, 2 * X), BF16),
                pltpu.SemaphoreType.DMA((4,)),
            ],
            128 * 1152 * CELLS,
            12,
            far=(0, 1, 2, 3, 4) if side == 0 else (1, 2, 3, 4),
            far_outs=(0,),
            aliases=((4, 0),),
        )
    (weight_grad,) = call(
        unpack_kernel,
        "unpack",
        (whole.reshape(NDEV * 8, 128),),
        [shape((2, 1024, C), F32)],
        [pltpu.VMEM((2, 1024, C), F32), pltpu.SemaphoreType.DMA((8,))],
        0,
        6,
        far_outs=(0,),
    )
    return (
        d_fake.reshape(1, C, 2, Y, X),
        d_real.reshape(1, C, 2, Y, X),
        image.reshape(1, G, 4, 2 * Y, 2 * X),
        weight_grad.reshape(4, 4, 4, G, C),
    )


def solution(mesh):
    split = P(("section", "rep"), None, "slab", None, None)
    in_specs = (split, P(), P(), P(), split, P(), split, split)
    out_specs = (split, split, split, P())
    return jax.shard_map(local, mesh=mesh, in_specs=in_specs, out_specs=out_specs, check_vma=False)
```

```python
import jax
import jax.numpy as jnp
from jax import lax
from jax.experimental import pallas as pl
from jax.experimental.pallas import tpu as pltpu
from jax.sharding import PartitionSpec as P

AXES = ("section", "slab", "rep")
NDEV = 128
C = 64
G = 32
Y = 8
X = 128
CELLS = Y * X
F32 = jnp.float32
BF16 = jnp.bfloat16

phase_taps = (((1, 0), (3, -1)), ((0, 1), (2, 0)))


def dot(a, b, dims=(1, 0)):
    return lax.dot_general(a, b, (((dims[0],), (dims[1],)), ((), ())), preferred_element_type=F32)


def lanes(shape):
    return lax.broadcasted_iota(jnp.int32, shape, len(shape) - 1)


def from_left(tile, lane):
    return jnp.where(lane == 0, 0.0, pltpu.roll(tile, 1, 1))


def from_right(tile, lane):
    return jnp.where(lane == X - 1, 0.0, pltpu.roll(tile, X - 1, 1))


def spread_weights(taps_ref, wide_ref):
    wide_ref[...] = jnp.zeros_like(wide_ref)
    for pz in range(2):
        for py in range(2):
            for px in range(2):
                row = ((1 - pz) * 4 + py * 2 + px) * G
                for kz, oz in phase_taps[pz]:
                    tz = oz if pz == 1 else oz + 1
                    for ky, oy in phase_taps[py]:
                        for kx, ox in phase_taps[px]:
                            col = (oy + 1) * 192 + (ox + 1) * 64
                            tap = (kz * 16 + ky * 4 + kx) * G
                            wide_ref[tz, row : row + G, col : col + C] = taps_ref[tap : tap + G, :]


def spread_cells(tile, depth, y, lane, patch_ref):
    for xi, moved in ((0, from_left(tile, lane)), (1, tile), (2, from_right(tile, lane))):
        piece = moved.astype(BF16)
        for yi in range(3):
            to = y - (yi - 1)
            if 0 <= to < Y:
                row = depth * 576 + yi * 192 + xi * 64
                patch_ref[row : row + C, to * X : (to + 1) * X] = piece


def clear_rims(depth, patch_ref):
    edge = jnp.zeros((192, X), BF16)
    patch_ref[depth * 576 : depth * 576 + 192, 0:X] = edge
    patch_ref[depth * 576 + 384 : depth * 576 + 576, CELLS - X : CELLS] = edge


def fetch(source, target, sem):
    copy = pltpu.make_async_copy(source, target, sem)
    copy.start()
    return copy


def as_row(column, shift):
    sub = lax.broadcasted_iota(jnp.int32, (G, 128), 0)
    return jnp.sum(jnp.where(lanes((G, 128)) == sub + shift, column, 0.0), axis=0, keepdims=True)


def as_column(row, shift):
    shape = (G, row.shape[1])
    sub = lax.broadcasted_iota(jnp.int32, shape, 0)
    return jnp.sum(jnp.where(lanes(shape) == sub + shift, row, 0.0), axis=1, keepdims=True)


def edge_kernel(lat_in, real_in, edge_ref, lat_edge, real_edge, sems):
    copies = [
        fetch(lat_in.at[:, 0], lat_edge, sems.at[0]),
        fetch(real_in.at[:, 0], real_edge, sems.at[1]),
    ]
    join_edge(copies, lat_edge, real_edge, edge_ref)


def join_edge(copies, lat_edge, real_edge, edge_ref):
    copies[0].wait()
    edge_ref[0:512, :] = lat_edge[...].reshape(512, X)
    copies[1].wait()
    edge = real_edge[...].reshape(512, 2 * X)
    edge_ref[512:1024, :] = edge[:, 0:X]
    edge_ref[1024:1536, :] = edge[:, X : 2 * X]


def cell_stats(ref, first, count):
    blocks = range(first, first + count)
    total = jnp.zeros((G, CELLS), F32)
    for block in blocks:
        total += ref[block * G : (block + 1) * G, :]
    mean = jnp.sum(total, axis=1, keepdims=True) * (1.0 / (count * CELLS))
    squares = jnp.zeros((G, CELLS), F32)
    for block in blocks:
        off = ref[block * G : (block + 1) * G, :] - mean
        squares += off * off
    return mean, jnp.sum(squares, axis=1, keepdims=True)


def own_kernel(
    lat_in,
    real_in,
    taps_in,
    taps_d_in,
    wide_out,
    first_out,
    middle_out,
    last_out,
    sums_ref,
    edge_ref,
    weight_out,
    lat_edge,
    real_edge,
    lat,
    taps,
    taps_d,
    weight,
    wide,
    first,
    middle,
    last,
    sems,
    patch,
    wide_lat,
):
    edge_copies = [
        fetch(lat_in.at[:, 1], lat_edge, sems.at[0]),
        fetch(real_in.at[:, 3], real_edge, sems.at[1]),
    ]
    lat_copy = fetch(lat_in, lat, sems.at[2])
    taps_copy = fetch(taps_in, taps, sems.at[3])
    taps_d_copy = fetch(taps_d_in, taps_d, sems.at[4])
    lat_copy.wait()
    wide_lat[...] = lat[...].reshape(1024, X).astype(F32)
    lane = lanes((C, X))
    for depth in range(2):
        clear_rims(depth, patch)
        for y in range(Y):
            spread_cells(wide_lat[pl.ds(depth * Y + y, C, stride=16), :], depth, y, lane, patch)
    taps_copy.wait()
    spread_weights(taps, wide)
    copies = [fetch(wide, wide_out, sems.at[5])]
    last[...] = dot(wide[0], patch[576:1152, :])
    copies.append(fetch(last, last_out, sems.at[6]))
    middle[...] = dot(wide[0], patch[0:576, :]) + dot(wide[1], patch[576:1152, :])
    copies.append(fetch(middle, middle_out, sems.at[7]))
    first[...] = dot(wide[1], patch[0:576, :])
    copies.append(fetch(first, first_out, sems.at[8]))
    taps_d_copy.wait()
    same = lax.broadcasted_iota(jnp.int32, (C, C), 0) == lanes((C, C))
    unit = jnp.where(same, 1.0, 0.0).astype(BF16)
    weight[...] = dot(unit, taps_d[...], (1, 1)).astype(BF16)
    copies.append(fetch(weight, weight_out, sems.at[9]))
    join_edge(edge_copies, lat_edge, real_edge, edge_ref)
    place = lanes((G, 128))
    sums = jnp.zeros((G, 128), F32)
    for at, column in enumerate(cell_stats(middle, 0, 8) + cell_stats(first, 4, 4)):
        sums = jnp.where(place == at, column, sums)
    sums_ref[...] = sums
    for copy in copies:
        copy.wait()


def rim_kernel(
    inside_ref,
    next_ref,
    sums_ref,
    gain_in,
    shift_in,
    wide_in,
    last_in,
    last_out,
    stats_out,
    real_next_out,
    patch,
    wide_lat,
    wide,
    last,
    stats,
    gain,
    shift,
    sems,
):
    wide_copy = fetch(wide_in.at[1], wide, sems.at[0])
    last_copy = fetch(last_in, last, sems.at[1])
    affine_copies = [fetch(gain_in, gain, sems.at[5]), fetch(shift_in, shift, sems.at[6])]
    copies = [fetch(next_ref.at[512:1536], real_next_out, sems.at[2])]
    wide_lat[...] = next_ref[0:512, :].astype(F32)
    lane = lanes((C, X))
    clear_rims(0, patch)
    for y in range(Y):
        spread_cells(wide_lat[pl.ds(y, C, stride=8), :], 0, y, lane, patch)
    wide_copy.wait()
    added = dot(wide[...], patch[...])
    last_copy.wait()
    last[...] += added
    copies.append(fetch(last, last_out, sems.at[3]))
    groups = [(2.0, sums_ref[:, 0:1], sums_ref[:, 1:2])]
    groups.append((jnp.where(inside_ref[0] > 0, 0.0, 1.0), sums_ref[:, 2:3], sums_ref[:, 3:4]))
    groups.append((1.0,) + cell_stats(last, 0, 4))
    groups.append((jnp.where(inside_ref[1] > 0, 1.0, 0.0),) + cell_stats(last, 4, 4))
    depths = jnp.zeros((G, 1), F32)
    mean = jnp.zeros((G, 1), F32)
    for weight, one, _ in groups:
        depths += weight
        mean += weight * one
    mean /= depths
    spread = jnp.zeros((G, 1), F32)
    for weight, one, squares in groups:
        own = squares if isinstance(weight, float) else weight * squares
        spread += own + weight * (4.0 * CELLS) * (one - mean) * (one - mean)
    row = as_row(mean, 0) + as_row(spread, G)
    for copy in affine_copies:
        copy.wait()
    row += as_row(as_column(gain[...], 0), 2 * G) + as_row(as_column(shift[...], 0), 3 * G)
    stats[...] = jnp.broadcast_to(row, (NDEV, 128))
    copies.append(fetch(stats, stats_out, sems.at[4]))
    for copy in copies:
        copy.wait()


def activate(before):
    squashed = jax.nn.sigmoid(4.0 * before)
    output = before * (0.2 + 0.8 * squashed)
    derivative = 0.2 + 0.8 * squashed + 3.2 * before * squashed * (1.0 - squashed)
    return (output, derivative)


def convolve(weight_ref, patch):
    early = weight_ref[:, 0:1024]
    late = weight_ref[:, 1024:2048]
    shared = dot(jnp.concatenate([late, early], axis=0), patch[1024:2048, :])
    return (
        dot(early, patch[0:1024, :]) + shared[0:C, :],
        shared[C : 2 * C, :] + dot(late, patch[2048:3072, :]),
    )


def finish(pre, cot_ref, out, wide_cot, wide_out, grad):
    wide_cot[...] = cot_ref[...].astype(F32)
    nothing = jnp.zeros((C, CELLS), BF16)
    grad[0:C, :] = nothing
    grad[3 * C : 4 * C, :] = nothing
    for m in range(2):
        for y in range(Y):
            output, slope = activate(pre[m][:, y * X : (y + 1) * X])
            wide_out[pl.ds(m * Y + y, C, stride=16), :] = output
            cot = wide_cot[pl.ds(m * Y + y, C, stride=16), :]
            grad[(2 - m) * C : (3 - m) * C, y * X : (y + 1) * X] = (cot * slope).astype(BF16)
    out[...] = wide_out[...].astype(BF16)


def kernel_terms(planes, grad):
    for half in range(2):
        terms = dot(planes[half], grad[128:256, :], (1, 1))
        terms += dot(planes[half + 2], grad[64:192, :], (1, 1))
        yield terms + dot(planes[half + 4], grad[0:128, :], (1, 1))


def split_depth(at, places, halves, rows, patch):
    base, stride = places
    column = lanes((2 * X, 4 * X))
    source = lax.broadcasted_iota(jnp.int32, (2 * X, 4 * X), 0)
    pick = jnp.where(source == 2 * (column % X) + column // X - 1, 1.0, 0.0).astype(BF16)
    edge = jnp.zeros((128, X), BF16)
    patch[at : at + 128, 0:X] = edge
    patch[at + 384 : at + 512, CELLS - X : CELLS] = edge
    for row in range(2 * Y):
        for half in range(2):
            cells = halves[half, pl.ds(base + row, G, stride=stride), :].astype(BF16)
            rows[at + row * G : at + (row + 1) * G, half * X : (half + 1) * X] = cells
    split = dot(rows[at : at + 512, :], pick).astype(BF16)
    for row in range(2 * Y):
        for kx in range(4):
            piece = split[row * G : (row + 1) * G, kx * X : (kx + 1) * X]
            for ky in range(4):
                if (row + 1 - ky) % 2 == 0 and 0 <= (row + 1 - ky) // 2 < Y:
                    y = (row + 1 - ky) // 2
                    place = at + ky * 128 + kx * G
                    patch[place : place + G, y * X : (y + 1) * X] = piece


def real_kernel(
    real_ref,
    prev_ref,
    next_in,
    weight_in,
    cot_ref,
    wide_in,
    first_in,
    out_out,
    terms_out,
    first_out,
    out,
    edge,
    weight,
    wide,
    first,
    terms_ref,
    sems,
    patch,
    lat_patch,
    halves,
    rows,
    wide_cot,
    wide_out,
    grad,
):
    edge_copy = fetch(next_in, edge, sems.at[0])
    for half in range(2):
        part = slice(512 + half * 512, 1024 + half * 512)
        halves[half, 0:2048, :] = real_ref[:, half * X : (half + 1) * X].astype(F32)
        halves[half, 2048:2560, :] = prev_ref[part, :].astype(F32)
    places = ((2048, 16), (0, 64), (16, 64), (32, 64), (48, 64), (2560, 16))
    for depth in range(2):
        split_depth(depth * 512, places[depth], halves, rows, patch)
    edge_copy.wait()
    copies = [
        fetch(weight_in, weight, sems.at[1]),
        fetch(wide_in.at[0], wide, sems.at[2]),
        fetch(first_in, first, sems.at[3]),
    ]
    for half in range(2):
        halves[half, 2560:3072, :] = edge[half * 512 : (half + 1) * 512, :].astype(F32)
    for depth in range(2, 6):
        split_depth(depth * 512, places[depth], halves, rows, patch)
    halves[0, 0:512, :] = prev_ref[0:512, :].astype(F32)
    lane = lanes((C, X))
    clear_rims(0, lat_patch)
    for y in range(Y):
        spread_cells(halves[0, pl.ds(y, C, stride=8), :], 0, y, lane, lat_patch)
    for copy in copies:
        copy.wait()
    first[...] += dot(wide[...], lat_patch[...])
    first_copy = fetch(first, first_out, sems.at[4])
    finish(convolve(weight, patch), cot_ref, out, wide_cot, wide_out, grad)
    stores = [first_copy, fetch(out, out_out, sems.at[5])]
    planes = [patch[depth * 512 : (depth + 1) * 512, :] for depth in range(6)]
    for half, terms in enumerate(kernel_terms(planes, grad)):
        terms_ref[half * 512 : (half + 1) * 512, :] = terms
        piece = pl.ds(half * 512, 512)
        stores.append(fetch(terms_ref.at[piece], terms_out.at[piece], sems.at[6 + half]))
    for store in stores:
        store.wait()


def fake_kernel(
    inside_ref,
    first_in,
    middle_in,
    last_ref,
    stats_ref,
    weight_in,
    cot_ref,
    real_terms_in,
    out_out,
    low_out,
    high_out,
    terms_out,
    out,
    terms_ref,
    first_ref,
    middle_ref,
    real_terms,
    weight_ref,
    sems,
    patch,
    wide_cot,
    wide_out,
    grad,
):
    middle_copy = fetch(middle_in, middle_ref, sems.at[4])
    first_copy = fetch(first_in, first_ref, sems.at[0])
    weight_copy = fetch(weight_in, weight_ref, sems.at[5])
    real_copy = fetch(real_terms_in, real_terms, sems.at[1])
    stats = stats_ref[...]
    slab = lax.broadcasted_iota(jnp.int32, (NDEV, 128), 0) // 2 % 32
    depths = jnp.where(slab == 0, 5.0, jnp.where(slab == 31, 3.0, 4.0))
    mean_row = jnp.sum(stats * depths, axis=0, keepdims=True) * (1.0 / (4.0 * NDEV))
    off = stats - mean_row
    between = as_column(jnp.sum(off * off * depths, axis=0, keepdims=True), 0)
    center = as_column(mean_row, 0)
    within = as_column(jnp.sum(stats, axis=0, keepdims=True), G)
    variance = (within + 4.0 * CELLS * between) * (1.0 / (16.0 * CELLS * NDEV))
    factor = as_column(stats[0:1, :], 2 * G) * lax.rsqrt(variance + 1e-05)
    shift = as_column(stats[0:1, :], 3 * G)
    lane = lanes((G, X))
    edge = jnp.zeros((128, X), BF16)
    for depth in (4, 5, 2, 3, 0, 1):
        if depth == 2:
            middle_copy.wait()
        elif depth == 0:
            first_copy.wait()
        before_ref = (first_ref, middle_ref, last_ref)[depth // 2]
        patch[depth * 512 : depth * 512 + 128, 0:X] = edge
        patch[depth * 512 + 384 : depth * 512 + 512, CELLS - X : CELLS] = edge
        for py in range(2):
            for px in range(2):
                block = (depth % 2 * 4 + py * 2 + px) * G
                for y in range(Y):
                    cells = before_ref[block : block + G, y * X : (y + 1) * X]
                    fake = jnp.maximum((cells - center) * factor + shift, 0.0)
                    if depth == 0:
                        fake = jnp.where(inside_ref[0] > 0, fake, 0.0)
                    if depth == 5:
                        fake = jnp.where(inside_ref[1] > 0, fake, 0.0)
                    if px == 1:
                        pieces = ((2, fake), (0, from_left(fake, lane)))
                    else:
                        pieces = ((1, fake), (3, from_right(fake, lane)))
                    for kx, piece in pieces:
                        piece = piece.astype(BF16)
                        for ky, to in ((2, y), (0, y + 1)) if py == 1 else ((1, y), (3, y - 1)):
                            if 0 <= to < Y:
                                at = depth * 512 + ky * 128 + kx * G
                                patch[at : at + G, to * X : (to + 1) * X] = piece
    weight_copy.wait()
    pre = convolve(weight_ref, patch)
    finish(pre, cot_ref, out, wide_cot, wide_out, grad)
    stores = [
        fetch(out, out_out, sems.at[6]),
        fetch(grad.at[2 * C : 3 * C], low_out, sems.at[2]),
        fetch(grad.at[C : 2 * C], high_out, sems.at[3]),
    ]
    planes = [patch[depth * 512 : (depth + 1) * 512, :] for depth in range(6)]
    real_copy.wait()
    for half, terms in enumerate(kernel_terms(planes, grad)):
        rows = slice(half * 512, (half + 1) * 512)
        terms_ref[rows, :] = terms + real_terms[rows, :]
        piece = pl.ds(half * 512, 512)
        stores.append(fetch(terms_ref.at[piece], terms_out.at[piece], sems.at[7 + half]))
    for store in stores:
        store.wait()


def sum_kernel(parts_ref, prev_ref, first_ref, sums_ref):
    del prev_ref, first_ref
    total = jnp.sum(parts_ref[...].reshape(NDEV, 8, 128), axis=0, keepdims=True)
    sums_ref[...] = jnp.broadcast_to(total, (NDEV, 8, 128)).reshape(NDEV * 8, 128).astype(BF16)


def unpack_kernel(sums_ref, out, whole, sems):
    copies = []
    for part in range(4):
        rows = slice(part * 256, (part + 1) * 256)
        sums = sums_ref[rows, :].astype(F32)
        whole[0, rows, :] = sums[:, 0:C]
        whole[1, rows, :] = sums[:, C : 2 * C]
        for half in range(2):
            piece = pl.ds(part * 256, 256)
            copies.append(fetch(whole.at[half, piece], out.at[half, piece], sems.at[2 * part + half]))
    for copy in copies:
        copy.wait()


def weave_into(result, first_row, stride, wide_out):
    column = lanes((2 * X, 2 * X))
    source = lax.broadcasted_iota(jnp.int32, (2 * X, 2 * X), 0)
    weave = jnp.where(source == (column % 2) * X + column // 2, 1.0, 0.0).astype(BF16)
    for py in range(2):
        even = result[py * 64 : py * 64 + G, :]
        odd = result[py * 64 + G : py * 64 + 2 * G, :]
        both = jnp.concatenate(
            [
                jnp.concatenate([even[:, y * X : (y + 1) * X], odd[:, y * X : (y + 1) * X]], axis=1)
                for y in range(Y)
            ],
            axis=0,
        )
        woven = dot(both, weave)
        for y in range(Y):
            rows = pl.ds(first_row + 2 * y + py, G, stride=stride)
            wide_out[0, rows, :] = woven[y * G : (y + 1) * G, 0:X]
            wide_out[1, rows, :] = woven[y * G : (y + 1) * G, X : 2 * X]


def spread_edge(cells, depth, patch):
    lane = lanes((C, X))
    clear_rims(depth, patch)
    for y in range(Y):
        spread_cells(cells[:, y * X : (y + 1) * X].astype(F32), depth, y, lane, patch)


def pull_own_kernel(
    low_in,
    high_in,
    taps_in,
    wide_out,
    first_out,
    last_out,
    image_out,
    cells,
    taps,
    wide,
    first,
    last,
    patch,
    wide_rows,
    image,
    sems,
):
    edges = [fetch(ref, cells.at[i], sems.at[i]) for i, ref in enumerate((low_in, high_in))]
    taps_copy = fetch(taps_in, taps, sems.at[2])
    for depth in range(2):
        edges[depth].wait()
        spread_edge(cells[depth], depth, patch)
    taps_copy.wait()
    spread_weights(taps, wide)
    copies = [fetch(wide, wide_out, sems.at[3])]
    first[...] = dot(wide[1, 128:256, :], patch[0:576, :])
    copies.append(fetch(first, first_out, sems.at[4]))
    last[...] = dot(wide[0, 0:128, :], patch[576:1152, :])
    copies.append(fetch(last, last_out, sems.at[5]))
    middle = dot(wide[0], patch[0:576, :]) + dot(wide[1], patch[576:1152, :])
    middle = middle.astype(BF16)
    weave_into(middle[0:128, :], 0, 32, wide_rows)
    weave_into(middle[128:256, :], 16, 32, wide_rows)
    for half in range(2):
        image[:, :, half * X : (half + 1) * X] = wide_rows[half].reshape(G, 32, X).astype(BF16)
    copies.append(fetch(image, image_out.at[:, 16:48], sems.at[6]))
    for copy in copies:
        copy.wait()


def add_edge(side, cells, wide, share, image_out, patch, wide_rows, image, sem):
    spread_edge(cells, 0, patch)
    rows = slice(128 - side * 128, 256 - side * 128)
    weave_into((share[...] + dot(wide[rows, :], patch[...])).astype(BF16), 0, 16, wide_rows)
    for half in range(2):
        image[:, :, half * X : (half + 1) * X] = wide_rows[half].reshape(G, 16, X).astype(BF16)
    return fetch(image, image_out.at[:, pl.ds(side * 48, 16)], sem)


def pull_prev_kernel(
    edge_in,
    wide_in,
    first_in,
    last_in,
    sums_ref,
    image_in,
    image_out,
    wide_next,
    last_ref,
    cells,
    wide,
    share,
    patch,
    wide_rows,
    image,
    sems,
):
    del sums_ref, image_in
    copies = [
        fetch(edge_in, cells, sems.at[0]),
        fetch(wide_in.at[0], wide, sems.at[1]),
        fetch(first_in, share, sems.at[2]),
    ]
    later = [
        fetch(wide_in.at[1], wide_next, sems.at[3]),
        fetch(last_in, last_ref, sems.at[4]),
    ]
    for copy in copies:
        copy.wait()
    later.append(add_edge(0, cells, wide, share, image_out, patch, wide_rows, image, sems.at[5]))
    for copy in later:
        copy.wait()


def pull_next_kernel(
    edge_ref, wide_ref, last_ref, image_in, image_out, patch, wide_rows, image, sem
):
    del image_in
    add_edge(1, edge_ref, wide_ref, last_ref, image_out, patch, wide_rows, image, sem).wait()


def call(body, name, args, outs, scratch, flops, mebibytes, smem=(), far=(), far_outs=(), aliases=()):
    moved = sum(a.size * a.dtype.itemsize for a in args) + sum(o.size * o.dtype.itemsize for o in outs)
    spaces = [
        pltpu.SMEM if i in smem else pl.ANY if i in far else pltpu.VMEM for i in range(len(args))
    ]
    out_spaces = [pltpu.HBM if i in far_outs else pltpu.VMEM for i in range(len(outs))]
    outs = [pltpu.HBM(o.shape, o.dtype) if i in far_outs else o for i, o in enumerate(outs)]
    args = [
        pltpu.with_memory_space_constraint(a, pltpu.HBM) if i in far else a for i, a in enumerate(args)
    ]
    return pl.pallas_call(
        body,
        name=name,
        out_shape=outs,
        in_specs=[pl.BlockSpec(memory_space=space) for space in spaces],
        out_specs=[pl.BlockSpec(memory_space=space) for space in out_spaces],
        scratch_shapes=scratch,
        input_output_aliases=dict(aliases),
        compiler_params=pltpu.CompilerParams(vmem_limit_bytes=mebibytes * 1024 * 1024),
        cost_estimate=pl.CostEstimate(flops=flops, bytes_accessed=moved, transcendentals=0),
    )(*args)


def to_next(edge):
    ends = lax.axis_size("slab") - 1
    return lax.ppermute(edge, "slab", [(i, i + 1) for i in range(ends)])


def to_prev(edge):
    ends = lax.axis_size("slab") - 1
    return lax.ppermute(edge, "slab", [(i + 1, i) for i in range(ends)])


def local(latent, g_weight, bn_gain, bn_shift, real_crops, d_weight, cot_fake, cot_real):
    shape = jax.ShapeDtypeStruct
    taps_g = g_weight.transpose(0, 1, 2, 4, 3).reshape(64 * G, C)
    taps_d = d_weight.reshape(64 * G, C)
    lat = latent[0]
    real = real_crops[0]
    at = lax.axis_index("slab")
    inside = jnp.stack([at > 0, at < lax.axis_size("slab") - 1]).astype(jnp.int32)
    (low,) = call(
        edge_kernel,
        "edges",
        (lat, real),
        [shape((1536, X), BF16)],
        [
            pltpu.VMEM((C, Y, X), BF16),
            pltpu.VMEM((G, 2 * Y, 2 * X), BF16),
            pltpu.SemaphoreType.DMA((2,)),
        ],
        0,
        4,
        far=(0, 1),
    )
    next_ = to_prev(low)
    wide, first, middle, last, sums, high, weight = call(
        own_kernel,
        "own_cells",
        (lat, real, taps_g, taps_d),
        [shape((2, 256, 576), BF16)]
        + [shape((256, CELLS), F32)] * 3
        + [shape((G, 128), F32), shape((1536, X), BF16), shape((C, 2048), BF16)],
        [
            pltpu.VMEM((C, Y, X), BF16),
            pltpu.VMEM((G, 2 * Y, 2 * X), BF16),
            pltpu.VMEM((C, 2, Y, X), BF16),
            pltpu.VMEM((2048, C), BF16),
            pltpu.VMEM((2048, C), BF16),
            pltpu.VMEM((C, 2048), BF16),
            pltpu.VMEM((2, 256, 576), BF16),
            pltpu.VMEM((256, CELLS), F32),
            pltpu.VMEM((256, CELLS), F32),
            pltpu.VMEM((256, CELLS), F32),
            pltpu.SemaphoreType.DMA((10,)),
            pltpu.VMEM((1152, CELLS), BF16),
            pltpu.VMEM((1024, X), F32),
        ],
        4 * 256 * 1152 * CELLS,
        16,
        far=(0, 1, 2, 3),
        far_outs=(0, 1, 2, 3, 6),
    )
    prev = to_next(high)
    last, stats, real_next = call(
        rim_kernel,
        "rim_cells",
        (inside, next_, sums, bn_gain.reshape(1, G), bn_shift.reshape(1, G), wide, last),
        [shape((256, CELLS), F32), shape((NDEV, 128), F32), shape((1024, X), BF16)],
        [
            pltpu.VMEM((576, CELLS), BF16),
            pltpu.VMEM((512, X), F32),
            pltpu.VMEM((256, 576), BF16),
            pltpu.VMEM((256, CELLS), F32),
            pltpu.VMEM((NDEV, 128), F32),
            pltpu.VMEM((1, G), F32),
            pltpu.VMEM((1, G), F32),
            pltpu.SemaphoreType.DMA((7,)),
        ],
        256 * 1152 * CELLS,
        12,
        smem=(0,),
        far=(3, 4, 5, 6),
        far_outs=(0, 1, 2),
    )
    stats = lax.all_to_all(stats, AXES, 0, 0, tiled=True)
    working = [
        pltpu.VMEM((C * 2 * Y, X), F32),
        pltpu.VMEM((C * 2 * Y, X), F32),
        pltpu.VMEM((4 * C, CELLS), BF16),
    ]
    d_real, real_terms, first = call(
        real_kernel,
        "real_branch",
        (
            real.reshape(G * 64, 2 * X),
            prev,
            real_next,
            weight,
            cot_real.reshape(C * 2 * Y, X),
            wide,
            first,
        ),
        [shape((C * 2 * Y, X), BF16), shape((1024, 2 * C), F32), shape((256, CELLS), F32)],
        [
            pltpu.VMEM((C * 2 * Y, X), BF16),
            pltpu.VMEM((1024, X), BF16),
            pltpu.VMEM((C, 2048), BF16),
            pltpu.VMEM((256, 576), BF16),
            pltpu.VMEM((256, CELLS), F32),
            pltpu.VMEM((1024, 2 * C), F32),
            pltpu.SemaphoreType.DMA((8,)),
            pltpu.VMEM((6 * 512, CELLS), BF16),
            pltpu.VMEM((576, CELLS), BF16),
            pltpu.VMEM((2, 3072, X), F32),
            pltpu.VMEM((3072, 2 * X), BF16),
        ]
        + working,
        16 * 2048 * C * CELLS,
        26,
        far=(2, 3, 5, 6),
        far_outs=(0, 1, 2),
    )
    d_fake, low, high, terms = call(
        fake_kernel,
        "fake_branch",
        (
            inside,
            first,
            middle,
            last,
            stats,
            weight,
            cot_fake.reshape(C * 2 * Y, X),
            real_terms,
        ),
        [
            shape((C * 2 * Y, X), BF16),
            shape((C, CELLS), BF16),
            shape((C, CELLS), BF16),
            shape((NDEV * 8, 128), F32),
        ],
        [
            pltpu.VMEM((C * 2 * Y, X), BF16),
            pltpu.VMEM((NDEV * 8, 128), F32),
            pltpu.VMEM((256, CELLS), F32),
            pltpu.VMEM((256, CELLS), F32),
            pltpu.VMEM((NDEV * 8, 128), F32),
            pltpu.VMEM((C, 2048), BF16),
            pltpu.SemaphoreType.DMA((9,)),
            pltpu.VMEM((6 * 512, CELLS), BF16),
        ]
        + working,
        8 * 2048 * C * CELLS * 2,
        26,
        smem=(0,),
        far=(1, 2, 5, 7),
        far_outs=(0, 1, 2, 3),
    )
    parts = lax.all_to_all(terms.reshape(NDEV, 8, 128), AXES, 0, 0, tiled=True)
    grad_prev = to_next(high)
    grad_next = to_prev(low)
    pull_wide, pull_first, pull_last, image = call(
        pull_own_kernel,
        "pull_own",
        (low, high, taps_d),
        [
            shape((2, 256, 576), BF16),
            shape((128, CELLS), F32),
            shape((128, CELLS), F32),
            shape((G, 64, 2 * X), BF16),
        ],
        [
            pltpu.VMEM((2, C, CELLS), BF16),
            pltpu.VMEM((2048, C), BF16),
            pltpu.VMEM((2, 256, 576), BF16),
            pltpu.VMEM((128, CELLS), F32),
            pltpu.VMEM((128, CELLS), F32),
            pltpu.VMEM((1152, CELLS), BF16),
            pltpu.VMEM((2, G * 32, X), F32),
            pltpu.VMEM((G, 32, 2 * X), BF16),
            pltpu.SemaphoreType.DMA((7,)),
        ],
        2 * 384 * 1152 * CELLS,
        16,
        far=(0, 1, 2),
        far_outs=(0, 1, 2, 3),
    )
    (sums,) = call(
        sum_kernel,
        "sum_terms",
        (parts.reshape(NDEV * 8, 128), grad_prev, pull_first),
        [shape((NDEV * 8, 128), BF16)],
        [],
        NDEV * 1024,
        6,
        far=(1, 2),
    )
    whole = lax.all_to_all(sums.reshape(NDEV, 8, 128), AXES, 0, 0, tiled=True)
    outer = [
        pltpu.VMEM((576, CELLS), BF16),
        pltpu.VMEM((2, G * 16, X), F32),
        pltpu.VMEM((G, 16, 2 * X), BF16),
    ]
    image, wide_next, last_share = call(
        pull_prev_kernel,
        "pull_prev",
        (grad_prev, pull_wide, pull_first, pull_last, sums, image),
        [shape((G, 64, 2 * X), BF16), shape((256, 576), BF16), shape((128, CELLS), F32)],
        [
            pltpu.VMEM((C, CELLS), BF16),
            pltpu.VMEM((256, 576), BF16),
            pltpu.VMEM((128, CELLS), F32),
        ]
        + outer
        + [pltpu.SemaphoreType.DMA((6,))],
        128 * 1152 * CELLS,
        12,
        far=(0, 1, 2, 3, 4, 5),
        far_outs=(0,),
        aliases=((5, 0),),
    )
    (image,) = call(
        pull_next_kernel,
        "pull_next",
        (grad_next, wide_next, last_share, image),
        [shape((G, 64, 2 * X), BF16)],
        outer + [pltpu.SemaphoreType.DMA],
        128 * 1152 * CELLS,
        12,
        far=(3,),
        far_outs=(0,),
        aliases=((3, 0),),
    )
    (weight_grad,) = call(
        unpack_kernel,
        "unpack",
        (whole.reshape(NDEV * 8, 128),),
        [shape((2, 1024, C), F32)],
        [pltpu.VMEM((2, 1024, C), F32), pltpu.SemaphoreType.DMA((8,))],
        0,
        6,
        far_outs=(0,),
    )
    return (
        d_fake.reshape(1, C, 2, Y, X),
        d_real.reshape(1, C, 2, Y, X),
        image.reshape(1, G, 4, 2 * Y, 2 * X),
        weight_grad.reshape(4, 4, 4, G, C),
    )


def solution(mesh):
    split = P(("section", "rep"), None, "slab", None, None)
    in_specs = (split, P(), P(), P(), split, P(), split, split)
    out_specs = (split, split, split, P())
    return jax.shard_map(local, mesh=mesh, in_specs=in_specs, out_specs=out_specs, check_vma=False)
```

```python
import jax
import jax.numpy as jnp
from jax import lax
from jax.experimental import pallas as pl
from jax.experimental.pallas import tpu as pltpu
from jax.sharding import PartitionSpec as P

AXES = ("section", "slab", "rep")
NDEV = 128
C = 64
G = 32
Y = 8
X = 128
CELLS = Y * X
F32 = jnp.float32
BF16 = jnp.bfloat16

phase_taps = (((1, 0), (3, -1)), ((0, 1), (2, 0)))


def dot(a, b, dims=(1, 0)):
    return lax.dot_general(a, b, (((dims[0],), (dims[1],)), ((), ())), preferred_element_type=F32)


def lanes(shape):
    return lax.broadcasted_iota(jnp.int32, shape, len(shape) - 1)


def from_left(tile, lane):
    return jnp.where(lane == 0, 0.0, pltpu.roll(tile, 1, 1))


def from_right(tile, lane):
    return jnp.where(lane == X - 1, 0.0, pltpu.roll(tile, X - 1, 1))


def spread_weights(taps_ref, wide_ref):
    wide_ref[...] = jnp.zeros_like(wide_ref)
    for pz in range(2):
        for py in range(2):
            for px in range(2):
                row = ((1 - pz) * 4 + py * 2 + px) * G
                for kz, oz in phase_taps[pz]:
                    tz = oz if pz == 1 else oz + 1
                    for ky, oy in phase_taps[py]:
                        for kx, ox in phase_taps[px]:
                            col = (oy + 1) * 192 + (ox + 1) * 64
                            tap = (kz * 16 + ky * 4 + kx) * G
                            wide_ref[tz, row : row + G, col : col + C] = taps_ref[tap : tap + G, :]


def spread_cells(tile, depth, y, lane, patch_ref):
    for xi, moved in ((0, from_left(tile, lane)), (1, tile), (2, from_right(tile, lane))):
        piece = moved.astype(BF16)
        for yi in range(3):
            to = y - (yi - 1)
            if 0 <= to < Y:
                row = depth * 576 + yi * 192 + xi * 64
                patch_ref[row : row + C, to * X : (to + 1) * X] = piece


def clear_rims(depth, patch_ref):
    edge = jnp.zeros((192, X), BF16)
    patch_ref[depth * 576 : depth * 576 + 192, 0:X] = edge
    patch_ref[depth * 576 + 384 : depth * 576 + 576, CELLS - X : CELLS] = edge


def fetch(source, target, sem):
    copy = pltpu.make_async_copy(source, target, sem)
    copy.start()
    return copy


def as_row(column, shift):
    sub = lax.broadcasted_iota(jnp.int32, (G, 128), 0)
    return jnp.sum(jnp.where(lanes((G, 128)) == sub + shift, column, 0.0), axis=0, keepdims=True)


def as_column(row, shift):
    shape = (G, row.shape[1])
    sub = lax.broadcasted_iota(jnp.int32, shape, 0)
    return jnp.sum(jnp.where(lanes(shape) == sub + shift, row, 0.0), axis=1, keepdims=True)


def edge_kernel(lat_in, real_in, edge_ref, lat_edge, real_edge, sems):
    copies = [
        fetch(lat_in.at[:, 0], lat_edge, sems.at[0]),
        fetch(real_in.at[:, 0], real_edge, sems.at[1]),
    ]
    join_edge(copies, lat_edge, real_edge, edge_ref)


def join_edge(copies, lat_edge, real_edge, edge_ref):
    copies[0].wait()
    edge_ref[0:512, :] = lat_edge[...].reshape(512, X)
    copies[1].wait()
    edge = real_edge[...].reshape(512, 2 * X)
    edge_ref[512:1024, :] = edge[:, 0:X]
    edge_ref[1024:1536, :] = edge[:, X : 2 * X]


def cell_stats(ref, first, count):
    blocks = range(first, first + count)
    total = jnp.zeros((G, CELLS), F32)
    for block in blocks:
        total += ref[block * G : (block + 1) * G, :]
    mean = jnp.sum(total, axis=1, keepdims=True) * (1.0 / (count * CELLS))
    squares = jnp.zeros((G, CELLS), F32)
    for block in blocks:
        off = ref[block * G : (block + 1) * G, :] - mean
        squares += off * off
    return mean, jnp.sum(squares, axis=1, keepdims=True)


def own_kernel(
    lat_in,
    real_in,
    taps_in,
    taps_d_in,
    wide_out,
    first_out,
    middle_out,
    last_out,
    sums_ref,
    edge_ref,
    weight_out,
    lat_edge,
    real_edge,
    lat,
    taps,
    taps_d,
    weight,
    wide,
    first,
    middle,
    last,
    sems,
    patch,
    wide_lat,
):
    edge_copies = [
        fetch(lat_in.at[:, 1], lat_edge, sems.at[0]),
        fetch(real_in.at[:, 3], real_edge, sems.at[1]),
    ]
    lat_copy = fetch(lat_in, lat, sems.at[2])
    taps_copy = fetch(taps_in, taps, sems.at[3])
    taps_d_copy = fetch(taps_d_in, taps_d, sems.at[4])
    lat_copy.wait()
    wide_lat[...] = lat[...].reshape(1024, X).astype(F32)
    lane = lanes((C, X))
    for depth in range(2):
        clear_rims(depth, patch)
        for y in range(Y):
            spread_cells(wide_lat[pl.ds(depth * Y + y, C, stride=16), :], depth, y, lane, patch)
    taps_copy.wait()
    spread_weights(taps, wide)
    copies = [fetch(wide, wide_out, sems.at[5])]
    last[...] = dot(wide[0], patch[576:1152, :])
    copies.append(fetch(last, last_out, sems.at[6]))
    middle[...] = dot(wide[0], patch[0:576, :]) + dot(wide[1], patch[576:1152, :])
    copies.append(fetch(middle, middle_out, sems.at[7]))
    first[...] = dot(wide[1], patch[0:576, :])
    copies.append(fetch(first, first_out, sems.at[8]))
    taps_d_copy.wait()
    same = lax.broadcasted_iota(jnp.int32, (C, C), 0) == lanes((C, C))
    unit = jnp.where(same, 1.0, 0.0).astype(BF16)
    weight[...] = dot(unit, taps_d[...], (1, 1)).astype(BF16)
    copies.append(fetch(weight, weight_out, sems.at[9]))
    join_edge(edge_copies, lat_edge, real_edge, edge_ref)
    place = lanes((G, 128))
    sums = jnp.zeros((G, 128), F32)
    for at, column in enumerate(cell_stats(middle, 0, 8) + cell_stats(first, 4, 4)):
        sums = jnp.where(place == at, column, sums)
    sums_ref[...] = sums
    for copy in copies:
        copy.wait()


def rim_kernel(
    inside_ref,
    next_ref,
    sums_ref,
    gain_in,
    shift_in,
    wide_in,
    last_in,
    last_out,
    stats_out,
    real_next_out,
    patch,
    wide_lat,
    wide,
    last,
    stats,
    gain,
    shift,
    sems,
):
    wide_copy = fetch(wide_in.at[1], wide, sems.at[0])
    last_copy = fetch(last_in, last, sems.at[1])
    affine_copies = [fetch(gain_in, gain, sems.at[5]), fetch(shift_in, shift, sems.at[6])]
    copies = [fetch(next_ref.at[512:1536], real_next_out, sems.at[2])]
    wide_lat[...] = next_ref[0:512, :].astype(F32)
    lane = lanes((C, X))
    clear_rims(0, patch)
    for y in range(Y):
        spread_cells(wide_lat[pl.ds(y, C, stride=8), :], 0, y, lane, patch)
    wide_copy.wait()
    added = dot(wide[...], patch[...])
    last_copy.wait()
    last[...] += added
    copies.append(fetch(last, last_out, sems.at[3]))
    groups = [(2.0, sums_ref[:, 0:1], sums_ref[:, 1:2])]
    groups.append((jnp.where(inside_ref[0] > 0, 0.0, 1.0), sums_ref[:, 2:3], sums_ref[:, 3:4]))
    groups.append((1.0,) + cell_stats(last, 0, 4))
    groups.append((jnp.where(inside_ref[1] > 0, 1.0, 0.0),) + cell_stats(last, 4, 4))
    depths = jnp.zeros((G, 1), F32)
    mean = jnp.zeros((G, 1), F32)
    for weight, one, _ in groups:
        depths += weight
        mean += weight * one
    mean /= depths
    spread = jnp.zeros((G, 1), F32)
    for weight, one, squares in groups:
        own = squares if isinstance(weight, float) else weight * squares
        spread += own + weight * (4.0 * CELLS) * (one - mean) * (one - mean)
    row = as_row(mean, 0) + as_row(spread, G)
    for copy in affine_copies:
        copy.wait()
    row += as_row(as_column(gain[...], 0), 2 * G) + as_row(as_column(shift[...], 0), 3 * G)
    stats[...] = jnp.broadcast_to(row, (NDEV, 128))
    copies.append(fetch(stats, stats_out, sems.at[4]))
    for copy in copies:
        copy.wait()


def activate(before):
    squashed = jax.nn.sigmoid(4.0 * before)
    output = before * (0.2 + 0.8 * squashed)
    derivative = 0.2 + 0.8 * squashed + 3.2 * before * squashed * (1.0 - squashed)
    return (output, derivative)


def convolve(weight_ref, patch, build):
    early = weight_ref[:, 0:1024]
    late = weight_ref[:, 1024:2048]
    second = dot(late, patch[2048:3072, :])
    build(2)
    build(3)
    shared = dot(jnp.concatenate([late, early], axis=0), patch[1024:2048, :])
    build(0)
    build(1)
    return dot(early, patch[0:1024, :]) + shared[0:C, :], second + shared[C : 2 * C, :]


def finish(pre, cot_ref, out, wide_cot, wide_out, grad):
    wide_cot[...] = cot_ref[...].astype(F32)
    nothing = jnp.zeros((C, CELLS), BF16)
    grad[0:C, :] = nothing
    grad[3 * C : 4 * C, :] = nothing
    for m in range(2):
        for y in range(Y):
            output, slope = activate(pre[m][:, y * X : (y + 1) * X])
            wide_out[pl.ds(m * Y + y, C, stride=16), :] = output
            cot = wide_cot[pl.ds(m * Y + y, C, stride=16), :]
            grad[(2 - m) * C : (3 - m) * C, y * X : (y + 1) * X] = (cot * slope).astype(BF16)
    out[...] = wide_out[...].astype(BF16)


def kernel_terms(planes, grad):
    for half in range(2):
        terms = dot(planes[half], grad[128:256, :], (1, 1))
        terms += dot(planes[half + 2], grad[64:192, :], (1, 1))
        yield terms + dot(planes[half + 4], grad[0:128, :], (1, 1))


def split_depth(at, places, halves, rows, patch):
    base, stride = places
    column = lanes((2 * X, 4 * X))
    source = lax.broadcasted_iota(jnp.int32, (2 * X, 4 * X), 0)
    pick = jnp.where(source == 2 * (column % X) + column // X - 1, 1.0, 0.0).astype(BF16)
    edge = jnp.zeros((128, X), BF16)
    patch[at : at + 128, 0:X] = edge
    patch[at + 384 : at + 512, CELLS - X : CELLS] = edge
    for row in range(2 * Y):
        for half in range(2):
            cells = halves[half, pl.ds(base + row, G, stride=stride), :].astype(BF16)
            rows[at + row * G : at + (row + 1) * G, half * X : (half + 1) * X] = cells
    split = dot(rows[at : at + 512, :], pick).astype(BF16)
    for row in range(2 * Y):
        for kx in range(4):
            piece = split[row * G : (row + 1) * G, kx * X : (kx + 1) * X]
            for ky in range(4):
                if (row + 1 - ky) % 2 == 0 and 0 <= (row + 1 - ky) // 2 < Y:
                    y = (row + 1 - ky) // 2
                    place = at + ky * 128 + kx * G
                    patch[place : place + G, y * X : (y + 1) * X] = piece


def real_kernel(
    real_ref,
    prev_ref,
    next_in,
    weight_in,
    cot_ref,
    wide_in,
    first_in,
    out_out,
    terms_out,
    first_out,
    out,
    edge,
    weight,
    wide,
    first,
    terms_ref,
    sems,
    patch,
    lat_patch,
    halves,
    rows,
    wide_cot,
    wide_out,
    grad,
):
    edge_copy = fetch(next_in, edge, sems.at[0])
    weight_copy = fetch(weight_in, weight, sems.at[1])
    copies = [
        fetch(wide_in.at[0], wide, sems.at[2]),
        fetch(first_in, first, sems.at[3]),
    ]
    for half in range(2):
        part = slice(512 + half * 512, 1024 + half * 512)
        halves[half, 0:2048, :] = real_ref[:, half * X : (half + 1) * X].astype(F32)
        halves[half, 2048:2560, :] = prev_ref[part, :].astype(F32)
    places = ((2048, 16), (0, 64), (16, 64), (32, 64), (48, 64), (2560, 16))

    def build(depth):
        split_depth(depth * 512, places[depth], halves, rows, patch)

    build(4)
    edge_copy.wait()
    for half in range(2):
        halves[half, 2560:3072, :] = edge[half * 512 : (half + 1) * 512, :].astype(F32)
    build(5)
    weight_copy.wait()
    pre = convolve(weight, patch, build)
    halves[0, 0:512, :] = prev_ref[0:512, :].astype(F32)
    lane = lanes((C, X))
    clear_rims(0, lat_patch)
    for y in range(Y):
        spread_cells(halves[0, pl.ds(y, C, stride=8), :], 0, y, lane, lat_patch)
    for copy in copies:
        copy.wait()
    first[...] += dot(wide[...], lat_patch[...])
    first_copy = fetch(first, first_out, sems.at[4])
    finish(pre, cot_ref, out, wide_cot, wide_out, grad)
    stores = [first_copy, fetch(out, out_out, sems.at[5])]
    planes = [patch[depth * 512 : (depth + 1) * 512, :] for depth in range(6)]
    for half, terms in enumerate(kernel_terms(planes, grad)):
        terms_ref[half * 512 : (half + 1) * 512, :] = terms
        piece = pl.ds(half * 512, 512)
        stores.append(fetch(terms_ref.at[piece], terms_out.at[piece], sems.at[6 + half]))
    for store in stores:
        store.wait()


def fake_kernel(
    inside_ref,
    first_in,
    middle_in,
    last_ref,
    stats_ref,
    weight_in,
    cot_ref,
    real_terms_in,
    out_out,
    low_out,
    high_out,
    terms_out,
    out,
    terms_ref,
    first_ref,
    middle_ref,
    real_terms,
    weight_ref,
    sems,
    patch,
    wide_cot,
    wide_out,
    grad,
):
    weight_copy = fetch(weight_in, weight_ref, sems.at[5])
    middle_copy = fetch(middle_in, middle_ref, sems.at[4])
    first_copy = fetch(first_in, first_ref, sems.at[0])
    real_copy = fetch(real_terms_in, real_terms, sems.at[1])
    stats = stats_ref[...]
    slab = lax.broadcasted_iota(jnp.int32, (NDEV, 128), 0) // 2 % 32
    depths = jnp.where(slab == 0, 5.0, jnp.where(slab == 31, 3.0, 4.0))
    mean_row = jnp.sum(stats * depths, axis=0, keepdims=True) * (1.0 / (4.0 * NDEV))
    off = stats - mean_row
    between = as_column(jnp.sum(off * off * depths, axis=0, keepdims=True), 0)
    center = as_column(mean_row, 0)
    within = as_column(jnp.sum(stats, axis=0, keepdims=True), G)
    variance = (within + 4.0 * CELLS * between) * (1.0 / (16.0 * CELLS * NDEV))
    factor = as_column(stats[0:1, :], 2 * G) * lax.rsqrt(variance + 1e-05)
    shift = as_column(stats[0:1, :], 3 * G)
    lane = lanes((G, X))
    edge = jnp.zeros((128, X), BF16)

    def build(depth):
        if depth == 2:
            middle_copy.wait()
        elif depth == 0:
            first_copy.wait()
        before_ref = (first_ref, middle_ref, last_ref)[depth // 2]
        patch[depth * 512 : depth * 512 + 128, 0:X] = edge
        patch[depth * 512 + 384 : depth * 512 + 512, CELLS - X : CELLS] = edge
        for py in range(2):
            for px in range(2):
                block = (depth % 2 * 4 + py * 2 + px) * G
                for y in range(Y):
                    cells = before_ref[block : block + G, y * X : (y + 1) * X]
                    fake = jnp.maximum((cells - center) * factor + shift, 0.0)
                    if depth == 0:
                        fake = jnp.where(inside_ref[0] > 0, fake, 0.0)
                    if depth == 5:
                        fake = jnp.where(inside_ref[1] > 0, fake, 0.0)
                    if px == 1:
                        pieces = ((2, fake), (0, from_left(fake, lane)))
                    else:
                        pieces = ((1, fake), (3, from_right(fake, lane)))
                    for kx, piece in pieces:
                        piece = piece.astype(BF16)
                        for ky, to in ((2, y), (0, y + 1)) if py == 1 else ((1, y), (3, y - 1)):
                            if 0 <= to < Y:
                                at = depth * 512 + ky * 128 + kx * G
                                patch[at : at + G, to * X : (to + 1) * X] = piece

    build(4)
    build(5)
    weight_copy.wait()
    pre = convolve(weight_ref, patch, build)
    finish(pre, cot_ref, out, wide_cot, wide_out, grad)
    stores = [
        fetch(out, out_out, sems.at[6]),
        fetch(grad.at[2 * C : 3 * C], low_out, sems.at[2]),
        fetch(grad.at[C : 2 * C], high_out, sems.at[3]),
    ]
    planes = [patch[depth * 512 : (depth + 1) * 512, :] for depth in range(6)]
    real_copy.wait()
    for half, terms in enumerate(kernel_terms(planes, grad)):
        rows = slice(half * 512, (half + 1) * 512)
        terms_ref[rows, :] = terms + real_terms[rows, :]
        piece = pl.ds(half * 512, 512)
        stores.append(fetch(terms_ref.at[piece], terms_out.at[piece], sems.at[7 + half]))
    for store in stores:
        store.wait()


def sum_kernel(parts_ref, prev_ref, first_ref, sums_ref):
    del prev_ref, first_ref
    total = jnp.sum(parts_ref[...].reshape(NDEV, 8, 128), axis=0, keepdims=True)
    sums_ref[...] = jnp.broadcast_to(total, (NDEV, 8, 128)).reshape(NDEV * 8, 128).astype(BF16)


def unpack_kernel(sums_ref, out, whole, sems):
    copies = []
    for part in range(4):
        rows = slice(part * 256, (part + 1) * 256)
        sums = sums_ref[rows, :].astype(F32)
        whole[0, rows, :] = sums[:, 0:C]
        whole[1, rows, :] = sums[:, C : 2 * C]
        for half in range(2):
            piece = pl.ds(part * 256, 256)
            copies.append(fetch(whole.at[half, piece], out.at[half, piece], sems.at[2 * part + half]))
    for copy in copies:
        copy.wait()


def weave_into(result, first_row, stride, wide_out):
    column = lanes((2 * X, 2 * X))
    source = lax.broadcasted_iota(jnp.int32, (2 * X, 2 * X), 0)
    weave = jnp.where(source == (column % 2) * X + column // 2, 1.0, 0.0).astype(BF16)
    for py in range(2):
        even = result[py * 64 : py * 64 + G, :]
        odd = result[py * 64 + G : py * 64 + 2 * G, :]
        both = jnp.concatenate(
            [
                jnp.concatenate([even[:, y * X : (y + 1) * X], odd[:, y * X : (y + 1) * X]], axis=1)
                for y in range(Y)
            ],
            axis=0,
        )
        woven = dot(both, weave)
        for y in range(Y):
            rows = pl.ds(first_row + 2 * y + py, G, stride=stride)
            wide_out[0, rows, :] = woven[y * G : (y + 1) * G, 0:X]
            wide_out[1, rows, :] = woven[y * G : (y + 1) * G, X : 2 * X]


def spread_edge(cells, depth, patch):
    lane = lanes((C, X))
    clear_rims(depth, patch)
    for y in range(Y):
        spread_cells(cells[:, y * X : (y + 1) * X].astype(F32), depth, y, lane, patch)


def pull_own_kernel(
    low_in,
    high_in,
    taps_in,
    wide_out,
    first_out,
    last_out,
    image_out,
    cells,
    taps,
    wide,
    first,
    last,
    patch,
    wide_rows,
    image,
    sems,
):
    edges = [fetch(ref, cells.at[i], sems.at[i]) for i, ref in enumerate((low_in, high_in))]
    taps_copy = fetch(taps_in, taps, sems.at[2])
    for depth in range(2):
        edges[depth].wait()
        spread_edge(cells[depth], depth, patch)
    taps_copy.wait()
    spread_weights(taps, wide)
    copies = [fetch(wide, wide_out, sems.at[3])]
    first[...] = dot(wide[1, 128:256, :], patch[0:576, :])
    copies.append(fetch(first, first_out, sems.at[4]))
    last[...] = dot(wide[0, 0:128, :], patch[576:1152, :])
    copies.append(fetch(last, last_out, sems.at[5]))
    middle = dot(wide[0], patch[0:576, :]) + dot(wide[1], patch[576:1152, :])
    middle = middle.astype(BF16)
    weave_into(middle[0:128, :], 0, 32, wide_rows)
    weave_into(middle[128:256, :], 16, 32, wide_rows)
    for half in range(2):
        image[:, :, half * X : (half + 1) * X] = wide_rows[half].reshape(G, 32, X).astype(BF16)
    copies.append(fetch(image, image_out.at[:, 16:48], sems.at[6]))
    for copy in copies:
        copy.wait()


def add_edge(side, cells, wide, share, image_out, patch, wide_rows, image, sem):
    spread_edge(cells, 0, patch)
    rows = slice(128 - side * 128, 256 - side * 128)
    weave_into((share[...] + dot(wide[rows, :], patch[...])).astype(BF16), 0, 16, wide_rows)
    for half in range(2):
        image[:, :, half * X : (half + 1) * X] = wide_rows[half].reshape(G, 16, X).astype(BF16)
    return fetch(image, image_out.at[:, pl.ds(side * 48, 16)], sem)


def pull_prev_kernel(
    edge_in,
    wide_in,
    first_in,
    last_in,
    sums_ref,
    image_in,
    image_out,
    wide_next,
    last_ref,
    cells,
    wide,
    share,
    patch,
    wide_rows,
    image,
    sems,
):
    del sums_ref, image_in
    copies = [
        fetch(edge_in, cells, sems.at[0]),
        fetch(wide_in.at[0], wide, sems.at[1]),
        fetch(first_in, share, sems.at[2]),
    ]
    later = [
        fetch(wide_in.at[1], wide_next, sems.at[3]),
        fetch(last_in, last_ref, sems.at[4]),
    ]
    for copy in copies:
        copy.wait()
    later.append(add_edge(0, cells, wide, share, image_out, patch, wide_rows, image, sems.at[5]))
    for copy in later:
        copy.wait()


def pull_next_kernel(
    edge_ref, wide_ref, last_ref, image_in, image_out, patch, wide_rows, image, sem
):
    del image_in
    add_edge(1, edge_ref, wide_ref, last_ref, image_out, patch, wide_rows, image, sem).wait()


def call(body, name, args, outs, scratch, flops, mebibytes, smem=(), far=(), far_outs=(), aliases=()):
    moved = sum(a.size * a.dtype.itemsize for a in args) + sum(o.size * o.dtype.itemsize for o in outs)
    spaces = [
        pltpu.SMEM if i in smem else pl.ANY if i in far else pltpu.VMEM for i in range(len(args))
    ]
    out_spaces = [pltpu.HBM if i in far_outs else pltpu.VMEM for i in range(len(outs))]
    outs = [pltpu.HBM(o.shape, o.dtype) if i in far_outs else o for i, o in enumerate(outs)]
    args = [
        pltpu.with_memory_space_constraint(a, pltpu.HBM) if i in far else a for i, a in enumerate(args)
    ]
    return pl.pallas_call(
        body,
        name=name,
        out_shape=outs,
        in_specs=[pl.BlockSpec(memory_space=space) for space in spaces],
        out_specs=[pl.BlockSpec(memory_space=space) for space in out_spaces],
        scratch_shapes=scratch,
        input_output_aliases=dict(aliases),
        compiler_params=pltpu.CompilerParams(vmem_limit_bytes=mebibytes * 1024 * 1024),
        cost_estimate=pl.CostEstimate(flops=flops, bytes_accessed=moved, transcendentals=0),
    )(*args)


def to_next(edge):
    ends = lax.axis_size("slab") - 1
    return lax.ppermute(edge, "slab", [(i, i + 1) for i in range(ends)])


def to_prev(edge):
    ends = lax.axis_size("slab") - 1
    return lax.ppermute(edge, "slab", [(i + 1, i) for i in range(ends)])


def local(latent, g_weight, bn_gain, bn_shift, real_crops, d_weight, cot_fake, cot_real):
    shape = jax.ShapeDtypeStruct
    taps_g = g_weight.transpose(0, 1, 2, 4, 3).reshape(64 * G, C)
    taps_d = d_weight.reshape(64 * G, C)
    lat = latent[0]
    real = real_crops[0]
    at = lax.axis_index("slab")
    inside = jnp.stack([at > 0, at < lax.axis_size("slab") - 1]).astype(jnp.int32)
    (low,) = call(
        edge_kernel,
        "edges",
        (lat, real),
        [shape((1536, X), BF16)],
        [
            pltpu.VMEM((C, Y, X), BF16),
            pltpu.VMEM((G, 2 * Y, 2 * X), BF16),
            pltpu.SemaphoreType.DMA((2,)),
        ],
        0,
        4,
        far=(0, 1),
    )
    next_ = to_prev(low)
    wide, first, middle, last, sums, high, weight = call(
        own_kernel,
        "own_cells",
        (lat, real, taps_g, taps_d),
        [shape((2, 256, 576), BF16)]
        + [shape((256, CELLS), F32)] * 3
        + [shape((G, 128), F32), shape((1536, X), BF16), shape((C, 2048), BF16)],
        [
            pltpu.VMEM((C, Y, X), BF16),
            pltpu.VMEM((G, 2 * Y, 2 * X), BF16),
            pltpu.VMEM((C, 2, Y, X), BF16),
            pltpu.VMEM((2048, C), BF16),
            pltpu.VMEM((2048, C), BF16),
            pltpu.VMEM((C, 2048), BF16),
            pltpu.VMEM((2, 256, 576), BF16),
            pltpu.VMEM((256, CELLS), F32),
            pltpu.VMEM((256, CELLS), F32),
            pltpu.VMEM((256, CELLS), F32),
            pltpu.SemaphoreType.DMA((10,)),
            pltpu.VMEM((1152, CELLS), BF16),
            pltpu.VMEM((1024, X), F32),
        ],
        4 * 256 * 1152 * CELLS,
        16,
        far=(0, 1, 2, 3),
        far_outs=(0, 1, 2, 3, 6),
    )
    prev = to_next(high)
    last, stats, real_next = call(
        rim_kernel,
        "rim_cells",
        (inside, next_, sums, bn_gain.reshape(1, G), bn_shift.reshape(1, G), wide, last),
        [shape((256, CELLS), F32), shape((NDEV, 128), F32), shape((1024, X), BF16)],
        [
            pltpu.VMEM((576, CELLS), BF16),
            pltpu.VMEM((512, X), F32),
            pltpu.VMEM((256, 576), BF16),
            pltpu.VMEM((256, CELLS), F32),
            pltpu.VMEM((NDEV, 128), F32),
            pltpu.VMEM((1, G), F32),
            pltpu.VMEM((1, G), F32),
            pltpu.SemaphoreType.DMA((7,)),
        ],
        256 * 1152 * CELLS,
        12,
        smem=(0,),
        far=(3, 4, 5, 6),
        far_outs=(0, 1, 2),
    )
    stats = lax.all_to_all(stats, AXES, 0, 0, tiled=True)
    working = [
        pltpu.VMEM((C * 2 * Y, X), F32),
        pltpu.VMEM((C * 2 * Y, X), F32),
        pltpu.VMEM((4 * C, CELLS), BF16),
    ]
    d_real, real_terms, first = call(
        real_kernel,
        "real_branch",
        (
            real.reshape(G * 64, 2 * X),
            prev,
            real_next,
            weight,
            cot_real.reshape(C * 2 * Y, X),
            wide,
            first,
        ),
        [shape((C * 2 * Y, X), BF16), shape((1024, 2 * C), F32), shape((256, CELLS), F32)],
        [
            pltpu.VMEM((C * 2 * Y, X), BF16),
            pltpu.VMEM((1024, X), BF16),
            pltpu.VMEM((C, 2048), BF16),
            pltpu.VMEM((256, 576), BF16),
            pltpu.VMEM((256, CELLS), F32),
            pltpu.VMEM((1024, 2 * C), F32),
            pltpu.SemaphoreType.DMA((8,)),
            pltpu.VMEM((6 * 512, CELLS), BF16),
            pltpu.VMEM((576, CELLS), BF16),
            pltpu.VMEM((2, 3072, X), F32),
            pltpu.VMEM((3072, 2 * X), BF16),
        ]
        + working,
        16 * 2048 * C * CELLS,
        26,
        far=(2, 3, 5, 6),
        far_outs=(0, 1, 2),
    )
    d_fake, low, high, terms = call(
        fake_kernel,
        "fake_branch",
        (
            inside,
            first,
            middle,
            last,
            stats,
            weight,
            cot_fake.reshape(C * 2 * Y, X),
            real_terms,
        ),
        [
            shape((C * 2 * Y, X), BF16),
            shape((C, CELLS), BF16),
            shape((C, CELLS), BF16),
            shape((NDEV * 8, 128), F32),
        ],
        [
            pltpu.VMEM((C * 2 * Y, X), BF16),
            pltpu.VMEM((NDEV * 8, 128), F32),
            pltpu.VMEM((256, CELLS), F32),
            pltpu.VMEM((256, CELLS), F32),
            pltpu.VMEM((NDEV * 8, 128), F32),
            pltpu.VMEM((C, 2048), BF16),
            pltpu.SemaphoreType.DMA((9,)),
            pltpu.VMEM((6 * 512, CELLS), BF16),
        ]
        + working,
        8 * 2048 * C * CELLS * 2,
        26,
        smem=(0,),
        far=(1, 2, 5, 7),
        far_outs=(0, 1, 2, 3),
    )
    parts = lax.all_to_all(terms.reshape(NDEV, 8, 128), AXES, 0, 0, tiled=True)
    grad_prev = to_next(high)
    grad_next = to_prev(low)
    pull_wide, pull_first, pull_last, image = call(
        pull_own_kernel,
        "pull_own",
        (low, high, taps_d),
        [
            shape((2, 256, 576), BF16),
            shape((128, CELLS), F32),
            shape((128, CELLS), F32),
            shape((G, 64, 2 * X), BF16),
        ],
        [
            pltpu.VMEM((2, C, CELLS), BF16),
            pltpu.VMEM((2048, C), BF16),
            pltpu.VMEM((2, 256, 576), BF16),
            pltpu.VMEM((128, CELLS), F32),
            pltpu.VMEM((128, CELLS), F32),
            pltpu.VMEM((1152, CELLS), BF16),
            pltpu.VMEM((2, G * 32, X), F32),
            pltpu.VMEM((G, 32, 2 * X), BF16),
            pltpu.SemaphoreType.DMA((7,)),
        ],
        2 * 384 * 1152 * CELLS,
        16,
        far=(0, 1, 2),
        far_outs=(0, 1, 2, 3),
    )
    (sums,) = call(
        sum_kernel,
        "sum_terms",
        (parts.reshape(NDEV * 8, 128), grad_prev, pull_first),
        [shape((NDEV * 8, 128), BF16)],
        [],
        NDEV * 1024,
        6,
        far=(1, 2),
    )
    whole = lax.all_to_all(sums.reshape(NDEV, 8, 128), AXES, 0, 0, tiled=True)
    outer = [
        pltpu.VMEM((576, CELLS), BF16),
        pltpu.VMEM((2, G * 16, X), F32),
        pltpu.VMEM((G, 16, 2 * X), BF16),
    ]
    image, wide_next, last_share = call(
        pull_prev_kernel,
        "pull_prev",
        (grad_prev, pull_wide, pull_first, pull_last, sums, image),
        [shape((G, 64, 2 * X), BF16), shape((256, 576), BF16), shape((128, CELLS), F32)],
        [
            pltpu.VMEM((C, CELLS), BF16),
            pltpu.VMEM((256, 576), BF16),
            pltpu.VMEM((128, CELLS), F32),
        ]
        + outer
        + [pltpu.SemaphoreType.DMA((6,))],
        128 * 1152 * CELLS,
        12,
        far=(0, 1, 2, 3, 4, 5),
        far_outs=(0,),
        aliases=((5, 0),),
    )
    (image,) = call(
        pull_next_kernel,
        "pull_next",
        (grad_next, wide_next, last_share, image),
        [shape((G, 64, 2 * X), BF16)],
        outer + [pltpu.SemaphoreType.DMA],
        128 * 1152 * CELLS,
        12,
        far=(3,),
        far_outs=(0,),
        aliases=((3, 0),),
    )
    (weight_grad,) = call(
        unpack_kernel,
        "unpack",
        (whole.reshape(NDEV * 8, 128),),
        [shape((2, 1024, C), F32)],
        [pltpu.VMEM((2, 1024, C), F32), pltpu.SemaphoreType.DMA((8,))],
        0,
        6,
        far_outs=(0,),
    )
    return (
        d_fake.reshape(1, C, 2, Y, X),
        d_real.reshape(1, C, 2, Y, X),
        image.reshape(1, G, 4, 2 * Y, 2 * X),
        weight_grad.reshape(4, 4, 4, G, C),
    )


def solution(mesh):
    split = P(("section", "rep"), None, "slab", None, None)
    in_specs = (split, P(), P(), P(), split, P(), split, split)
    out_specs = (split, split, split, P())
    return jax.shard_map(local, mesh=mesh, in_specs=in_specs, out_specs=out_specs, check_vma=False)
```

```python
import jax
import jax.numpy as jnp
from jax import lax
from jax.experimental import pallas as pl
from jax.experimental.pallas import tpu as pltpu
from jax.sharding import PartitionSpec as P

AXES = ("section", "slab", "rep")
NDEV = 128
C = 64
G = 32
Y = 8
X = 128
CELLS = Y * X
F32 = jnp.float32
BF16 = jnp.bfloat16

phase_taps = (((1, 0), (3, -1)), ((0, 1), (2, 0)))


def dot(a, b, dims=(1, 0)):
    return lax.dot_general(a, b, (((dims[0],), (dims[1],)), ((), ())), preferred_element_type=F32)


def lanes(shape):
    return lax.broadcasted_iota(jnp.int32, shape, len(shape) - 1)


def from_left(tile, lane):
    return jnp.where(lane == 0, 0.0, pltpu.roll(tile, 1, 1))


def from_right(tile, lane):
    return jnp.where(lane == X - 1, 0.0, pltpu.roll(tile, X - 1, 1))


def spread_weights(taps_ref, wide_ref):
    wide_ref[...] = jnp.zeros_like(wide_ref)
    for pz in range(2):
        for py in range(2):
            for px in range(2):
                row = ((1 - pz) * 4 + py * 2 + px) * G
                for kz, oz in phase_taps[pz]:
                    tz = oz if pz == 1 else oz + 1
                    for ky, oy in phase_taps[py]:
                        for kx, ox in phase_taps[px]:
                            col = (oy + 1) * 192 + (ox + 1) * 64
                            tap = (kz * 16 + ky * 4 + kx) * G
                            wide_ref[tz, row : row + G, col : col + C] = taps_ref[tap : tap + G, :]


def spread_cells(tile, depth, y, lane, patch_ref):
    for xi, moved in ((0, from_left(tile, lane)), (1, tile), (2, from_right(tile, lane))):
        piece = moved.astype(BF16)
        for yi in range(3):
            to = y - (yi - 1)
            if 0 <= to < Y:
                row = depth * 576 + yi * 192 + xi * 64
                patch_ref[row : row + C, to * X : (to + 1) * X] = piece


def clear_rims(depth, patch_ref):
    edge = jnp.zeros((192, X), BF16)
    patch_ref[depth * 576 : depth * 576 + 192, 0:X] = edge
    patch_ref[depth * 576 + 384 : depth * 576 + 576, CELLS - X : CELLS] = edge


def fetch(source, target, sem):
    copy = pltpu.make_async_copy(source, target, sem)
    copy.start()
    return copy


def as_row(column, shift):
    sub = lax.broadcasted_iota(jnp.int32, (G, 128), 0)
    return jnp.sum(jnp.where(lanes((G, 128)) == sub + shift, column, 0.0), axis=0, keepdims=True)


def as_column(row, shift):
    shape = (G, row.shape[1])
    sub = lax.broadcasted_iota(jnp.int32, shape, 0)
    return jnp.sum(jnp.where(lanes(shape) == sub + shift, row, 0.0), axis=1, keepdims=True)


def edge_kernel(lat_in, real_in, edge_ref, lat_edge, real_edge, sems):
    copies = [
        fetch(lat_in.at[:, 0], lat_edge, sems.at[0]),
        fetch(real_in.at[:, 0], real_edge, sems.at[1]),
    ]
    join_edge(copies, lat_edge, real_edge, edge_ref)


def join_edge(copies, lat_edge, real_edge, edge_ref):
    copies[0].wait()
    edge_ref[0:512, :] = lat_edge[...].reshape(512, X)
    copies[1].wait()
    edge = real_edge[...].reshape(512, 2 * X)
    edge_ref[512:1024, :] = edge[:, 0:X]
    edge_ref[1024:1536, :] = edge[:, X : 2 * X]


def wide_column(row, shift):
    return jnp.broadcast_to(as_column(row, shift), (G, X))


def cell_stats(ref, first, count):
    blocks = range(first, first + count)
    total = jnp.zeros((G, CELLS), F32)
    for block in blocks:
        total += ref[block * G : (block + 1) * G, :]
    mean = jnp.sum(total, axis=1, keepdims=True) * (1.0 / (count * CELLS))
    squares = jnp.zeros((G, CELLS), F32)
    for block in blocks:
        off = ref[block * G : (block + 1) * G, :] - mean
        squares += off * off
    return mean, jnp.sum(squares, axis=1, keepdims=True)


def own_kernel(
    lat_in,
    real_in,
    taps_in,
    taps_d_in,
    wide_out,
    first_out,
    middle_out,
    last_out,
    sums_ref,
    edge_ref,
    weight_out,
    lat_edge,
    real_edge,
    lat,
    taps,
    taps_d,
    weight,
    wide,
    first,
    middle,
    last,
    sems,
    patch,
    wide_lat,
):
    edge_copies = [
        fetch(lat_in.at[:, 1], lat_edge, sems.at[0]),
        fetch(real_in.at[:, 3], real_edge, sems.at[1]),
    ]
    lat_copy = fetch(lat_in, lat, sems.at[2])
    taps_copy = fetch(taps_in, taps, sems.at[3])
    taps_d_copy = fetch(taps_d_in, taps_d, sems.at[4])
    lat_copy.wait()
    wide_lat[...] = lat[...].reshape(1024, X).astype(F32)
    lane = lanes((C, X))
    for depth in range(2):
        clear_rims(depth, patch)
        for y in range(Y):
            spread_cells(wide_lat[pl.ds(depth * Y + y, C, stride=16), :], depth, y, lane, patch)
    taps_copy.wait()
    spread_weights(taps, wide)
    copies = [fetch(wide, wide_out, sems.at[5])]
    last[...] = dot(wide[0], patch[576:1152, :])
    copies.append(fetch(last, last_out, sems.at[6]))
    middle[...] = dot(wide[0], patch[0:576, :]) + dot(wide[1], patch[576:1152, :])
    copies.append(fetch(middle, middle_out, sems.at[7]))
    first[...] = dot(wide[1], patch[0:576, :])
    copies.append(fetch(first, first_out, sems.at[8]))
    taps_d_copy.wait()
    same = lax.broadcasted_iota(jnp.int32, (C, C), 0) == lanes((C, C))
    unit = jnp.where(same, 1.0, 0.0).astype(BF16)
    weight[...] = dot(unit, taps_d[...], (1, 1)).astype(BF16)
    copies.append(fetch(weight, weight_out, sems.at[9]))
    join_edge(edge_copies, lat_edge, real_edge, edge_ref)
    place = lanes((G, 128))
    sums = jnp.zeros((G, 128), F32)
    for at, column in enumerate(cell_stats(middle, 0, 8) + cell_stats(first, 4, 4)):
        sums = jnp.where(place == at, column, sums)
    sums_ref[...] = sums
    for copy in copies:
        copy.wait()


def rim_kernel(
    inside_ref,
    next_ref,
    sums_ref,
    gain_in,
    shift_in,
    wide_in,
    last_in,
    last_out,
    stats_out,
    real_next_out,
    patch,
    wide_lat,
    wide,
    last,
    stats,
    gain,
    shift,
    sems,
):
    wide_copy = fetch(wide_in.at[1], wide, sems.at[0])
    last_copy = fetch(last_in, last, sems.at[1])
    affine_copies = [fetch(gain_in, gain, sems.at[5]), fetch(shift_in, shift, sems.at[6])]
    copies = [fetch(next_ref.at[512:1536], real_next_out, sems.at[2])]
    wide_lat[...] = next_ref[0:512, :].astype(F32)
    lane = lanes((C, X))
    clear_rims(0, patch)
    for y in range(Y):
        spread_cells(wide_lat[pl.ds(y, C, stride=8), :], 0, y, lane, patch)
    wide_copy.wait()
    added = dot(wide[...], patch[...])
    last_copy.wait()
    last[...] += added
    copies.append(fetch(last, last_out, sems.at[3]))
    groups = [(2.0, sums_ref[:, 0:1], sums_ref[:, 1:2])]
    groups.append((jnp.where(inside_ref[0] > 0, 0.0, 1.0), sums_ref[:, 2:3], sums_ref[:, 3:4]))
    groups.append((1.0,) + cell_stats(last, 0, 4))
    groups.append((jnp.where(inside_ref[1] > 0, 1.0, 0.0),) + cell_stats(last, 4, 4))
    depths = jnp.zeros((G, 1), F32)
    mean = jnp.zeros((G, 1), F32)
    for weight, one, _ in groups:
        depths += weight
        mean += weight * one
    mean /= depths
    spread = jnp.zeros((G, 1), F32)
    for weight, one, squares in groups:
        own = squares if isinstance(weight, float) else weight * squares
        spread += own + weight * (4.0 * CELLS) * (one - mean) * (one - mean)
    row = as_row(mean, 0) + as_row(spread, G)
    for copy in affine_copies:
        copy.wait()
    row += as_row(as_column(gain[...], 0), 2 * G) + as_row(as_column(shift[...], 0), 3 * G)
    stats[...] = jnp.broadcast_to(row, (NDEV, 128))
    copies.append(fetch(stats, stats_out, sems.at[4]))
    for copy in copies:
        copy.wait()


def activate(before):
    squashed = jax.nn.sigmoid(4.0 * before)
    output = before * (0.2 + 0.8 * squashed)
    derivative = 0.2 + 0.8 * squashed + 3.2 * before * squashed * (1.0 - squashed)
    return (output, derivative)


def convolve(weight_ref, patch, build):
    early = weight_ref[:, 0:1024]
    late = weight_ref[:, 1024:2048]
    second = dot(late, patch[2048:3072, :])
    build(2)
    build(3)
    shared = dot(jnp.concatenate([late, early], axis=0), patch[1024:2048, :])
    build(0)
    build(1)
    return dot(early, patch[0:1024, :]) + shared[0:C, :], second + shared[C : 2 * C, :]


def finish(pre, cot_ref, out, wide_cot, wide_out, grad):
    wide_cot[...] = cot_ref[...].astype(F32)
    nothing = jnp.zeros((C, CELLS), BF16)
    grad[0:C, :] = nothing
    grad[3 * C : 4 * C, :] = nothing
    for m in range(2):
        for y in range(Y):
            output, slope = activate(pre[m][:, y * X : (y + 1) * X])
            wide_out[pl.ds(m * Y + y, C, stride=16), :] = output
            cot = wide_cot[pl.ds(m * Y + y, C, stride=16), :]
            grad[(2 - m) * C : (3 - m) * C, y * X : (y + 1) * X] = (cot * slope).astype(BF16)
    out[...] = wide_out[...].astype(BF16)


def kernel_terms(planes, grad):
    for half in range(2):
        terms = dot(planes[half], grad[128:256, :], (1, 1))
        terms += dot(planes[half + 2], grad[64:192, :], (1, 1))
        yield terms + dot(planes[half + 4], grad[0:128, :], (1, 1))


def column_picker():
    column = lanes((2 * X, 4 * X))
    source = lax.broadcasted_iota(jnp.int32, (2 * X, 4 * X), 0)
    return jnp.where(source == 2 * (column % X) + column // X - 1, 1.0, 0.0).astype(BF16)


def split_depth(at, places, halves, rows, patch, pick):
    base, stride = places
    edge = jnp.zeros((128, X), BF16)
    patch[at : at + 128, 0:X] = edge
    patch[at + 384 : at + 512, CELLS - X : CELLS] = edge
    for row in range(2 * Y):
        for half in range(2):
            cells = halves[half, pl.ds(base + row, G, stride=stride), :].astype(BF16)
            rows[at + row * G : at + (row + 1) * G, half * X : (half + 1) * X] = cells
    split = dot(rows[at : at + 512, :], pick[...]).astype(BF16)
    for row in range(2 * Y):
        for kx in range(4):
            piece = split[row * G : (row + 1) * G, kx * X : (kx + 1) * X]
            for ky in range(4):
                if (row + 1 - ky) % 2 == 0 and 0 <= (row + 1 - ky) // 2 < Y:
                    y = (row + 1 - ky) // 2
                    place = at + ky * 128 + kx * G
                    patch[place : place + G, y * X : (y + 1) * X] = piece


def real_kernel(
    real_ref,
    prev_ref,
    next_in,
    weight_in,
    cot_ref,
    wide_in,
    first_in,
    out_out,
    terms_out,
    first_out,
    out,
    edge,
    weight,
    wide,
    first,
    terms_ref,
    pick,
    sems,
    patch,
    lat_patch,
    halves,
    rows,
    wide_cot,
    wide_out,
    grad,
):
    edge_copy = fetch(next_in, edge, sems.at[0])
    weight_copy = fetch(weight_in, weight, sems.at[1])
    copies = [
        fetch(wide_in.at[0], wide, sems.at[2]),
        fetch(first_in, first, sems.at[3]),
    ]
    for half in range(2):
        part = slice(512 + half * 512, 1024 + half * 512)
        halves[half, 0:2048, :] = real_ref[:, half * X : (half + 1) * X].astype(F32)
        halves[half, 2048:2560, :] = prev_ref[part, :].astype(F32)
    places = ((2048, 16), (0, 64), (16, 64), (32, 64), (48, 64), (2560, 16))

    def build(depth):
        split_depth(depth * 512, places[depth], halves, rows, patch, pick)

    pick[...] = column_picker()
    build(4)
    edge_copy.wait()
    for half in range(2):
        halves[half, 2560:3072, :] = edge[half * 512 : (half + 1) * 512, :].astype(F32)
    build(5)
    weight_copy.wait()
    pre = convolve(weight, patch, build)
    halves[0, 0:512, :] = prev_ref[0:512, :].astype(F32)
    lane = lanes((C, X))
    clear_rims(0, lat_patch)
    for y in range(Y):
        spread_cells(halves[0, pl.ds(y, C, stride=8), :], 0, y, lane, lat_patch)
    for copy in copies:
        copy.wait()
    first[...] += dot(wide[...], lat_patch[...])
    first_copy = fetch(first, first_out, sems.at[4])
    finish(pre, cot_ref, out, wide_cot, wide_out, grad)
    stores = [first_copy, fetch(out, out_out, sems.at[5])]
    planes = [patch[depth * 512 : (depth + 1) * 512, :] for depth in range(6)]
    for half, terms in enumerate(kernel_terms(planes, grad)):
        terms_ref[half * 512 : (half + 1) * 512, :] = terms
        piece = pl.ds(half * 512, 512)
        stores.append(fetch(terms_ref.at[piece], terms_out.at[piece], sems.at[6 + half]))
    for store in stores:
        store.wait()


def fake_kernel(
    inside_ref,
    first_in,
    middle_in,
    last_ref,
    stats_ref,
    weight_in,
    cot_ref,
    real_terms_in,
    out_out,
    low_out,
    high_out,
    terms_out,
    out,
    terms_ref,
    first_ref,
    middle_ref,
    real_terms,
    weight_ref,
    sems,
    patch,
    wide_cot,
    wide_out,
    grad,
):
    weight_copy = fetch(weight_in, weight_ref, sems.at[5])
    middle_copy = fetch(middle_in, middle_ref, sems.at[4])
    first_copy = fetch(first_in, first_ref, sems.at[0])
    real_copy = fetch(real_terms_in, real_terms, sems.at[1])
    stats = stats_ref[...]
    slab = lax.broadcasted_iota(jnp.int32, (NDEV, 128), 0) // 2 % 32
    depths = jnp.where(slab == 0, 5.0, jnp.where(slab == 31, 3.0, 4.0))
    mean_row = jnp.sum(stats * depths, axis=0, keepdims=True) * (1.0 / (4.0 * NDEV))
    off = stats - mean_row
    between = wide_column(jnp.sum(off * off * depths, axis=0, keepdims=True), 0)
    center = wide_column(mean_row, 0)
    within = wide_column(jnp.sum(stats, axis=0, keepdims=True), G)
    variance = (within + 4.0 * CELLS * between) * (1.0 / (16.0 * CELLS * NDEV))
    factor = wide_column(stats[0:1, :], 2 * G) * lax.rsqrt(variance + 1e-05)
    shift = wide_column(stats[0:1, :], 3 * G)
    lane = lanes((G, X))
    edge = jnp.zeros((128, X), BF16)

    def build(depth):
        if depth == 2:
            middle_copy.wait()
        elif depth == 0:
            first_copy.wait()
        before_ref = (first_ref, middle_ref, last_ref)[depth // 2]
        patch[depth * 512 : depth * 512 + 128, 0:X] = edge
        patch[depth * 512 + 384 : depth * 512 + 512, CELLS - X : CELLS] = edge
        for py in range(2):
            for px in range(2):
                block = (depth % 2 * 4 + py * 2 + px) * G
                for y in range(Y):
                    cells = before_ref[block : block + G, y * X : (y + 1) * X]
                    fake = jnp.maximum((cells - center) * factor + shift, 0.0)
                    if depth == 0:
                        fake = jnp.where(inside_ref[0] > 0, fake, 0.0)
                    if depth == 5:
                        fake = jnp.where(inside_ref[1] > 0, fake, 0.0)
                    if px == 1:
                        pieces = ((2, fake), (0, from_left(fake, lane)))
                    else:
                        pieces = ((1, fake), (3, from_right(fake, lane)))
                    for kx, piece in pieces:
                        piece = piece.astype(BF16)
                        for ky, to in ((2, y), (0, y + 1)) if py == 1 else ((1, y), (3, y - 1)):
                            if 0 <= to < Y:
                                at = depth * 512 + ky * 128 + kx * G
                                patch[at : at + G, to * X : (to + 1) * X] = piece

    build(4)
    build(5)
    weight_copy.wait()
    pre = convolve(weight_ref, patch, build)
    finish(pre, cot_ref, out, wide_cot, wide_out, grad)
    stores = [
        fetch(out, out_out, sems.at[6]),
        fetch(grad.at[2 * C : 3 * C], low_out, sems.at[2]),
        fetch(grad.at[C : 2 * C], high_out, sems.at[3]),
    ]
    planes = [patch[depth * 512 : (depth + 1) * 512, :] for depth in range(6)]
    real_copy.wait()
    for half, terms in enumerate(kernel_terms(planes, grad)):
        rows = slice(half * 512, (half + 1) * 512)
        terms_ref[rows, :] = terms + real_terms[rows, :]
        piece = pl.ds(half * 512, 512)
        stores.append(fetch(terms_ref.at[piece], terms_out.at[piece], sems.at[7 + half]))
    for store in stores:
        store.wait()


def sum_kernel(parts_ref, prev_ref, first_ref, sums_ref):
    del prev_ref, first_ref
    total = jnp.sum(parts_ref[...].reshape(NDEV, 8, 128), axis=0, keepdims=True)
    sums_ref[...] = jnp.broadcast_to(total, (NDEV, 8, 128)).reshape(NDEV * 8, 128).astype(BF16)


def unpack_kernel(sums_ref, out, whole, sems):
    copies = []
    for part in range(4):
        rows = slice(part * 256, (part + 1) * 256)
        sums = sums_ref[rows, :].astype(F32)
        whole[0, rows, :] = sums[:, 0:C]
        whole[1, rows, :] = sums[:, C : 2 * C]
        for half in range(2):
            piece = pl.ds(part * 256, 256)
            copies.append(fetch(whole.at[half, piece], out.at[half, piece], sems.at[2 * part + half]))
    for copy in copies:
        copy.wait()


def weave_into(result, first_row, stride, wide_out):
    column = lanes((2 * X, 2 * X))
    source = lax.broadcasted_iota(jnp.int32, (2 * X, 2 * X), 0)
    weave = jnp.where(source == (column % 2) * X + column // 2, 1.0, 0.0).astype(BF16)
    for py in range(2):
        even = result[py * 64 : py * 64 + G, :]
        odd = result[py * 64 + G : py * 64 + 2 * G, :]
        both = jnp.concatenate(
            [
                jnp.concatenate([even[:, y * X : (y + 1) * X], odd[:, y * X : (y + 1) * X]], axis=1)
                for y in range(Y)
            ],
            axis=0,
        )
        woven = dot(both, weave)
        for y in range(Y):
            rows = pl.ds(first_row + 2 * y + py, G, stride=stride)
            wide_out[0, rows, :] = woven[y * G : (y + 1) * G, 0:X]
            wide_out[1, rows, :] = woven[y * G : (y + 1) * G, X : 2 * X]


def spread_edge(cells, depth, patch):
    lane = lanes((C, X))
    clear_rims(depth, patch)
    for y in range(Y):
        spread_cells(cells[:, y * X : (y + 1) * X].astype(F32), depth, y, lane, patch)


def pull_own_kernel(
    low_in,
    high_in,
    taps_in,
    wide_out,
    first_out,
    last_out,
    image_out,
    cells,
    taps,
    wide,
    first,
    last,
    patch,
    wide_rows,
    image,
    sems,
):
    edges = [fetch(ref, cells.at[i], sems.at[i]) for i, ref in enumerate((low_in, high_in))]
    taps_copy = fetch(taps_in, taps, sems.at[2])
    for depth in range(2):
        edges[depth].wait()
        spread_edge(cells[depth], depth, patch)
    taps_copy.wait()
    spread_weights(taps, wide)
    copies = [fetch(wide, wide_out, sems.at[3])]
    first[...] = dot(wide[1, 128:256, :], patch[0:576, :])
    copies.append(fetch(first, first_out, sems.at[4]))
    last[...] = dot(wide[0, 0:128, :], patch[576:1152, :])
    copies.append(fetch(last, last_out, sems.at[5]))
    middle = dot(wide[0], patch[0:576, :]) + dot(wide[1], patch[576:1152, :])
    middle = middle.astype(BF16)
    weave_into(middle[0:128, :], 0, 32, wide_rows)
    weave_into(middle[128:256, :], 16, 32, wide_rows)
    for half in range(2):
        image[:, :, half * X : (half + 1) * X] = wide_rows[half].reshape(G, 32, X).astype(BF16)
    copies.append(fetch(image, image_out.at[:, 16:48], sems.at[6]))
    for copy in copies:
        copy.wait()


def add_edge(side, cells, wide, share, image_out, patch, wide_rows, image, sem):
    spread_edge(cells, 0, patch)
    rows = slice(128 - side * 128, 256 - side * 128)
    weave_into((share[...] + dot(wide[rows, :], patch[...])).astype(BF16), 0, 16, wide_rows)
    for half in range(2):
        image[:, :, half * X : (half + 1) * X] = wide_rows[half].reshape(G, 16, X).astype(BF16)
    return fetch(image, image_out.at[:, pl.ds(side * 48, 16)], sem)


def pull_prev_kernel(
    edge_in,
    wide_in,
    first_in,
    last_in,
    sums_ref,
    image_in,
    image_out,
    wide_next,
    last_ref,
    cells,
    wide,
    share,
    patch,
    wide_rows,
    image,
    sems,
):
    del sums_ref, image_in
    copies = [
        fetch(edge_in, cells, sems.at[0]),
        fetch(wide_in.at[0], wide, sems.at[1]),
        fetch(first_in, share, sems.at[2]),
    ]
    later = [
        fetch(wide_in.at[1], wide_next, sems.at[3]),
        fetch(last_in, last_ref, sems.at[4]),
    ]
    for copy in copies:
        copy.wait()
    later.append(add_edge(0, cells, wide, share, image_out, patch, wide_rows, image, sems.at[5]))
    for copy in later:
        copy.wait()


def pull_next_kernel(
    edge_ref, wide_ref, last_ref, image_in, image_out, patch, wide_rows, image, sem
):
    del image_in
    add_edge(1, edge_ref, wide_ref, last_ref, image_out, patch, wide_rows, image, sem).wait()


def call(body, name, args, outs, scratch, flops, mebibytes, smem=(), far=(), far_outs=(), aliases=()):
    moved = sum(a.size * a.dtype.itemsize for a in args) + sum(o.size * o.dtype.itemsize for o in outs)
    spaces = [
        pltpu.SMEM if i in smem else pl.ANY if i in far else pltpu.VMEM for i in range(len(args))
    ]
    out_spaces = [pltpu.HBM if i in far_outs else pltpu.VMEM for i in range(len(outs))]
    outs = [pltpu.HBM(o.shape, o.dtype) if i in far_outs else o for i, o in enumerate(outs)]
    args = [
        pltpu.with_memory_space_constraint(a, pltpu.HBM) if i in far else a for i, a in enumerate(args)
    ]
    return pl.pallas_call(
        body,
        name=name,
        out_shape=outs,
        in_specs=[pl.BlockSpec(memory_space=space) for space in spaces],
        out_specs=[pl.BlockSpec(memory_space=space) for space in out_spaces],
        scratch_shapes=scratch,
        input_output_aliases=dict(aliases),
        compiler_params=pltpu.CompilerParams(vmem_limit_bytes=mebibytes * 1024 * 1024),
        cost_estimate=pl.CostEstimate(flops=flops, bytes_accessed=moved, transcendentals=0),
    )(*args)


def to_next(edge):
    ends = lax.axis_size("slab") - 1
    return lax.ppermute(edge, "slab", [(i, i + 1) for i in range(ends)])


def to_prev(edge):
    ends = lax.axis_size("slab") - 1
    return lax.ppermute(edge, "slab", [(i + 1, i) for i in range(ends)])


def local(latent, g_weight, bn_gain, bn_shift, real_crops, d_weight, cot_fake, cot_real):
    shape = jax.ShapeDtypeStruct
    taps_g = g_weight.transpose(0, 1, 2, 4, 3).reshape(64 * G, C)
    taps_d = d_weight.reshape(64 * G, C)
    lat = latent[0]
    real = real_crops[0]
    at = lax.axis_index("slab")
    inside = jnp.stack([at > 0, at < lax.axis_size("slab") - 1]).astype(jnp.int32)
    (low,) = call(
        edge_kernel,
        "edges",
        (lat, real),
        [shape((1536, X), BF16)],
        [
            pltpu.VMEM((C, Y, X), BF16),
            pltpu.VMEM((G, 2 * Y, 2 * X), BF16),
            pltpu.SemaphoreType.DMA((2,)),
        ],
        0,
        4,
        far=(0, 1),
    )
    next_ = to_prev(low)
    wide, first, middle, last, sums, high, weight = call(
        own_kernel,
        "own_cells",
        (lat, real, taps_g, taps_d),
        [shape((2, 256, 576), BF16)]
        + [shape((256, CELLS), F32)] * 3
        + [shape((G, 128), F32), shape((1536, X), BF16), shape((C, 2048), BF16)],
        [
            pltpu.VMEM((C, Y, X), BF16),
            pltpu.VMEM((G, 2 * Y, 2 * X), BF16),
            pltpu.VMEM((C, 2, Y, X), BF16),
            pltpu.VMEM((2048, C), BF16),
            pltpu.VMEM((2048, C), BF16),
            pltpu.VMEM((C, 2048), BF16),
            pltpu.VMEM((2, 256, 576), BF16),
            pltpu.VMEM((256, CELLS), F32),
            pltpu.VMEM((256, CELLS), F32),
            pltpu.VMEM((256, CELLS), F32),
            pltpu.SemaphoreType.DMA((10,)),
            pltpu.VMEM((1152, CELLS), BF16),
            pltpu.VMEM((1024, X), F32),
        ],
        4 * 256 * 1152 * CELLS,
        16,
        far=(0, 1, 2, 3),
        far_outs=(0, 1, 2, 3, 6),
    )
    prev = to_next(high)
    last, stats, real_next = call(
        rim_kernel,
        "rim_cells",
        (inside, next_, sums, bn_gain.reshape(1, G), bn_shift.reshape(1, G), wide, last),
        [shape((256, CELLS), F32), shape((NDEV, 128), F32), shape((1024, X), BF16)],
        [
            pltpu.VMEM((576, CELLS), BF16),
            pltpu.VMEM((512, X), F32),
            pltpu.VMEM((256, 576), BF16),
            pltpu.VMEM((256, CELLS), F32),
            pltpu.VMEM((NDEV, 128), F32),
            pltpu.VMEM((1, G), F32),
            pltpu.VMEM((1, G), F32),
            pltpu.SemaphoreType.DMA((7,)),
        ],
        256 * 1152 * CELLS,
        12,
        smem=(0,),
        far=(3, 4, 5, 6),
        far_outs=(0, 1, 2),
    )
    stats = lax.all_to_all(stats, AXES, 0, 0, tiled=True)
    working = [
        pltpu.VMEM((C * 2 * Y, X), F32),
        pltpu.VMEM((C * 2 * Y, X), F32),
        pltpu.VMEM((4 * C, CELLS), BF16),
    ]
    d_real, real_terms, first = call(
        real_kernel,
        "real_branch",
        (
            real.reshape(G * 64, 2 * X),
            prev,
            real_next,
            weight,
            cot_real.reshape(C * 2 * Y, X),
            wide,
            first,
        ),
        [shape((C * 2 * Y, X), BF16), shape((1024, 2 * C), F32), shape((256, CELLS), F32)],
        [
            pltpu.VMEM((C * 2 * Y, X), BF16),
            pltpu.VMEM((1024, X), BF16),
            pltpu.VMEM((C, 2048), BF16),
            pltpu.VMEM((256, 576), BF16),
            pltpu.VMEM((256, CELLS), F32),
            pltpu.VMEM((1024, 2 * C), F32),
            pltpu.VMEM((2 * X, 4 * X), BF16),
            pltpu.SemaphoreType.DMA((8,)),
            pltpu.VMEM((6 * 512, CELLS), BF16),
            pltpu.VMEM((576, CELLS), BF16),
            pltpu.VMEM((2, 3072, X), F32),
            pltpu.VMEM((3072, 2 * X), BF16),
        ]
        + working,
        16 * 2048 * C * CELLS,
        26,
        far=(2, 3, 5, 6),
        far_outs=(0, 1, 2),
    )
    d_fake, low, high, terms = call(
        fake_kernel,
        "fake_branch",
        (
            inside,
            first,
            middle,
            last,
            stats,
            weight,
            cot_fake.reshape(C * 2 * Y, X),
            real_terms,
        ),
        [
            shape((C * 2 * Y, X), BF16),
            shape((C, CELLS), BF16),
            shape((C, CELLS), BF16),
            shape((NDEV * 8, 128), F32),
        ],
        [
            pltpu.VMEM((C * 2 * Y, X), BF16),
            pltpu.VMEM((NDEV * 8, 128), F32),
            pltpu.VMEM((256, CELLS), F32),
            pltpu.VMEM((256, CELLS), F32),
            pltpu.VMEM((NDEV * 8, 128), F32),
            pltpu.VMEM((C, 2048), BF16),
            pltpu.SemaphoreType.DMA((9,)),
            pltpu.VMEM((6 * 512, CELLS), BF16),
        ]
        + working,
        8 * 2048 * C * CELLS * 2,
        26,
        smem=(0,),
        far=(1, 2, 5, 7),
        far_outs=(0, 1, 2, 3),
    )
    parts = lax.all_to_all(terms.reshape(NDEV, 8, 128), AXES, 0, 0, tiled=True)
    grad_prev = to_next(high)
    grad_next = to_prev(low)
    pull_wide, pull_first, pull_last, image = call(
        pull_own_kernel,
        "pull_own",
        (low, high, taps_d),
        [
            shape((2, 256, 576), BF16),
            shape((128, CELLS), F32),
            shape((128, CELLS), F32),
            shape((G, 64, 2 * X), BF16),
        ],
        [
            pltpu.VMEM((2, C, CELLS), BF16),
            pltpu.VMEM((2048, C), BF16),
            pltpu.VMEM((2, 256, 576), BF16),
            pltpu.VMEM((128, CELLS), F32),
            pltpu.VMEM((128, CELLS), F32),
            pltpu.VMEM((1152, CELLS), BF16),
            pltpu.VMEM((2, G * 32, X), F32),
            pltpu.VMEM((G, 32, 2 * X), BF16),
            pltpu.SemaphoreType.DMA((7,)),
        ],
        2 * 384 * 1152 * CELLS,
        16,
        far=(0, 1, 2),
        far_outs=(0, 1, 2, 3),
    )
    (sums,) = call(
        sum_kernel,
        "sum_terms",
        (parts.reshape(NDEV * 8, 128), grad_prev, pull_first),
        [shape((NDEV * 8, 128), BF16)],
        [],
        NDEV * 1024,
        6,
        far=(1, 2),
    )
    whole = lax.all_to_all(sums.reshape(NDEV, 8, 128), AXES, 0, 0, tiled=True)
    outer = [
        pltpu.VMEM((576, CELLS), BF16),
        pltpu.VMEM((2, G * 16, X), F32),
        pltpu.VMEM((G, 16, 2 * X), BF16),
    ]
    image, wide_next, last_share = call(
        pull_prev_kernel,
        "pull_prev",
        (grad_prev, pull_wide, pull_first, pull_last, sums, image),
        [shape((G, 64, 2 * X), BF16), shape((256, 576), BF16), shape((128, CELLS), F32)],
        [
            pltpu.VMEM((C, CELLS), BF16),
            pltpu.VMEM((256, 576), BF16),
            pltpu.VMEM((128, CELLS), F32),
        ]
        + outer
        + [pltpu.SemaphoreType.DMA((6,))],
        128 * 1152 * CELLS,
        12,
        far=(0, 1, 2, 3, 4, 5),
        far_outs=(0,),
        aliases=((5, 0),),
    )
    (image,) = call(
        pull_next_kernel,
        "pull_next",
        (grad_next, wide_next, last_share, image),
        [shape((G, 64, 2 * X), BF16)],
        outer + [pltpu.SemaphoreType.DMA],
        128 * 1152 * CELLS,
        12,
        far=(3,),
        far_outs=(0,),
        aliases=((3, 0),),
    )
    (weight_grad,) = call(
        unpack_kernel,
        "unpack",
        (whole.reshape(NDEV * 8, 128),),
        [shape((2, 1024, C), F32)],
        [pltpu.VMEM((2, 1024, C), F32), pltpu.SemaphoreType.DMA((8,))],
        0,
        6,
        far_outs=(0,),
    )
    return (
        d_fake.reshape(1, C, 2, Y, X),
        d_real.reshape(1, C, 2, Y, X),
        image.reshape(1, G, 4, 2 * Y, 2 * X),
        weight_grad.reshape(4, 4, 4, G, C),
    )


def solution(mesh):
    split = P(("section", "rep"), None, "slab", None, None)
    in_specs = (split, P(), P(), P(), split, P(), split, split)
    out_specs = (split, split, split, P())
    return jax.shard_map(local, mesh=mesh, in_specs=in_specs, out_specs=out_specs, check_vma=False)
```

```python
import jax
import jax.numpy as jnp
from jax import lax
from jax.experimental import pallas as pl
from jax.experimental.pallas import tpu as pltpu
from jax.sharding import PartitionSpec as P

AXES = ("section", "slab", "rep")
NDEV = 128
C = 64
G = 32
Y = 8
X = 128
CELLS = Y * X
F32 = jnp.float32
BF16 = jnp.bfloat16

phase_taps = (((1, 0), (3, -1)), ((0, 1), (2, 0)))


def dot(a, b, dims=(1, 0)):
    return lax.dot_general(a, b, (((dims[0],), (dims[1],)), ((), ())), preferred_element_type=F32)


def lanes(shape):
    return lax.broadcasted_iota(jnp.int32, shape, len(shape) - 1)


def from_left(tile, lane):
    return jnp.where(lane == 0, 0.0, pltpu.roll(tile, 1, 1))


def from_right(tile, lane):
    return jnp.where(lane == X - 1, 0.0, pltpu.roll(tile, X - 1, 1))


def spread_weights(taps_ref, wide_ref):
    wide_ref[...] = jnp.zeros_like(wide_ref)
    for pz in range(2):
        for py in range(2):
            for px in range(2):
                row = ((1 - pz) * 4 + py * 2 + px) * G
                for kz, oz in phase_taps[pz]:
                    tz = oz if pz == 1 else oz + 1
                    for ky, oy in phase_taps[py]:
                        for kx, ox in phase_taps[px]:
                            col = (oy + 1) * 192 + (ox + 1) * 64
                            tap = (kz * 16 + ky * 4 + kx) * G
                            wide_ref[tz, row : row + G, col : col + C] = taps_ref[tap : tap + G, :]


def spread_cells(tile, depth, y, lane, patch_ref):
    for xi, moved in ((0, from_left(tile, lane)), (1, tile), (2, from_right(tile, lane))):
        piece = moved.astype(BF16)
        for yi in range(3):
            to = y - (yi - 1)
            if 0 <= to < Y:
                row = depth * 576 + yi * 192 + xi * 64
                patch_ref[row : row + C, to * X : (to + 1) * X] = piece


def clear_rims(depth, patch_ref):
    edge = jnp.zeros((192, X), BF16)
    patch_ref[depth * 576 : depth * 576 + 192, 0:X] = edge
    patch_ref[depth * 576 + 384 : depth * 576 + 576, CELLS - X : CELLS] = edge


def fetch(source, target, sem):
    copy = pltpu.make_async_copy(source, target, sem)
    copy.start()
    return copy


def as_row(column, shift):
    sub = lax.broadcasted_iota(jnp.int32, (G, 128), 0)
    return jnp.sum(jnp.where(lanes((G, 128)) == sub + shift, column, 0.0), axis=0, keepdims=True)


def as_column(row, shift):
    shape = (G, row.shape[1])
    sub = lax.broadcasted_iota(jnp.int32, shape, 0)
    return jnp.sum(jnp.where(lanes(shape) == sub + shift, row, 0.0), axis=1, keepdims=True)


def edge_kernel(lat_in, real_in, edge_ref, lat_edge, real_edge, sems):
    copies = [
        fetch(lat_in.at[:, 0], lat_edge, sems.at[0]),
        fetch(real_in.at[:, 0], real_edge, sems.at[1]),
    ]
    join_edge(copies, lat_edge, real_edge, edge_ref)


def join_edge(copies, lat_edge, real_edge, edge_ref):
    copies[0].wait()
    edge_ref[0:512, :] = lat_edge[...].reshape(512, X)
    copies[1].wait()
    edge = real_edge[...].reshape(512, 2 * X)
    edge_ref[512:1024, :] = edge[:, 0:X]
    edge_ref[1024:1536, :] = edge[:, X : 2 * X]


def cell_stats(ref, first, count):
    blocks = range(first, first + count)
    total = jnp.zeros((G, CELLS), F32)
    for block in blocks:
        total += ref[block * G : (block + 1) * G, :]
    mean = jnp.sum(total, axis=1, keepdims=True) * (1.0 / (count * CELLS))
    squares = jnp.zeros((G, CELLS), F32)
    for block in blocks:
        off = ref[block * G : (block + 1) * G, :] - mean
        squares += off * off
    return mean, jnp.sum(squares, axis=1, keepdims=True)


def own_kernel(
    lat_in,
    real_in,
    taps_in,
    taps_d_in,
    wide_out,
    first_out,
    middle_out,
    last_out,
    sums_ref,
    edge_ref,
    weight_out,
    lat_edge,
    real_edge,
    lat,
    taps,
    taps_d,
    weight,
    wide,
    first,
    middle,
    last,
    sems,
    patch,
    wide_lat,
):
    edge_copies = [
        fetch(lat_in.at[:, 1], lat_edge, sems.at[0]),
        fetch(real_in.at[:, 3], real_edge, sems.at[1]),
    ]
    lat_copy = fetch(lat_in, lat, sems.at[2])
    taps_copy = fetch(taps_in, taps, sems.at[3])
    taps_d_copy = fetch(taps_d_in, taps_d, sems.at[4])
    lat_copy.wait()
    wide_lat[...] = lat[...].reshape(1024, X).astype(F32)
    lane = lanes((C, X))
    for depth in range(2):
        clear_rims(depth, patch)
        for y in range(Y):
            spread_cells(wide_lat[pl.ds(depth * Y + y, C, stride=16), :], depth, y, lane, patch)
    taps_copy.wait()
    spread_weights(taps, wide)
    copies = [fetch(wide, wide_out, sems.at[5])]
    last[...] = dot(wide[0], patch[576:1152, :])
    copies.append(fetch(last, last_out, sems.at[6]))
    middle[...] = dot(wide[0], patch[0:576, :]) + dot(wide[1], patch[576:1152, :])
    copies.append(fetch(middle, middle_out, sems.at[7]))
    first[...] = dot(wide[1], patch[0:576, :])
    copies.append(fetch(first, first_out, sems.at[8]))
    taps_d_copy.wait()
    same = lax.broadcasted_iota(jnp.int32, (C, C), 0) == lanes((C, C))
    unit = jnp.where(same, 1.0, 0.0).astype(BF16)
    weight[...] = dot(unit, taps_d[...], (1, 1)).astype(BF16)
    copies.append(fetch(weight, weight_out, sems.at[9]))
    join_edge(edge_copies, lat_edge, real_edge, edge_ref)
    place = lanes((G, 128))
    sums = jnp.zeros((G, 128), F32)
    for at, column in enumerate(cell_stats(middle, 0, 8) + cell_stats(first, 4, 4)):
        sums = jnp.where(place == at, column, sums)
    sums_ref[...] = sums
    for copy in copies:
        copy.wait()


def rim_kernel(
    inside_ref,
    next_ref,
    sums_ref,
    gain_in,
    shift_in,
    wide_in,
    last_in,
    last_out,
    stats_out,
    real_next_out,
    patch,
    wide_lat,
    wide,
    last,
    stats,
    gain,
    shift,
    sems,
):
    wide_copy = fetch(wide_in.at[1], wide, sems.at[0])
    last_copy = fetch(last_in, last, sems.at[1])
    affine_copies = [fetch(gain_in, gain, sems.at[5]), fetch(shift_in, shift, sems.at[6])]
    copies = [fetch(next_ref.at[512:1536], real_next_out, sems.at[2])]
    wide_lat[...] = next_ref[0:512, :].astype(F32)
    lane = lanes((C, X))
    clear_rims(0, patch)
    for y in range(Y):
        spread_cells(wide_lat[pl.ds(y, C, stride=8), :], 0, y, lane, patch)
    wide_copy.wait()
    added = dot(wide[...], patch[...])
    last_copy.wait()
    last[...] += added
    copies.append(fetch(last, last_out, sems.at[3]))
    groups = [(2.0, sums_ref[:, 0:1], sums_ref[:, 1:2])]
    groups.append((jnp.where(inside_ref[0] > 0, 0.0, 1.0), sums_ref[:, 2:3], sums_ref[:, 3:4]))
    groups.append((1.0,) + cell_stats(last, 0, 4))
    groups.append((jnp.where(inside_ref[1] > 0, 1.0, 0.0),) + cell_stats(last, 4, 4))
    depths = jnp.zeros((G, 1), F32)
    mean = jnp.zeros((G, 1), F32)
    for weight, one, _ in groups:
        depths += weight
        mean += weight * one
    mean /= depths
    spread = jnp.zeros((G, 1), F32)
    for weight, one, squares in groups:
        own = squares if isinstance(weight, float) else weight * squares
        spread += own + weight * (4.0 * CELLS) * (one - mean) * (one - mean)
    row = as_row(mean, 0) + as_row(spread, G)
    for copy in affine_copies:
        copy.wait()
    row += as_row(as_column(gain[...], 0), 2 * G) + as_row(as_column(shift[...], 0), 3 * G)
    stats[...] = jnp.broadcast_to(row, (NDEV, 128))
    copies.append(fetch(stats, stats_out, sems.at[4]))
    for copy in copies:
        copy.wait()


def activate(before):
    squashed = jax.nn.sigmoid(4.0 * before)
    output = before * (0.2 + 0.8 * squashed)
    derivative = 0.2 + 0.8 * squashed + 3.2 * before * squashed * (1.0 - squashed)
    return (output, derivative)


def convolve(weight_ref, patch, build, finish):
    early = weight_ref[:, 0:1024]
    late = weight_ref[:, 1024:2048]
    second = dot(late, patch[2048:3072, :])
    build(2)
    build(3)
    shared = dot(jnp.concatenate([late, early], axis=0), patch[1024:2048, :])
    finish(1, second + shared[C : 2 * C, :])
    build(0)
    build(1)
    finish(0, dot(early, patch[0:1024, :]) + shared[0:C, :])


def finisher(cot_ref, wide_cot, wide_out, grad):
    nothing = jnp.zeros((C, CELLS), BF16)
    grad[0:C, :] = nothing
    grad[3 * C : 4 * C, :] = nothing

    def finish(m, pre):
        if m == 1:
            wide_cot[...] = cot_ref[...].astype(F32)
        for y in range(Y):
            output, slope = activate(pre[:, y * X : (y + 1) * X])
            wide_out[pl.ds(m * Y + y, C, stride=16), :] = output
            cot = wide_cot[pl.ds(m * Y + y, C, stride=16), :]
            grad[(2 - m) * C : (3 - m) * C, y * X : (y + 1) * X] = (cot * slope).astype(BF16)

    return finish


def kernel_terms(planes, grad):
    for half in range(2):
        terms = dot(planes[half], grad[128:256, :], (1, 1))
        terms += dot(planes[half + 2], grad[64:192, :], (1, 1))
        yield terms + dot(planes[half + 4], grad[0:128, :], (1, 1))


def split_depth(at, places, halves, rows, patch):
    base, stride = places
    column = lanes((2 * X, 4 * X))
    source = lax.broadcasted_iota(jnp.int32, (2 * X, 4 * X), 0)
    pick = jnp.where(source == 2 * (column % X) + column // X - 1, 1.0, 0.0).astype(BF16)
    edge = jnp.zeros((128, X), BF16)
    patch[at : at + 128, 0:X] = edge
    patch[at + 384 : at + 512, CELLS - X : CELLS] = edge
    for row in range(2 * Y):
        for half in range(2):
            cells = halves[half, pl.ds(base + row, G, stride=stride), :].astype(BF16)
            rows[at + row * G : at + (row + 1) * G, half * X : (half + 1) * X] = cells
    split = dot(rows[at : at + 512, :], pick).astype(BF16)
    for row in range(2 * Y):
        for kx in range(4):
            piece = split[row * G : (row + 1) * G, kx * X : (kx + 1) * X]
            for ky in range(4):
                if (row + 1 - ky) % 2 == 0 and 0 <= (row + 1 - ky) // 2 < Y:
                    y = (row + 1 - ky) // 2
                    place = at + ky * 128 + kx * G
                    patch[place : place + G, y * X : (y + 1) * X] = piece


def real_kernel(
    real_ref,
    prev_ref,
    next_in,
    weight_in,
    cot_ref,
    wide_in,
    first_in,
    out_out,
    terms_out,
    first_out,
    out,
    edge,
    weight,
    wide,
    first,
    terms_ref,
    sems,
    patch,
    lat_patch,
    halves,
    rows,
    wide_cot,
    wide_out,
    grad,
):
    edge_copy = fetch(next_in, edge, sems.at[0])
    weight_copy = fetch(weight_in, weight, sems.at[1])
    copies = [
        fetch(wide_in.at[0], wide, sems.at[2]),
        fetch(first_in, first, sems.at[3]),
    ]
    for half in range(2):
        part = slice(512 + half * 512, 1024 + half * 512)
        halves[half, 0:2048, :] = real_ref[:, half * X : (half + 1) * X].astype(F32)
        halves[half, 2048:2560, :] = prev_ref[part, :].astype(F32)
    places = ((2048, 16), (0, 64), (16, 64), (32, 64), (48, 64), (2560, 16))

    def build(depth):
        split_depth(depth * 512, places[depth], halves, rows, patch)

    build(4)
    edge_copy.wait()
    for half in range(2):
        halves[half, 2560:3072, :] = edge[half * 512 : (half + 1) * 512, :].astype(F32)
    build(5)
    weight_copy.wait()
    convolve(weight, patch, build, finisher(cot_ref, wide_cot, wide_out, grad))
    halves[0, 0:512, :] = prev_ref[0:512, :].astype(F32)
    lane = lanes((C, X))
    clear_rims(0, lat_patch)
    for y in range(Y):
        spread_cells(halves[0, pl.ds(y, C, stride=8), :], 0, y, lane, lat_patch)
    for copy in copies:
        copy.wait()
    first[...] += dot(wide[...], lat_patch[...])
    first_copy = fetch(first, first_out, sems.at[4])
    out[...] = wide_out[...].astype(BF16)
    stores = [first_copy, fetch(out, out_out, sems.at[5])]
    planes = [patch[depth * 512 : (depth + 1) * 512, :] for depth in range(6)]
    for half, terms in enumerate(kernel_terms(planes, grad)):
        terms_ref[half * 512 : (half + 1) * 512, :] = terms
        piece = pl.ds(half * 512, 512)
        stores.append(fetch(terms_ref.at[piece], terms_out.at[piece], sems.at[6 + half]))
    for store in stores:
        store.wait()


def fake_kernel(
    inside_ref,
    first_in,
    middle_in,
    last_ref,
    stats_ref,
    weight_in,
    cot_ref,
    real_terms_in,
    out_out,
    low_out,
    high_out,
    terms_out,
    out,
    terms_ref,
    first_ref,
    middle_ref,
    real_terms,
    weight_ref,
    sems,
    patch,
    wide_cot,
    wide_out,
    grad,
):
    weight_copy = fetch(weight_in, weight_ref, sems.at[5])
    middle_copy = fetch(middle_in, middle_ref, sems.at[4])
    first_copy = fetch(first_in, first_ref, sems.at[0])
    real_copy = fetch(real_terms_in, real_terms, sems.at[1])
    stats = stats_ref[...]
    slab = lax.broadcasted_iota(jnp.int32, (NDEV, 128), 0) // 2 % 32
    depths = jnp.where(slab == 0, 5.0, jnp.where(slab == 31, 3.0, 4.0))
    mean_row = jnp.sum(stats * depths, axis=0, keepdims=True) * (1.0 / (4.0 * NDEV))
    off = stats - mean_row
    between = as_column(jnp.sum(off * off * depths, axis=0, keepdims=True), 0)
    center = as_column(mean_row, 0)
    within = as_column(jnp.sum(stats, axis=0, keepdims=True), G)
    variance = (within + 4.0 * CELLS * between) * (1.0 / (16.0 * CELLS * NDEV))
    factor = as_column(stats[0:1, :], 2 * G) * lax.rsqrt(variance + 1e-05)
    shift = as_column(stats[0:1, :], 3 * G)
    lane = lanes((G, X))
    edge = jnp.zeros((128, X), BF16)

    def build(depth):
        if depth == 2:
            middle_copy.wait()
        elif depth == 0:
            first_copy.wait()
        before_ref = (first_ref, middle_ref, last_ref)[depth // 2]
        patch[depth * 512 : depth * 512 + 128, 0:X] = edge
        patch[depth * 512 + 384 : depth * 512 + 512, CELLS - X : CELLS] = edge
        for py in range(2):
            for px in range(2):
                block = (depth % 2 * 4 + py * 2 + px) * G
                for y in range(Y):
                    cells = before_ref[block : block + G, y * X : (y + 1) * X]
                    fake = jnp.maximum((cells - center) * factor + shift, 0.0)
                    if depth == 0:
                        fake = jnp.where(inside_ref[0] > 0, fake, 0.0)
                    if depth == 5:
                        fake = jnp.where(inside_ref[1] > 0, fake, 0.0)
                    if px == 1:
                        pieces = ((2, fake), (0, from_left(fake, lane)))
                    else:
                        pieces = ((1, fake), (3, from_right(fake, lane)))
                    for kx, piece in pieces:
                        piece = piece.astype(BF16)
                        for ky, to in ((2, y), (0, y + 1)) if py == 1 else ((1, y), (3, y - 1)):
                            if 0 <= to < Y:
                                at = depth * 512 + ky * 128 + kx * G
                                patch[at : at + G, to * X : (to + 1) * X] = piece

    build(4)
    build(5)
    weight_copy.wait()
    convolve(weight_ref, patch, build, finisher(cot_ref, wide_cot, wide_out, grad))
    out[...] = wide_out[...].astype(BF16)
    stores = [
        fetch(out, out_out, sems.at[6]),
        fetch(grad.at[2 * C : 3 * C], low_out, sems.at[2]),
        fetch(grad.at[C : 2 * C], high_out, sems.at[3]),
    ]
    planes = [patch[depth * 512 : (depth + 1) * 512, :] for depth in range(6)]
    real_copy.wait()
    for half, terms in enumerate(kernel_terms(planes, grad)):
        rows = slice(half * 512, (half + 1) * 512)
        terms_ref[rows, :] = terms + real_terms[rows, :]
        piece = pl.ds(half * 512, 512)
        stores.append(fetch(terms_ref.at[piece], terms_out.at[piece], sems.at[7 + half]))
    for store in stores:
        store.wait()


def sum_kernel(parts_ref, prev_ref, first_ref, sums_ref):
    del prev_ref, first_ref
    total = jnp.sum(parts_ref[...].reshape(NDEV, 8, 128), axis=0, keepdims=True)
    sums_ref[...] = jnp.broadcast_to(total, (NDEV, 8, 128)).reshape(NDEV * 8, 128).astype(BF16)


def unpack_kernel(sums_ref, out, whole, sems):
    copies = []
    for part in range(4):
        rows = slice(part * 256, (part + 1) * 256)
        sums = sums_ref[rows, :].astype(F32)
        whole[0, rows, :] = sums[:, 0:C]
        whole[1, rows, :] = sums[:, C : 2 * C]
        for half in range(2):
            piece = pl.ds(part * 256, 256)
            copies.append(fetch(whole.at[half, piece], out.at[half, piece], sems.at[2 * part + half]))
    for copy in copies:
        copy.wait()


def weave_into(result, first_row, stride, wide_out):
    column = lanes((2 * X, 2 * X))
    source = lax.broadcasted_iota(jnp.int32, (2 * X, 2 * X), 0)
    weave = jnp.where(source == (column % 2) * X + column // 2, 1.0, 0.0).astype(BF16)
    for py in range(2):
        even = result[py * 64 : py * 64 + G, :]
        odd = result[py * 64 + G : py * 64 + 2 * G, :]
        both = jnp.concatenate(
            [
                jnp.concatenate([even[:, y * X : (y + 1) * X], odd[:, y * X : (y + 1) * X]], axis=1)
                for y in range(Y)
            ],
            axis=0,
        )
        woven = dot(both, weave)
        for y in range(Y):
            rows = pl.ds(first_row + 2 * y + py, G, stride=stride)
            wide_out[0, rows, :] = woven[y * G : (y + 1) * G, 0:X]
            wide_out[1, rows, :] = woven[y * G : (y + 1) * G, X : 2 * X]


def spread_edge(cells, depth, patch):
    lane = lanes((C, X))
    clear_rims(depth, patch)
    for y in range(Y):
        spread_cells(cells[:, y * X : (y + 1) * X].astype(F32), depth, y, lane, patch)


def pull_own_kernel(
    low_in,
    high_in,
    taps_in,
    wide_out,
    first_out,
    last_out,
    image_out,
    cells,
    taps,
    wide,
    first,
    last,
    patch,
    wide_rows,
    image,
    sems,
):
    edges = [fetch(ref, cells.at[i], sems.at[i]) for i, ref in enumerate((low_in, high_in))]
    taps_copy = fetch(taps_in, taps, sems.at[2])
    for depth in range(2):
        edges[depth].wait()
        spread_edge(cells[depth], depth, patch)
    taps_copy.wait()
    spread_weights(taps, wide)
    copies = [fetch(wide, wide_out, sems.at[3])]
    first[...] = dot(wide[1, 128:256, :], patch[0:576, :])
    copies.append(fetch(first, first_out, sems.at[4]))
    last[...] = dot(wide[0, 0:128, :], patch[576:1152, :])
    copies.append(fetch(last, last_out, sems.at[5]))
    middle = dot(wide[0], patch[0:576, :]) + dot(wide[1], patch[576:1152, :])
    middle = middle.astype(BF16)
    weave_into(middle[0:128, :], 0, 32, wide_rows)
    weave_into(middle[128:256, :], 16, 32, wide_rows)
    for half in range(2):
        image[:, :, half * X : (half + 1) * X] = wide_rows[half].reshape(G, 32, X).astype(BF16)
    copies.append(fetch(image, image_out.at[:, 16:48], sems.at[6]))
    for copy in copies:
        copy.wait()


def add_edge(side, cells, wide, share, image_out, patch, wide_rows, image, sem):
    spread_edge(cells, 0, patch)
    rows = slice(128 - side * 128, 256 - side * 128)
    weave_into((share[...] + dot(wide[rows, :], patch[...])).astype(BF16), 0, 16, wide_rows)
    for half in range(2):
        image[:, :, half * X : (half + 1) * X] = wide_rows[half].reshape(G, 16, X).astype(BF16)
    return fetch(image, image_out.at[:, pl.ds(side * 48, 16)], sem)


def pull_prev_kernel(
    edge_in,
    wide_in,
    first_in,
    last_in,
    sums_ref,
    image_in,
    image_out,
    wide_next,
    last_ref,
    cells,
    wide,
    share,
    patch,
    wide_rows,
    image,
    sems,
):
    del sums_ref, image_in
    copies = [
        fetch(edge_in, cells, sems.at[0]),
        fetch(wide_in.at[0], wide, sems.at[1]),
        fetch(first_in, share, sems.at[2]),
    ]
    later = [
        fetch(wide_in.at[1], wide_next, sems.at[3]),
        fetch(last_in, last_ref, sems.at[4]),
    ]
    for copy in copies:
        copy.wait()
    later.append(add_edge(0, cells, wide, share, image_out, patch, wide_rows, image, sems.at[5]))
    for copy in later:
        copy.wait()


def pull_next_kernel(
    edge_ref, wide_ref, last_ref, image_in, image_out, patch, wide_rows, image, sem
):
    del image_in
    add_edge(1, edge_ref, wide_ref, last_ref, image_out, patch, wide_rows, image, sem).wait()


def call(body, name, args, outs, scratch, flops, mebibytes, smem=(), far=(), far_outs=(), aliases=()):
    moved = sum(a.size * a.dtype.itemsize for a in args) + sum(o.size * o.dtype.itemsize for o in outs)
    spaces = [
        pltpu.SMEM if i in smem else pl.ANY if i in far else pltpu.VMEM for i in range(len(args))
    ]
    out_spaces = [pltpu.HBM if i in far_outs else pltpu.VMEM for i in range(len(outs))]
    outs = [pltpu.HBM(o.shape, o.dtype) if i in far_outs else o for i, o in enumerate(outs)]
    args = [
        pltpu.with_memory_space_constraint(a, pltpu.HBM) if i in far else a for i, a in enumerate(args)
    ]
    return pl.pallas_call(
        body,
        name=name,
        out_shape=outs,
        in_specs=[pl.BlockSpec(memory_space=space) for space in spaces],
        out_specs=[pl.BlockSpec(memory_space=space) for space in out_spaces],
        scratch_shapes=scratch,
        input_output_aliases=dict(aliases),
        compiler_params=pltpu.CompilerParams(vmem_limit_bytes=mebibytes * 1024 * 1024),
        cost_estimate=pl.CostEstimate(flops=flops, bytes_accessed=moved, transcendentals=0),
    )(*args)


def to_next(edge):
    ends = lax.axis_size("slab") - 1
    return lax.ppermute(edge, "slab", [(i, i + 1) for i in range(ends)])


def to_prev(edge):
    ends = lax.axis_size("slab") - 1
    return lax.ppermute(edge, "slab", [(i + 1, i) for i in range(ends)])


def local(latent, g_weight, bn_gain, bn_shift, real_crops, d_weight, cot_fake, cot_real):
    shape = jax.ShapeDtypeStruct
    taps_g = g_weight.transpose(0, 1, 2, 4, 3).reshape(64 * G, C)
    taps_d = d_weight.reshape(64 * G, C)
    lat = latent[0]
    real = real_crops[0]
    at = lax.axis_index("slab")
    inside = jnp.stack([at > 0, at < lax.axis_size("slab") - 1]).astype(jnp.int32)
    (low,) = call(
        edge_kernel,
        "edges",
        (lat, real),
        [shape((1536, X), BF16)],
        [
            pltpu.VMEM((C, Y, X), BF16),
            pltpu.VMEM((G, 2 * Y, 2 * X), BF16),
            pltpu.SemaphoreType.DMA((2,)),
        ],
        0,
        4,
        far=(0, 1),
    )
    next_ = to_prev(low)
    wide, first, middle, last, sums, high, weight = call(
        own_kernel,
        "own_cells",
        (lat, real, taps_g, taps_d),
        [shape((2, 256, 576), BF16)]
        + [shape((256, CELLS), F32)] * 3
        + [shape((G, 128), F32), shape((1536, X), BF16), shape((C, 2048), BF16)],
        [
            pltpu.VMEM((C, Y, X), BF16),
            pltpu.VMEM((G, 2 * Y, 2 * X), BF16),
            pltpu.VMEM((C, 2, Y, X), BF16),
            pltpu.VMEM((2048, C), BF16),
            pltpu.VMEM((2048, C), BF16),
            pltpu.VMEM((C, 2048), BF16),
            pltpu.VMEM((2, 256, 576), BF16),
            pltpu.VMEM((256, CELLS), F32),
            pltpu.VMEM((256, CELLS), F32),
            pltpu.VMEM((256, CELLS), F32),
            pltpu.SemaphoreType.DMA((10,)),
            pltpu.VMEM((1152, CELLS), BF16),
            pltpu.VMEM((1024, X), F32),
        ],
        4 * 256 * 1152 * CELLS,
        16,
        far=(0, 1, 2, 3),
        far_outs=(0, 1, 2, 3, 6),
    )
    prev = to_next(high)
    last, stats, real_next = call(
        rim_kernel,
        "rim_cells",
        (inside, next_, sums, bn_gain.reshape(1, G), bn_shift.reshape(1, G), wide, last),
        [shape((256, CELLS), F32), shape((NDEV, 128), F32), shape((1024, X), BF16)],
        [
            pltpu.VMEM((576, CELLS), BF16),
            pltpu.VMEM((512, X), F32),
            pltpu.VMEM((256, 576), BF16),
            pltpu.VMEM((256, CELLS), F32),
            pltpu.VMEM((NDEV, 128), F32),
            pltpu.VMEM((1, G), F32),
            pltpu.VMEM((1, G), F32),
            pltpu.SemaphoreType.DMA((7,)),
        ],
        256 * 1152 * CELLS,
        12,
        smem=(0,),
        far=(3, 4, 5, 6),
        far_outs=(0, 1, 2),
    )
    stats = lax.all_to_all(stats, AXES, 0, 0, tiled=True)
    working = [
        pltpu.VMEM((C * 2 * Y, X), F32),
        pltpu.VMEM((C * 2 * Y, X), F32),
        pltpu.VMEM((4 * C, CELLS), BF16),
    ]
    d_real, real_terms, first = call(
        real_kernel,
        "real_branch",
        (
            real.reshape(G * 64, 2 * X),
            prev,
            real_next,
            weight,
            cot_real.reshape(C * 2 * Y, X),
            wide,
            first,
        ),
        [shape((C * 2 * Y, X), BF16), shape((1024, 2 * C), F32), shape((256, CELLS), F32)],
        [
            pltpu.VMEM((C * 2 * Y, X), BF16),
            pltpu.VMEM((1024, X), BF16),
            pltpu.VMEM((C, 2048), BF16),
            pltpu.VMEM((256, 576), BF16),
            pltpu.VMEM((256, CELLS), F32),
            pltpu.VMEM((1024, 2 * C), F32),
            pltpu.SemaphoreType.DMA((8,)),
            pltpu.VMEM((6 * 512, CELLS), BF16),
            pltpu.VMEM((576, CELLS), BF16),
            pltpu.VMEM((2, 3072, X), F32),
            pltpu.VMEM((3072, 2 * X), BF16),
        ]
        + working,
        16 * 2048 * C * CELLS,
        26,
        far=(2, 3, 5, 6),
        far_outs=(0, 1, 2),
    )
    d_fake, low, high, terms = call(
        fake_kernel,
        "fake_branch",
        (
            inside,
            first,
            middle,
            last,
            stats,
            weight,
            cot_fake.reshape(C * 2 * Y, X),
            real_terms,
        ),
        [
            shape((C * 2 * Y, X), BF16),
            shape((C, CELLS), BF16),
            shape((C, CELLS), BF16),
            shape((NDEV * 8, 128), F32),
        ],
        [
            pltpu.VMEM((C * 2 * Y, X), BF16),
            pltpu.VMEM((NDEV * 8, 128), F32),
            pltpu.VMEM((256, CELLS), F32),
            pltpu.VMEM((256, CELLS), F32),
            pltpu.VMEM((NDEV * 8, 128), F32),
            pltpu.VMEM((C, 2048), BF16),
            pltpu.SemaphoreType.DMA((9,)),
            pltpu.VMEM((6 * 512, CELLS), BF16),
        ]
        + working,
        8 * 2048 * C * CELLS * 2,
        26,
        smem=(0,),
        far=(1, 2, 5, 7),
        far_outs=(0, 1, 2, 3),
    )
    parts = lax.all_to_all(terms.reshape(NDEV, 8, 128), AXES, 0, 0, tiled=True)
    grad_prev = to_next(high)
    grad_next = to_prev(low)
    pull_wide, pull_first, pull_last, image = call(
        pull_own_kernel,
        "pull_own",
        (low, high, taps_d),
        [
            shape((2, 256, 576), BF16),
            shape((128, CELLS), F32),
            shape((128, CELLS), F32),
            shape((G, 64, 2 * X), BF16),
        ],
        [
            pltpu.VMEM((2, C, CELLS), BF16),
            pltpu.VMEM((2048, C), BF16),
            pltpu.VMEM((2, 256, 576), BF16),
            pltpu.VMEM((128, CELLS), F32),
            pltpu.VMEM((128, CELLS), F32),
            pltpu.VMEM((1152, CELLS), BF16),
            pltpu.VMEM((2, G * 32, X), F32),
            pltpu.VMEM((G, 32, 2 * X), BF16),
            pltpu.SemaphoreType.DMA((7,)),
        ],
        2 * 384 * 1152 * CELLS,
        16,
        far=(0, 1, 2),
        far_outs=(0, 1, 2, 3),
    )
    (sums,) = call(
        sum_kernel,
        "sum_terms",
        (parts.reshape(NDEV * 8, 128), grad_prev, pull_first),
        [shape((NDEV * 8, 128), BF16)],
        [],
        NDEV * 1024,
        6,
        far=(1, 2),
    )
    whole = lax.all_to_all(sums.reshape(NDEV, 8, 128), AXES, 0, 0, tiled=True)
    outer = [
        pltpu.VMEM((576, CELLS), BF16),
        pltpu.VMEM((2, G * 16, X), F32),
        pltpu.VMEM((G, 16, 2 * X), BF16),
    ]
    image, wide_next, last_share = call(
        pull_prev_kernel,
        "pull_prev",
        (grad_prev, pull_wide, pull_first, pull_last, sums, image),
        [shape((G, 64, 2 * X), BF16), shape((256, 576), BF16), shape((128, CELLS), F32)],
        [
            pltpu.VMEM((C, CELLS), BF16),
            pltpu.VMEM((256, 576), BF16),
            pltpu.VMEM((128, CELLS), F32),
        ]
        + outer
        + [pltpu.SemaphoreType.DMA((6,))],
        128 * 1152 * CELLS,
        12,
        far=(0, 1, 2, 3, 4, 5),
        far_outs=(0,),
        aliases=((5, 0),),
    )
    (image,) = call(
        pull_next_kernel,
        "pull_next",
        (grad_next, wide_next, last_share, image),
        [shape((G, 64, 2 * X), BF16)],
        outer + [pltpu.SemaphoreType.DMA],
        128 * 1152 * CELLS,
        12,
        far=(3,),
        far_outs=(0,),
        aliases=((3, 0),),
    )
    (weight_grad,) = call(
        unpack_kernel,
        "unpack",
        (whole.reshape(NDEV * 8, 128),),
        [shape((2, 1024, C), F32)],
        [pltpu.VMEM((2, 1024, C), F32), pltpu.SemaphoreType.DMA((8,))],
        0,
        6,
        far_outs=(0,),
    )
    return (
        d_fake.reshape(1, C, 2, Y, X),
        d_real.reshape(1, C, 2, Y, X),
        image.reshape(1, G, 4, 2 * Y, 2 * X),
        weight_grad.reshape(4, 4, 4, G, C),
    )


def solution(mesh):
    split = P(("section", "rep"), None, "slab", None, None)
    in_specs = (split, P(), P(), P(), split, P(), split, split)
    out_specs = (split, split, split, P())
    return jax.shard_map(local, mesh=mesh, in_specs=in_specs, out_specs=out_specs, check_vma=False)
```
